128 devices in a mesh: dp: 16 (over z, y_hi, core), ctx: 8 (over y_lo, x).
Axes of the slice: x: 4, y: 4 (y_hi: 2, y_lo: 2; y = y_hi * 2 + y_lo), z: 4, core: 2. Of those that a mesh axis runs over, the one named last changes fastest.
Arguments:
- residual_in: bfloat16 [16, 1024, 1536], P('dp', 'ctx'), may hold values from -64 to 64
- query_rows: bfloat16 [16, 1024, 1536], P('dp', 'ctx'), may hold values from -6 to 6
- key_rows: bfloat16 [16, 1024, 1536], P('dp', 'ctx'), may hold values from -6 to 6
- value_rows: bfloat16 [16, 1024, 1536], P('dp', 'ctx'), may hold values from -6 to 6
- lengths: int32 [16], P('dp'), may hold values from 256 to 1024, as said below
- out_weight: bfloat16 [1536, 1536], replicated, may hold values from -0.15625 to 0.15625
- norm_gain: float32 [1536], replicated, may hold values from 0.25 to 1.75
- conv_kernel: float32 [31, 1536], replicated, may hold values from -1 to 1
- conv_bias: float32 [1536], replicated, may hold values from -3 to 3
- conv_gain: float32 [1536], replicated, may hold values from 0.25 to 1.75
- point_weight: bfloat16 [1536, 1536], replicated, may hold values from -0.15625 to 0.15625
- grad_out: bfloat16 [16, 1024, 1536], P('dp', 'ctx'), may hold values from -6 to 6
Outputs:
- block_out: bfloat16 [16, 1024, 1536], P('dp', 'ctx')
- grad_residual: bfloat16 [16, 1024, 1536], P('dp', 'ctx')
- grad_query: bfloat16 [16, 1024, 1536], P('dp', 'ctx')
- grad_key: bfloat16 [16, 1024, 1536], P('dp', 'ctx')
- grad_value: bfloat16 [16, 1024, 1536], P('dp', 'ctx')
- grad_out_weight: float32 [1536, 1536], P(None, ('dp', 'ctx'))
- grad_point_weight: float32 [1536, 1536], P(None, ('dp', 'ctx'))
- grad_kernel: float32 [31, 1536], P(None, ('dp', 'ctx'))
- grad_vectors: float32 [3, 1536], P(None, ('dp', 'ctx'))
The draws below stay inside these ranges and needn't reach their ends.
Inputs may be any that keep to these rules, and one draw needn't show every extreme that they name: `lengths`: in every draw some utterance has all 1024 frames.
All inputs are finite; a program needn't handle non-finite values.
Results may differ from the reference program's by a relative error of at most 0.028.
Values may be sent and summed in bfloat16 or wider, within the bound.
A program may use at most 192 MiB of HBM per device.

```python
import jax
import jax.numpy as jnp
from jax import lax

D = 1536
HEADS = 24
HEAD_DIM = 64
KERN = 31
ATT = 1536
HALF = 15
S = 1024
B = 16


def draw_query_rows(key, part):
    own_key = jax.random.fold_in(key, 5)
    return jnp.clip(jax.random.normal(own_key, (B, S, ATT), jnp.float32), -4.0, 4.0).astype(jnp.bfloat16)


def draw_key_rows(key, part):
    own_key = jax.random.fold_in(key, 6)
    return jnp.clip(jax.random.normal(own_key, (B, S, ATT), jnp.float32), -4.0, 4.0).astype(jnp.bfloat16)


def draw_residual_in(key, part):
    own_key = jax.random.fold_in(key, 7)
    row_key, column_key, base_key = jax.random.split(own_key, 3)
    row_scale = jnp.exp(jax.random.uniform(row_key, (B, S, 1), jnp.float32, -0.916, 1.386))
    column_scale = jnp.exp(jax.random.uniform(column_key, (1, 1, D), jnp.float32, -0.916, 1.386))
    base = jnp.clip(jax.random.normal(base_key, (B, S, D), jnp.float32), -4.0, 4.0)
    return (base * column_scale * row_scale).astype(jnp.bfloat16)


def draw_lengths(key, part):
    own_key = jax.random.fold_in(key, 9)
    length_key, pick_key = jax.random.split(own_key)
    drawn = jax.random.randint(length_key, (B,), S // 4, S + 1)
    fullest = jax.random.randint(pick_key, (), 0, B)
    return jnp.where(jnp.arange(B, dtype=jnp.int32) == fullest, S, drawn).astype(jnp.int32)


def spiked(values, key, source, target, parts, factor):
    def block_of(position):
        return (jnp.arange(values.shape[position]) // (values.shape[position] // parts)).reshape((-1,) + (1,) * (values.ndim - 1 - position))

    one_side = jax.random.permutation(key, parts)[block_of(target)]
    other_side = (block_of(target) + parts // 2) % parts
    return jnp.where((block_of(source) == one_side) | (block_of(source) == other_side), factor * values, values)


def level_of(stream_key, shape, cuts, least, largest):
    level = 1.0
    for axis_at, parts in cuts:
        steps = jax.random.uniform(jax.random.fold_in(jax.random.fold_in(stream_key, 6), axis_at), (parts,), jnp.float32, least / len(cuts), largest / len(cuts))
        level = level * jnp.repeat(jnp.exp(steps), shape[axis_at] // parts).reshape((-1,) + (1,) * (len(shape) - 1 - axis_at))
    return level


def normal_values(rng, extent, scale, bound, cuts=(), held_as=jnp.bfloat16):
    result = jax.random.normal(rng, extent, jnp.float32) * scale
    if len(cuts) > 0:
        result = level_of(rng, extent, cuts, -0.22, 0.18) * result
    return jnp.clip(result, min=-bound, max=bound).astype(held_as)


def bell_draw_with(rng, extent, width, most, pieces, heavy, kind=jnp.bfloat16):
    array = width * jax.random.normal(rng, extent, jnp.float32)
    if pieces:
        array = array * level_of(rng, extent, pieces, -0.22, 0.18)
    return jnp.clip(spiked(array, jax.random.fold_in(rng, 3), *heavy), -most, most).astype(kind)


def setup_inputs(seed: int = 0) -> dict:
    key_of = jax.random.split(jax.random.key(seed), 13)
    return {
        "residual_in": draw_residual_in(jax.random.fold_in(key_of[12], 71), 0),
        "query_rows": draw_query_rows(jax.random.fold_in(key_of[12], 71), 0),
        "key_rows": draw_key_rows(jax.random.fold_in(key_of[12], 71), 0),
        "value_rows": normal_values(key_of[3], (B, S, ATT), 1.0, 6.0, ((0, 16), (1, 8))),
        "lengths": draw_lengths(jax.random.fold_in(key_of[12], 71), 0),
        "out_weight": normal_values(key_of[5], (ATT, D), ATT ** -0.5, 0.15625),
        "norm_gain": jnp.clip(1.0 + 0.15 * jax.random.normal(key_of[6], (D,), jnp.float32), 0.25, 1.75),
        "conv_kernel": normal_values(key_of[7], (KERN, D), KERN ** -0.5, 1.0, (), jnp.float32),
        "conv_bias": normal_values(key_of[8], (D,), 0.5, 3.0, (), jnp.float32),
        "conv_gain": jnp.clip(1.0 + 0.15 * jax.random.normal(key_of[9], (D,), jnp.float32), 0.25, 1.75),
        "point_weight": normal_values(key_of[10], (D, D), D ** -0.5, 0.15625),
        "grad_out": bell_draw_with(key_of[11], (B, S, D), 1.0, 6.0, ((0, 16), (1, 8)), (0, 2, 16, 2.0)),
    }


NEG_FILL = -1e+30
EPSILON = 1e-05

def low_float(values):
    return lax.optimization_barrier(values.astype(jnp.bfloat16)).astype(jnp.float32)

def layer_norm(rows, gain):
    centre = lax.optimization_barrier(jnp.mean(rows, axis=-1, keepdims=True))
    centred = rows - centre
    inv_scale = lax.rsqrt(lax.optimization_barrier(jnp.mean(centred * centred, axis=-1, keepdims=True)) + EPSILON)
    normed = centred * inv_scale
    return (normed * gain, normed, inv_scale)

def layer_norm_back(grad_scaled, normed, inv_scale, gain):
    grad_normed = grad_scaled * gain
    first_mean = lax.optimization_barrier(jnp.mean(grad_normed, axis=-1, keepdims=True))
    second_mean = lax.optimization_barrier(jnp.mean(grad_normed * normed, axis=-1, keepdims=True))
    grad_rows = inv_scale * (grad_normed - first_mean - normed * second_mean)
    grad_gain = lax.optimization_barrier(jnp.sum((grad_scaled * normed).reshape(-1, normed.shape[-1]), axis=0))
    return (grad_rows, grad_gain)

def depthwise(padded, taps, count):
    total = jnp.zeros((padded.shape[0], count, padded.shape[2]), jnp.float32)
    for offset in range(taps.shape[0]):
        total = total + padded[:, offset:offset + count, :].astype(jnp.float32) * taps[offset]
    return total

def kernel_grad(padded, grad_conv, count, tap_count):
    rows_list = []
    for offset in range(tap_count):
        product = padded[:, offset:offset + count, :].astype(jnp.float32) * grad_conv
        rows_list.append(lax.optimization_barrier(jnp.sum(product.reshape(-1, grad_conv.shape[2]), axis=0)))
    return jnp.stack(rows_list)

def masked_scores(query_one, key_one, valid_one):
    score_scale = HEAD_DIM ** (-0.5)
    scores = jnp.einsum('qhd,khd->hqk', query_one.astype(jnp.float32), key_one.astype(jnp.float32)) * score_scale
    return jnp.where(valid_one[None, None, :], scores, NEG_FILL)

def attend_one(inputs):
    query_one, key_one, value_one, valid_one = inputs
    scores = masked_scores(query_one, key_one, valid_one)
    row_max = lax.optimization_barrier(jnp.max(scores, axis=-1))
    weights = jnp.exp(scores - row_max[..., None]) * valid_one[None, None, :].astype(jnp.float32)
    total = lax.optimization_barrier(jnp.sum(weights, axis=-1))
    summed = jnp.einsum('hqk,khd->qhd', low_float(weights), value_one.astype(jnp.float32))
    attended_one = (summed / jnp.transpose(total)[:, :, None]).astype(jnp.bfloat16)
    return (attended_one, row_max + jnp.log(total))

def attend_back(inputs):
    query_one, key_one, value_one, valid_one, grad_one, log_one, delta_one = inputs
    score_scale = HEAD_DIM ** (-0.5)
    scores = masked_scores(query_one, key_one, valid_one)
    probs = jnp.where(valid_one[None, None, :], jnp.exp(scores - log_one[..., None]), 0.0)
    grad_float = grad_one.astype(jnp.float32)
    value_grad = jnp.einsum('hqk,qhd->khd', low_float(probs), grad_float)
    prob_grad = jnp.einsum('qhd,khd->hqk', grad_float, value_one.astype(jnp.float32))
    score_grad = low_float(probs * (prob_grad - delta_one[..., None]) * score_scale)
    query_grad = jnp.einsum('hqk,khd->qhd', score_grad, key_one.astype(jnp.float32))
    key_grad = jnp.einsum('hqk,qhd->khd', score_grad, query_one.astype(jnp.float32))
    return (query_grad.astype(jnp.bfloat16), key_grad.astype(jnp.bfloat16), value_grad.astype(jnp.bfloat16))

def reference(residual_in, query_rows, key_rows, value_rows, lengths, out_weight, norm_gain, conv_kernel, conv_bias, conv_gain, point_weight, grad_out):
    positions = jnp.arange(S, dtype=jnp.int32)
    frame_valid = positions[None, :] < lengths[:, None]
    valid_rows = frame_valid[..., None].astype(jnp.float32)
    heads_shape = (B, S, HEADS, HEAD_DIM)
    query_heads = query_rows.reshape(heads_shape)
    key_heads = key_rows.reshape(heads_shape)
    value_heads = value_rows.reshape(heads_shape)
    attended_heads, log_total = lax.map(attend_one, (query_heads, key_heads, value_heads, frame_valid))
    attended = attended_heads.reshape(B, S, ATT)
    mixed = residual_in.astype(jnp.float32) + jnp.dot(attended.reshape(-1, ATT), out_weight, preferred_element_type=jnp.float32).reshape(B, S, D)
    scaled_one, normed_one, inv_one = layer_norm(mixed, norm_gain)
    conv_in = (scaled_one * valid_rows).astype(jnp.bfloat16)
    conv_padded = jnp.pad(conv_in, ((0, 0), (HALF, HALF), (0, 0)))
    conv_sum = depthwise(conv_padded, conv_kernel, S) + conv_bias
    scaled_two, normed_two, inv_two = layer_norm(conv_sum, conv_gain)
    gate_value = jax.nn.sigmoid(scaled_two)
    conv_act = (scaled_two * gate_value).astype(jnp.bfloat16)
    block_out = (mixed + jnp.dot(conv_act.reshape(-1, D), point_weight, preferred_element_type=jnp.float32).reshape(B, S, D)).astype(jnp.bfloat16)
    grad_masked = jnp.where(frame_valid[..., None], grad_out, jnp.zeros_like(grad_out))
    grad_act = jnp.dot(grad_masked.reshape(-1, D), point_weight.T, preferred_element_type=jnp.float32).reshape(B, S, D)
    grad_point_weight = jnp.dot(conv_act.reshape(-1, D).T, grad_masked.reshape(-1, D), preferred_element_type=jnp.float32)
    grad_scaled_two = grad_act * gate_value * (1.0 + scaled_two * (1.0 - gate_value))
    grad_conv, conv_gain_grad = layer_norm_back(grad_scaled_two, normed_two, inv_two, conv_gain)
    bias_grad = lax.optimization_barrier(jnp.sum(grad_conv.reshape(-1, D), axis=0))
    grad_kernel = kernel_grad(conv_padded, grad_conv, S, KERN)
    grad_conv_low = grad_conv.astype(jnp.bfloat16)
    grad_padded = jnp.pad(grad_conv_low, ((0, 0), (HALF, HALF), (0, 0)))
    grad_conv_in = depthwise(grad_padded, conv_kernel[::-1], S) * valid_rows
    grad_mixed, norm_gain_grad = layer_norm_back(grad_conv_in, normed_one, inv_one, norm_gain)
    grad_vectors = jnp.stack([bias_grad, norm_gain_grad, conv_gain_grad])
    grad_residual = (grad_masked.astype(jnp.float32) + grad_mixed).astype(jnp.bfloat16)
    grad_out_weight = jnp.dot(attended.reshape(-1, ATT).T, grad_residual.reshape(-1, D), preferred_element_type=jnp.float32)
    grad_attended = jnp.dot(grad_residual.reshape(-1, D), out_weight.T, preferred_element_type=jnp.float32).astype(jnp.bfloat16)
    grad_heads = grad_attended.reshape(heads_shape)
    delta = jnp.einsum('bqhd,bqhd->bhq', grad_heads.astype(jnp.float32), attended_heads.astype(jnp.float32))
    grad_query, grad_key, grad_value = lax.map(attend_back, (query_heads, key_heads, value_heads, frame_valid, grad_heads, log_total, delta))
    return (block_out, grad_residual, grad_query.reshape(B, S, ATT), grad_key.reshape(B, S, ATT), grad_value.reshape(B, S, ATT), grad_out_weight, grad_point_weight, grad_kernel, grad_vectors)
```

```python
import jax
import jax.numpy as jnp
from jax import lax
from jax.experimental import pallas as pl
from jax.experimental.pallas import tpu as pltpu
from jax.sharding import PartitionSpec as P

N = 8
F = 128
D = 1536
S = 1024
HD = 64
KERN = 31
NB = D // 128
TILE = 256
EPSILON = 1e-05
MASKED = -1e30
MESH = pl.DeviceIdType.MESH
BF = jnp.bfloat16
F32 = jnp.float32


def dot(a, b):
    return jnp.dot(a, b, preferred_element_type=F32)


def dot_nt(a, b):
    return lax.dot_general(a, b, (((1,), (1,)), ((), ())), preferred_element_type=F32)


def iota(shape, dim):
    return lax.broadcasted_iota(jnp.int32, shape, dim)


def kernel(
    len_ref, q_ref, k_ref, v_ref, res_ref, go_ref, wo_hbm, wp_hbm, ng_ref, taps_ref, cb_ref, cg_ref,
    bo_ref, gr_ref, gq_ref, gk_ref, gv_ref, gp_ref, gw_ref, small_ref,
    wo, wp, snd, rcv, kaug, qaug, vta, vaug, pt, inv, obuf, att_t, att, mixed, n1, r1, cin, cp, csum,
    gact, gm, act, gc, gcl, gpad, vacc, lh, rh, dsnd, do, doaug, qz, dz, kt, dst, snd2, rcv2,
    w_sem, s_q, r_q, s_o, r_o, s_d, r_d, s_g, r_g, s_h, r_h,
):
    me = lax.axis_index("ctx")
    dp = lax.axis_index("dp")
    length = len_ref[0]

    def at(offset):
        return lax.rem(me + (offset + N), N)

    wp_copy = pltpu.make_async_copy(wp_hbm, wp, w_sem.at[0])
    wo_copy = pltpu.make_async_copy(wo_hbm, wo, w_sem.at[1])
    wp_copy.start()
    wo_copy.start()

    barrier = pltpu.get_barrier_semaphore()
    for o in range(1, N):
        pl.semaphore_signal(barrier, inc=1, device_id=(dp, at(o)), device_id_type=MESH)

    def exchange(source, target, send_sem, recv_sem, h):
        def copy(o):
            return pltpu.make_async_remote_copy(
                src_ref=source.at[h, at(o)],
                dst_ref=target.at[h, me],
                send_sem=send_sem.at[h, o],
                recv_sem=recv_sem.at[h, o],
                device_id=(dp, at(o)),
                device_id_type=MESH,
            )

        def arrival(o):
            block = target.at[h, at(-o)]
            return pltpu.make_async_remote_copy(
                src_ref=block,
                dst_ref=block,
                send_sem=send_sem.at[h, o],
                recv_sem=recv_sem.at[h, o],
                device_id=(dp, at(-o)),
                device_id_type=MESH,
            )

        def start():
            for o in (4, 3, 5, 2, 6, 1, 7):
                copy(o).start()
            target[h, me] = source[h, me]

        def wait():
            for o in range(1, N):
                arrival(o).wait_recv()

        def drain():
            for o in range(1, N):
                copy(o).wait_send()

        return start, wait, drain

    ex_q = [exchange(snd, rcv, s_q, r_q, h) for h in range(3)]
    ex_o = [exchange(obuf, att_t, s_o, r_o, h) for h in range(3)]
    ex_d = [exchange(dsnd, do, s_d, r_d, h) for h in range(3)]
    ex_g = [exchange(snd2, rcv2, s_g, r_g, h) for h in range(3)]

    for h in range(3):
        for b in range(4):
            cols = slice((4 * h + b) * 128, (4 * h + b + 1) * 128)
            for a, ref in enumerate((q_ref, k_ref, v_ref)):
                block = ref[:, cols]
                if a == 0:
                    block = (block.astype(F32) * 0.125).astype(BF)
                block = block.T
                snd[h, 2 * b, a * HD : (a + 1) * HD, :] = block[:HD]
                snd[h, 2 * b + 1, a * HD : (a + 1) * HD, :] = block[HD:]
        if h == 0:
            pl.semaphore_wait(barrier, N - 1)
        ex_q[h][0]()

    own_valid = me * F + iota((F, 1), 0) < length
    gm[...] = jnp.where(own_valid, go_ref[...], jnp.zeros_like(go_ref))
    wp_copy.wait()

    def act_grad(c, carry):
        cols = pl.ds(pl.multiple_of(c * 256, 256), 256)
        gact[:, cols] = dot_nt(gm[...], wp[cols, :])
        return carry

    lax.fori_loop(0, D // 256, act_grad, 0)

    qaug[HD:, :] = (iota((HD, S), 0) == 0).astype(F32).astype(BF)
    vta[HD:, :] = (iota((16, S), 0) == 0).astype(F32).astype(BF)
    qz[HD:, :] = jnp.zeros((HD, S), BF)
    dz[:HD, :] = jnp.zeros((HD, S), BF)
    doaug[16:HD, :] = jnp.zeros((HD - 16, S), BF)

    for h in range(3):
        ex_q[h][1]()
        lane = iota((F, 128), 1)
        for j in range(N):
            cols = slice(j * F, (j + 1) * F)
            qaug[:HD, cols] = rcv[h, j, :HD, :]
            vta[:HD, cols] = rcv[h, j, 2 * HD :, :]
            both = rcv[h, j, HD:, :].T
            bias = jnp.where(j * F + iota((F, 128), 0) < length, 0.0, MASKED)
            bias = jnp.where(lane == HD, bias, 0.0).astype(BF)
            ones = jnp.where(lane < 2, 1.0, 0.0).astype(BF)
            kaug[cols, :] = jnp.where(lane < HD, both, bias)
            vaug[h, cols, :] = jnp.where(lane < HD, ones, both)

        def attend(i, carry, h=h):
            cols = pl.ds(pl.multiple_of(i * TILE, TILE), TILE)
            scores = dot(kaug[...], qaug[:, cols])
            top = jnp.max(scores, axis=0, keepdims=True)
            weights = jnp.exp(scores - top).astype(BF)
            pt[h, :, cols] = weights
            summed = dot(vta[...], weights)
            scale = 1.0 / summed[HD : HD + 1, :]
            inv[h, :, cols] = scale
            rows = (summed[:HD] * scale).astype(BF)
            for a in range(TILE // F):
                obuf[h, i * (TILE // F) + a] = rows[:, a * F : (a + 1) * F]
            return carry

        lax.fori_loop(0, S // TILE, attend, 0)
        ex_o[h][0]()

    wo_copy.wait()
    for h in range(3):
        ex_o[h][1]()
        for b in range(4):
            pair = jnp.concatenate([att_t[h, 2 * b], att_t[h, 2 * b + 1]], axis=0)
            att[:, (4 * h + b) * 128 : (4 * h + b + 1) * 128] = pair.T

        def project(c, carry, h=h):
            cols = pl.ds(pl.multiple_of(c * 256, 256), 256)
            before = res_ref[:, cols].astype(F32) if h == 0 else mixed[:, cols]
            mixed[:, cols] = before + dot(
                att[:, 512 * h : 512 * (h + 1)], wo[512 * h : 512 * (h + 1), cols]
            )
            return carry

        lax.fori_loop(0, D // 256, project, 0)

    def mean_of(x):
        return jnp.sum(x, axis=1, keepdims=True) * (1.0 / D)

    def first_norm(i, carry):
        rows = pl.ds(pl.multiple_of(i * 16, 16), 16)
        x = mixed[rows, :]
        x = x - mean_of(x)
        r = lax.rsqrt(mean_of(x * x) + EPSILON)
        n = x * r
        n1[rows, :] = n
        r1[rows, :] = r
        valid = me * F + i * 16 + iota((16, 1), 0) < length
        low = jnp.where(valid, n * ng_ref[...], 0.0).astype(BF)
        cin[rows, :] = low
        wide = low.astype(F32)
        for c in range(NB):
            cp[c, pl.ds(pl.multiple_of(16 + i * 16, 16), 16), :] = wide[:, c * 128 : (c + 1) * 128]
        return carry

    lax.fori_loop(0, F // 16, first_norm, 0)

    def edges(buffer, k):
        to_right = pltpu.make_async_remote_copy(
            src_ref=buffer.at[pl.ds(F - 16, 16)],
            dst_ref=lh.at[k],
            send_sem=s_h.at[2 * k],
            recv_sem=r_h.at[2 * k],
            device_id=(dp, at(1)),
            device_id_type=MESH,
        )
        to_left = pltpu.make_async_remote_copy(
            src_ref=buffer.at[pl.ds(0, 16)],
            dst_ref=rh.at[k],
            send_sem=s_h.at[2 * k + 1],
            recv_sem=r_h.at[2 * k + 1],
            device_id=(dp, at(-1)),
            device_id_type=MESH,
        )
        return to_right, to_left

    def place_edges(k, padded):
        left = jnp.where(me > 0, lh[k].astype(F32), 0.0)
        right = jnp.where(me < N - 1, rh[k].astype(F32), 0.0)
        for c in range(NB):
            padded[c, 0:16, :] = left[:, c * 128 : (c + 1) * 128]
            padded[c, F + 16 : F + 32, :] = right[:, c * 128 : (c + 1) * 128]

    halo = edges(cin, 0)
    for copy in halo:
        copy.start()
    for copy in halo:
        copy.wait()
    place_edges(0, cp)

    def convolve(c, carry):
        cols = pl.ds(pl.multiple_of(c * 128, 128), 128)
        total = jnp.broadcast_to(cb_ref[:, cols], (F, 128))
        for t in range(KERN):
            total = total + cp[c, t + 1 : t + 1 + F, :] * taps_ref[t : t + 1, cols]
        csum[:, cols] = total
        return carry

    lax.fori_loop(0, NB, convolve, 0)

    vacc[...] = jnp.zeros_like(vacc)

    def fold(x):
        return x[:8] + x[8:]

    def second_norm(i, carry):
        rows = pl.ds(pl.multiple_of(i * 16, 16), 16)
        x = csum[rows, :]
        x = x - mean_of(x)
        r = lax.rsqrt(mean_of(x * x) + EPSILON)
        n = x * r
        y = n * cg_ref[...]
        g = jax.nn.sigmoid(y)
        act[rows, :] = (y * g).astype(BF)
        back = gact[rows, :] * g * (1.0 + y * (1.0 - g))
        vacc[2] += fold(back * n)
        u = back * cg_ref[...]
        grad = r * (u - mean_of(u) - n * mean_of(u * n))
        vacc[0] += fold(grad)
        low = grad.astype(BF)
        gcl[rows, :] = low
        wide = low.astype(F32)
        for c in range(NB):
            cols = slice(c * 128, (c + 1) * 128)
            gc[c, rows, :] = grad[:, cols]
            gpad[c, pl.ds(pl.multiple_of(16 + i * 16, 16), 16), :] = wide[:, cols]
        return carry

    lax.fori_loop(0, F // 16, second_norm, 0)

    halo2 = edges(gcl, 1)
    for copy in halo2:
        copy.start()

    def block_cols(c, carry):
        cols = pl.ds(pl.multiple_of(c * 256, 256), 256)
        bo_ref[:, cols] = (mixed[:, cols] + dot(act[...], wp[:, cols])).astype(BF)
        return carry

    lax.fori_loop(0, D // 256, block_cols, 0)

    def point_rows(c, carry):
        cols = pl.ds(pl.multiple_of(c * 128, 128), 128)
        gp_ref[cols, :] = dot(gm[:, cols].T, act[...])
        return carry

    lax.fori_loop(0, NB, point_rows, 0)

    for copy in halo2:
        copy.wait()
    place_edges(1, gpad)

    def convolve_back(c, carry):
        cols = pl.ds(pl.multiple_of(c * 128, 128), 128)
        total = jnp.zeros((F, 128), F32)
        for t in range(KERN):
            total = total + gpad[c, KERN - t : KERN - t + F, :] * taps_ref[t : t + 1, cols]
        csum[:, cols] = jnp.where(me * F + iota((F, 1), 0) < length, total, 0.0)
        return carry

    lax.fori_loop(0, NB, convolve_back, 0)

    def first_norm_back(i, carry):
        rows = pl.ds(pl.multiple_of(i * 16, 16), 16)
        x = csum[rows, :]
        n = n1[rows, :]
        vacc[1] += fold(x * n)
        u = x * ng_ref[...]
        grad = r1[rows, :] * (u - mean_of(u) - n * mean_of(u * n))
        gr_ref[rows, :] = (gm[rows, :].astype(F32) + grad).astype(BF)
        return carry

    lax.fori_loop(0, F // 16, first_norm_back, 0)

    for h in range(3):

        def attended_rows(j, carry, h=h):
            for a in range(2):
                rows = pl.ds(pl.multiple_of(512 * h + (2 * j + a) * 128, 128), 128)
                part = dot_nt(wo[rows, :], gr_ref[...]).astype(BF)
                dsnd[h, 4 * j + 2 * a] = part[:HD]
                dsnd[h, 4 * j + 2 * a + 1] = part[HD:]
            return carry

        lax.fori_loop(0, 2, attended_rows, 0)
        ex_d[h][0]()

    def out_rows(c, carry):
        cols = pl.ds(pl.multiple_of(c * 128, 128), 128)
        gw_ref[cols, :] = dot(gr_ref[:, cols].T, att[...])
        return carry

    lax.fori_loop(0, NB, out_rows, 0)

    def tap_rows(c, carry):
        cols = pl.ds(pl.multiple_of(c * 128, 128), 128)
        grad = gc[c]
        for t in range(KERN):
            small_ref[t : t + 1, cols] = jnp.sum(cp[c, t + 1 : t + 1 + F, :] * grad, axis=0, keepdims=True)
        return carry

    lax.fori_loop(0, NB, tap_rows, 0)
    for i in range(3):
        small_ref[KERN + i : KERN + i + 1, :] = jnp.sum(vacc[i], axis=0, keepdims=True)
    small_ref[KERN + 3 :, :] = jnp.zeros((40 - KERN - 3, D), F32)

    for h in range(3):
        ex_d[h][1]()
        row = iota((16, F), 0)
        for j in range(N):
            cols = slice(j * F, (j + 1) * F)
            grad = do[h, j].astype(F32)
            scale = inv[h, :, cols]
            delta = -scale * jnp.sum(grad * obuf[h, j].astype(F32), axis=0, keepdims=True)
            high = delta.astype(BF).astype(F32)
            doaug[:16, cols] = jnp.where(row == 0, high, jnp.where(row == 1, delta - high, 0.0)).astype(BF)
            scaled = (grad * scale).astype(BF)
            doaug[HD:, cols] = scaled
            dz[HD:, cols] = scaled
            qz[:HD, cols] = rcv[h, j, :HD, :]
            kt[:, cols] = rcv[h, j, HD : 2 * HD, :]

        def back_queries(i, carry, h=h):
            cols = pl.ds(pl.multiple_of(i * TILE, TILE), TILE)
            grads = dot(vaug[h], doaug[:, cols])
            grads = (pt[h, :, cols].astype(F32) * grads).astype(BF)
            dst[:, cols] = grads
            rows = (dot(kt[...], grads) * 0.125).astype(BF)
            for a in range(TILE // F):
                snd2[h, i * (TILE // F) + a, :HD] = rows[:, a * F : (a + 1) * F]
            return carry

        lax.fori_loop(0, S // TILE, back_queries, 0)

        def back_keys(j, carry, h=h):
            rows = pl.ds(pl.multiple_of(j * F, F), F)
            both = dot_nt(dst[rows, :], qz[...]) + dot_nt(pt[h, rows, :], dz[...])
            snd2[h, j, HD:] = both.T.astype(BF)
            return carry

        lax.fori_loop(0, N, back_keys, 0)
        ex_g[h][0]()

    for h in range(3):
        ex_g[h][1]()
        for b in range(4):
            cols = slice((4 * h + b) * 128, (4 * h + b + 1) * 128)
            for a, ref in enumerate((gq_ref, gk_ref, gv_ref)):
                part = slice(a * HD, (a + 1) * HD)
                pair = jnp.concatenate([rcv2[h, 2 * b, part], rcv2[h, 2 * b + 1, part]], axis=0)
                ref[:, cols] = pair.T

    for group in (ex_q, ex_o, ex_d, ex_g):
        for h in range(3):
            group[h][2]()


def fused(lengths, q, k, v, res, go, wo, wp, ng, taps, cb, cg):
    vmem = pl.BlockSpec(memory_space=pltpu.VMEM)
    hbm = pl.BlockSpec(memory_space=pl.ANY)
    smem = pl.BlockSpec(memory_space=pltpu.SMEM)
    rows = jax.ShapeDtypeStruct((F, D), BF)
    dma = pltpu.SemaphoreType.DMA
    scratch = [
        pltpu.VMEM((D, D), BF),
        pltpu.VMEM((D, D), BF),
        pltpu.VMEM((3, N, 3 * HD, F), BF),
        pltpu.VMEM((3, N, 3 * HD, F), BF),
        pltpu.VMEM((S, 128), BF),
        pltpu.VMEM((128, S), BF),
        pltpu.VMEM((HD + 16, S), BF),
        pltpu.VMEM((3, S, 128), BF),
        pltpu.VMEM((3, S, S), BF),
        pltpu.VMEM((3, 1, S), F32),
        pltpu.VMEM((3, N, HD, F), BF),
        pltpu.VMEM((3, N, HD, F), BF),
        pltpu.VMEM((F, D), BF),
        pltpu.VMEM((F, D), F32),
        pltpu.VMEM((F, D), F32),
        pltpu.VMEM((F, 1), F32),
        pltpu.VMEM((F, D), BF),
        pltpu.VMEM((NB, F + 32, 128), F32),
        pltpu.VMEM((F, D), F32),
        pltpu.VMEM((F, D), F32),
        pltpu.VMEM((F, D), BF),
        pltpu.VMEM((F, D), BF),
        pltpu.VMEM((NB, F, 128), F32),
        pltpu.VMEM((F, D), BF),
        pltpu.VMEM((NB, F + 32, 128), F32),
        pltpu.VMEM((3, 8, D), F32),
        pltpu.VMEM((2, 16, D), BF),
        pltpu.VMEM((2, 16, D), BF),
        pltpu.VMEM((3, N, HD, F), BF),
        pltpu.VMEM((3, N, HD, F), BF),
        pltpu.VMEM((128, S), BF),
        pltpu.VMEM((128, S), BF),
        pltpu.VMEM((128, S), BF),
        pltpu.VMEM((HD, S), BF),
        pltpu.VMEM((S, S), BF),
        pltpu.VMEM((3, N, 3 * HD, F), BF),
        pltpu.VMEM((3, N, 3 * HD, F), BF),
        dma((2,)),
        dma((3, N)), dma((3, N)),
        dma((3, N)), dma((3, N)),
        dma((3, N)), dma((3, N)),
        dma((3, N)), dma((3, N)),
        dma((4,)), dma((4,)),
    ]
    return pl.pallas_call(
        kernel,
        out_shape=[rows] * 5
        + [
            jax.ShapeDtypeStruct((D, D), F32),
            jax.ShapeDtypeStruct((D, D), F32),
            jax.ShapeDtypeStruct((40, D), F32),
        ],
        in_specs=[smem] + [vmem] * 5 + [hbm] * 2 + [vmem] * 4,
        out_specs=[vmem] * 8,
        scratch_shapes=scratch,
        compiler_params=pltpu.CompilerParams(
            collective_id=0, has_side_effects=True, vmem_limit_bytes=60 * 1024 * 1024
        ),
    )(lengths, q, k, v, res, go, wo, wp, ng, taps, cb, cg)


def local(
    residual_in, query_rows, key_rows, value_rows, lengths, out_weight, norm_gain, conv_kernel,
    conv_bias, conv_gain, point_weight, grad_out,
):
    outs = fused(
        lengths, query_rows[0], key_rows[0], value_rows[0], residual_in[0], grad_out[0],
        out_weight, point_weight, norm_gain[None], conv_kernel, conv_bias[None], conv_gain[None],
    )
    rows = [x[None] for x in outs[:5]]
    point_term, out_term, small = outs[5:]
    axes = ("dp", "ctx")
    out_grad = lax.psum_scatter(out_term, axes, scatter_dimension=0, tiled=True).T
    point_grad = lax.psum_scatter(point_term, axes, scatter_dimension=0, tiled=True).T
    small = lax.psum_scatter(small, axes, scatter_dimension=1, tiled=True)
    return (*rows, out_grad, point_grad, small[:KERN], small[KERN : KERN + 3])


def solution(mesh):
    rows = P("dp", "ctx", None)
    split = P(None, ("dp", "ctx"))
    in_specs = (rows,) * 4 + (P("dp"),) + (P(),) * 6 + (rows,)
    out_specs = (rows,) * 5 + (split,) * 4
    return jax.shard_map(local, mesh=mesh, in_specs=in_specs, out_specs=out_specs, check_vma=False)
```

```python
import jax
import jax.numpy as jnp
from jax import lax
from jax.experimental import pallas as pl
from jax.experimental.pallas import tpu as pltpu
from jax.sharding import PartitionSpec as P

N = 8
F = 128
D = 1536
S = 1024
HD = 64
KERN = 31
NB = D // 128
TILE = 256
EPSILON = 1e-05
MASKED = -1e30
MESH = pl.DeviceIdType.MESH
BF = jnp.bfloat16
F32 = jnp.float32


def dot(a, b):
    return jnp.dot(a, b, preferred_element_type=F32)


def dot_nt(a, b):
    return lax.dot_general(a, b, (((1,), (1,)), ((), ())), preferred_element_type=F32)


def iota(shape, dim):
    return lax.broadcasted_iota(jnp.int32, shape, dim)


def kernel(
    len_ref, q_ref, k_ref, v_ref, res_ref, go_ref, wo_hbm, wp_hbm, ng_ref, taps_ref, cb_ref, cg_ref,
    bo_ref, gr_ref, gq_ref, gk_ref, gv_ref, gow_ref, gpw_ref, gker_ref, gvec_ref,
    wo, wp, snd, rcv, kaug, qaug, vta, vaug, pt, inv, obuf, att_t, att, mixed, n1, r1, cin, cp, csum,
    gact, gm, act, gc, gcl, gpad, vacc, lh, rh, dsnd, do, doaug, qz, dz, kt, dst, snd2, rcv2,
    ng, cg, small_t, rows_t, pterm, p1, pa, pb, p3, px, p4, oterm, o1, oa, ob, o3, ox, o4, wide,
    w_sem, s_q, r_q, s_o, r_o, s_d, r_d, s_g, r_g, s_h, r_h, s_p, r_p, s_w, r_w,
):
    me = lax.axis_index("ctx")
    dp = lax.axis_index("dp")
    length = len_ref[0]
    core = lax.rem(dp, 2)
    y = lax.rem(lax.div(dp, 2), 2)
    z = lax.div(dp, 4)
    z_up, z_down, z_far = lax.rem(z + 1, 4), lax.rem(z + 3, 4), lax.rem(z + 2, 4)
    sibling = (dp + 1 - 2 * core, me)
    across = (dp + 2 - 4 * y, me)
    upper = (4 * z_up + 2 * y + core, me)
    lower = (4 * z_down + 2 * y + core, me)

    def at(offset):
        return lax.rem(me + (offset + N), N)

    wp_copy = pltpu.make_async_copy(wp_hbm, wp, w_sem.at[0])
    wo_copy = pltpu.make_async_copy(wo_hbm, wo, w_sem.at[1])
    wp_copy.start()
    wo_copy.start()

    barrier = pltpu.get_barrier_semaphore()
    for o in range(1, N):
        pl.semaphore_signal(barrier, inc=1, device_id=(dp, at(o)), device_id_type=MESH)
    for peer in (sibling, across, upper, lower):
        pl.semaphore_signal(barrier, inc=1, device_id=peer, device_id_type=MESH)

    def exchange(source, target, send_sem, recv_sem, h):
        def copy(o):
            return pltpu.make_async_remote_copy(
                src_ref=source.at[h, at(o)],
                dst_ref=target.at[h, me],
                send_sem=send_sem.at[h, o],
                recv_sem=recv_sem.at[h, o],
                device_id=(dp, at(o)),
                device_id_type=MESH,
            )

        def arrival(o):
            block = target.at[h, at(-o)]
            return pltpu.make_async_remote_copy(
                src_ref=block,
                dst_ref=block,
                send_sem=send_sem.at[h, o],
                recv_sem=recv_sem.at[h, o],
                device_id=(dp, at(-o)),
                device_id_type=MESH,
            )

        def start():
            for o in (4, 3, 5, 2, 6, 1, 7):
                copy(o).start()
            target[h, me] = source[h, me]

        def wait():
            for o in range(1, N):
                arrival(o).wait_recv()

        def drain():
            for o in range(1, N):
                copy(o).wait_send()

        return start, wait, drain

    ex_q = [exchange(snd, rcv, s_q, r_q, h) for h in range(3)]
    ex_o = [exchange(obuf, att_t, s_o, r_o, h) for h in range(3)]
    ex_d = [exchange(dsnd, do, s_d, r_d, h) for h in range(3)]
    ex_g = [exchange(snd2, rcv2, s_g, r_g, h) for h in range(3)]

    def reducer(term, first, far, near, pair, split, last, send_sem, recv_sem):
        def to(source, target, k, device):
            return pltpu.make_async_remote_copy(
                src_ref=source,
                dst_ref=target,
                send_sem=send_sem.at[k],
                recv_sem=recv_sem.at[k],
                device_id=device,
                device_id_type=MESH,
            )

        def cores(i):
            return to(term.at[1 - core, i], first.at[i], i, sibling)

        far_copies = (
            to(term.at[core, 2 * z_far], far.at[0], 8, upper),
            to(term.at[core, 2 * z_far + 1], far.at[1], 9, lower),
        )
        plain_copies = (
            to(term.at[core, 2 * z_up + 1], near.at[0, 1], 10, upper),
            to(term.at[core, 2 * z_down], near.at[1, 0], 11, lower),
        )
        joint_copies = (
            to(term.at[core, 2 * z_up], near.at[0, 0], 12, upper),
            to(term.at[core, 2 * z_down + 1], near.at[1, 1], 13, lower),
        )
        y_copy = to(term.at[core, 2 * z + 1 - y], pair, 14, across)

        def ctx_copy(o):
            return to(split.at[at(o)], last.at[me], 15 + o, (dp, at(o)))

        def ctx_arrival(o):
            return to(split.at[at(o)], last.at[at(-o)], 15 + o, (dp, at(-o)))

        def start_z():
            def add(i, carry):
                cores(i).wait_recv()
                term[core, i] = term[core, i] + first[i]
                return carry

            lax.fori_loop(0, 8, add, 0)
            for copy in far_copies + plain_copies:
                copy.start()

        def join_z():
            for copy, i in zip(far_copies, (2 * z_up, 2 * z_down + 1)):
                copy.wait_recv()
                term[core, i] = term[core, i] + far[0 if copy is far_copies[0] else 1]
            for copy in joint_copies:
                copy.start()

        def start_y():
            for copy in plain_copies + joint_copies:
                copy.wait_recv()
            for a in (0, 1):
                total = near[0, a].astype(F32) + near[1, a].astype(F32)
                term[core, 2 * z + a] = (term[core, 2 * z + a].astype(F32) + total).astype(BF)
            y_copy.start()

        def start_ctx():
            y_copy.wait_recv()
            width = term.shape[3]
            wide[96:, :width] = jnp.zeros((8, width), F32)
            wide[:96, :width] = term[core, 2 * z + y].astype(F32) + pair[...].astype(F32)
            for j in range(N):
                split[j] = wide[12 * j : 12 * j + 16, :width].astype(BF)
            for o in range(1, N):
                ctx_copy(o).start()
            last[me] = split[me]

        def finish():
            for o in range(1, N):
                ctx_arrival(o).wait_recv()
            total = last[0].astype(F32)
            for j in range(1, N):
                total = total + last[j].astype(F32)
            return total

        def drain():
            for i in range(8):
                cores(i).wait_send()
            for copy in far_copies + plain_copies + joint_copies + (y_copy,):
                copy.wait_send()
            for o in range(1, N):
                ctx_copy(o).wait_send()

        return cores, start_z, join_z, start_y, start_ctx, finish, drain

    point = reducer(pterm, p1, pa, pb, p3, px, p4, s_p, r_p)
    out = reducer(oterm, o1, oa, ob, o3, ox, o4, s_w, r_w)

    def weight_term(rows, others, term, send):
        for c in range(NB):
            rows_t[c * 128 : (c + 1) * 128, :] = rows[:, c * 128 : (c + 1) * 128].T

        def block(i, carry):
            left = rows_t[pl.ds(pl.multiple_of(i * 192, 192), 192), :]
            for n in range(3):
                cols = slice(n * 512, (n + 1) * 512)
                part = dot(left, others[:, cols]).astype(BF)
                term[0, i, :, cols] = part[:96]
                term[1, i, :, cols] = part[96:]
            if term.shape[3] > D:
                for a in range(2):
                    at_rows = pl.ds(pl.multiple_of(i * 192 + a * 96, 96), 96)
                    term[a, i, :, D:] = small_t[at_rows, :]
            send(i).start()
            return carry

        lax.fori_loop(0, 8, block, 0)

    for h in range(3):
        for b in range(4):
            cols = slice((4 * h + b) * 128, (4 * h + b + 1) * 128)
            for a, ref in enumerate((q_ref, k_ref, v_ref)):
                block = ref[:, cols]
                if a == 0:
                    block = (block.astype(F32) * 0.125).astype(BF)
                block = block.T
                snd[h, 2 * b, a * HD : (a + 1) * HD, :] = block[:HD]
                snd[h, 2 * b + 1, a * HD : (a + 1) * HD, :] = block[HD:]
        if h == 0:
            pl.semaphore_wait(barrier, N + 3)
        ex_q[h][0]()

    for c in range(NB):
        ng[:, c * 128 : (c + 1) * 128] = ng_ref[c : c + 1, :]
        cg[:, c * 128 : (c + 1) * 128] = cg_ref[c : c + 1, :]

    own_valid = me * F + iota((F, 1), 0) < length
    gm[...] = jnp.where(own_valid, go_ref[...], jnp.zeros_like(go_ref))
    wp_copy.wait()

    def act_grad(c, carry):
        cols = pl.ds(pl.multiple_of(c * 256, 256), 256)
        gact[:, cols] = dot_nt(gm[...], wp[cols, :])
        return carry

    lax.fori_loop(0, D // 256, act_grad, 0)

    qaug[HD:, :] = (iota((HD, S), 0) == 0).astype(F32).astype(BF)
    vta[HD:, :] = (iota((16, S), 0) == 0).astype(F32).astype(BF)
    qz[HD:, :] = jnp.zeros((HD, S), BF)
    dz[:HD, :] = jnp.zeros((HD, S), BF)
    doaug[16:HD, :] = jnp.zeros((HD - 16, S), BF)

    for h in range(3):
        ex_q[h][1]()
        lane = iota((F, 128), 1)
        for j in range(N):
            cols = slice(j * F, (j + 1) * F)
            qaug[:HD, cols] = rcv[h, j, :HD, :]
            vta[:HD, cols] = rcv[h, j, 2 * HD :, :]
            both = rcv[h, j, HD:, :].T
            bias = jnp.where(j * F + iota((F, 128), 0) < length, 0.0, MASKED)
            bias = jnp.where(lane == HD, bias, 0.0).astype(BF)
            ones = jnp.where(lane < 2, 1.0, 0.0).astype(BF)
            kaug[cols, :] = jnp.where(lane < HD, both, bias)
            vaug[h, cols, :] = jnp.where(lane < HD, ones, both)

        def attend(i, carry, h=h):
            cols = pl.ds(pl.multiple_of(i * TILE, TILE), TILE)
            scores = dot(kaug[...], qaug[:, cols])
            top = jnp.max(scores, axis=0, keepdims=True)
            weights = jnp.exp(scores - top).astype(BF)
            pt[h, :, cols] = weights
            summed = dot(vta[...], weights)
            scale = 1.0 / summed[HD : HD + 1, :]
            inv[h, :, cols] = scale
            rows = (summed[:HD] * scale).astype(BF)
            for a in range(TILE // F):
                obuf[h, i * (TILE // F) + a] = rows[:, a * F : (a + 1) * F]
            return carry

        lax.fori_loop(0, S // TILE, attend, 0)
        ex_o[h][0]()

    wo_copy.wait()
    for h in range(3):
        ex_o[h][1]()
        for b in range(4):
            pair = jnp.concatenate([att_t[h, 2 * b], att_t[h, 2 * b + 1]], axis=0)
            att[:, (4 * h + b) * 128 : (4 * h + b + 1) * 128] = pair.T

        def project(c, carry, h=h):
            cols = pl.ds(pl.multiple_of(c * 256, 256), 256)
            before = res_ref[:, cols].astype(F32) if h == 0 else mixed[:, cols]
            mixed[:, cols] = before + dot(
                att[:, 512 * h : 512 * (h + 1)], wo[512 * h : 512 * (h + 1), cols]
            )
            return carry

        lax.fori_loop(0, D // 256, project, 0)

    def mean_of(x):
        return jnp.sum(x, axis=1, keepdims=True) * (1.0 / D)

    def first_norm(i, carry):
        rows = pl.ds(pl.multiple_of(i * 16, 16), 16)
        x = mixed[rows, :]
        x = x - mean_of(x)
        r = lax.rsqrt(mean_of(x * x) + EPSILON)
        n = x * r
        n1[rows, :] = n
        r1[rows, :] = r
        valid = me * F + i * 16 + iota((16, 1), 0) < length
        low = jnp.where(valid, n * ng[...], 0.0).astype(BF)
        cin[rows, :] = low
        wide = low.astype(F32)
        for c in range(NB):
            cp[c, pl.ds(pl.multiple_of(16 + i * 16, 16), 16), :] = wide[:, c * 128 : (c + 1) * 128]
        return carry

    lax.fori_loop(0, F // 16, first_norm, 0)

    def edges(buffer, k):
        to_right = pltpu.make_async_remote_copy(
            src_ref=buffer.at[pl.ds(F - 16, 16)],
            dst_ref=lh.at[k],
            send_sem=s_h.at[2 * k],
            recv_sem=r_h.at[2 * k],
            device_id=(dp, at(1)),
            device_id_type=MESH,
        )
        to_left = pltpu.make_async_remote_copy(
            src_ref=buffer.at[pl.ds(0, 16)],
            dst_ref=rh.at[k],
            send_sem=s_h.at[2 * k + 1],
            recv_sem=r_h.at[2 * k + 1],
            device_id=(dp, at(-1)),
            device_id_type=MESH,
        )
        return to_right, to_left

    def place_edges(k, padded):
        left = jnp.where(me > 0, lh[k].astype(F32), 0.0)
        right = jnp.where(me < N - 1, rh[k].astype(F32), 0.0)
        for c in range(NB):
            padded[c, 0:16, :] = left[:, c * 128 : (c + 1) * 128]
            padded[c, F + 16 : F + 32, :] = right[:, c * 128 : (c + 1) * 128]

    halo = edges(cin, 0)
    for copy in halo:
        copy.start()
    for copy in halo:
        copy.wait()
    place_edges(0, cp)

    def convolve(c, carry):
        cols = pl.ds(pl.multiple_of(c * 128, 128), 128)
        total = jnp.broadcast_to(cb_ref[pl.ds(c, 1), :], (F, 128))
        for t in range(KERN):
            total = total + cp[c, t + 1 : t + 1 + F, :] * taps_ref[t : t + 1, cols]
        csum[:, cols] = total
        return carry

    lax.fori_loop(0, NB, convolve, 0)

    vacc[...] = jnp.zeros_like(vacc)

    def fold(x):
        return x[:8] + x[8:]

    def second_norm(i, carry):
        rows = pl.ds(pl.multiple_of(i * 16, 16), 16)
        x = csum[rows, :]
        x = x - mean_of(x)
        r = lax.rsqrt(mean_of(x * x) + EPSILON)
        n = x * r
        y = n * cg[...]
        g = jax.nn.sigmoid(y)
        act[rows, :] = (y * g).astype(BF)
        back = gact[rows, :] * g * (1.0 + y * (1.0 - g))
        vacc[2] += fold(back * n)
        u = back * cg[...]
        grad = r * (u - mean_of(u) - n * mean_of(u * n))
        vacc[0] += fold(grad)
        low = grad.astype(BF)
        gcl[rows, :] = low
        wide = low.astype(F32)
        for c in range(NB):
            cols = slice(c * 128, (c + 1) * 128)
            gc[c, rows, :] = grad[:, cols]
            gpad[c, pl.ds(pl.multiple_of(16 + i * 16, 16), 16), :] = wide[:, cols]
        return carry

    lax.fori_loop(0, F // 16, second_norm, 0)

    halo2 = edges(gcl, 1)
    for copy in halo2:
        copy.start()

    def block_cols(c, carry):
        cols = pl.ds(pl.multiple_of(c * 256, 256), 256)
        bo_ref[:, cols] = (mixed[:, cols] + dot(act[...], wp[:, cols])).astype(BF)
        return carry

    lax.fori_loop(0, D // 256, block_cols, 0)

    weight_term(gm, act, pterm, point[0])

    for copy in halo2:
        copy.wait()
    place_edges(1, gpad)

    def convolve_back(c, carry):
        cols = pl.ds(pl.multiple_of(c * 128, 128), 128)
        total = jnp.zeros((F, 128), F32)
        for t in range(KERN):
            total = total + gpad[c, KERN - t : KERN - t + F, :] * taps_ref[t : t + 1, cols]
        csum[:, cols] = jnp.where(me * F + iota((F, 1), 0) < length, total, 0.0)
        return carry

    lax.fori_loop(0, NB, convolve_back, 0)
    point[1]()

    def first_norm_back(i, carry):
        rows = pl.ds(pl.multiple_of(i * 16, 16), 16)
        x = csum[rows, :]
        n = n1[rows, :]
        vacc[1] += fold(x * n)
        u = x * ng[...]
        grad = r1[rows, :] * (u - mean_of(u) - n * mean_of(u * n))
        gr_ref[rows, :] = (gm[rows, :].astype(F32) + grad).astype(BF)
        return carry

    lax.fori_loop(0, F // 16, first_norm_back, 0)

    for h in range(3):

        def attended_rows(j, carry, h=h):
            for a in range(2):
                rows = pl.ds(pl.multiple_of(512 * h + (2 * j + a) * 128, 128), 128)
                part = dot_nt(wo[rows, :], gr_ref[...]).astype(BF)
                dsnd[h, 4 * j + 2 * a] = part[:HD]
                dsnd[h, 4 * j + 2 * a + 1] = part[HD:]
            return carry

        lax.fori_loop(0, 2, attended_rows, 0)
        ex_d[h][0]()

    small = csum

    def tap_rows(c, carry):
        cols = pl.ds(pl.multiple_of(c * 128, 128), 128)
        grad = gc[c]
        for t in range(KERN):
            small[t : t + 1, cols] = jnp.sum(cp[c, t + 1 : t + 1 + F, :] * grad, axis=0, keepdims=True)
        return carry

    lax.fori_loop(0, NB, tap_rows, 0)
    for i in range(3):
        small[KERN + i : KERN + i + 1, :] = jnp.sum(vacc[i], axis=0, keepdims=True)
    small[KERN + 3 :, :] = jnp.zeros((128 - KERN - 3, D), F32)
    for c in range(NB):
        small_t[c * 128 : (c + 1) * 128, :] = small[:, c * 128 : (c + 1) * 128].T.astype(BF)
    weight_term(gr_ref, att, oterm, out[0])
    point[2]()

    for h in range(3):
        ex_d[h][1]()
        row = iota((16, F), 0)
        for j in range(N):
            cols = slice(j * F, (j + 1) * F)
            grad = do[h, j].astype(F32)
            scale = inv[h, :, cols]
            delta = -scale * jnp.sum(grad * obuf[h, j].astype(F32), axis=0, keepdims=True)
            high = delta.astype(BF).astype(F32)
            doaug[:16, cols] = jnp.where(row == 0, high, jnp.where(row == 1, delta - high, 0.0)).astype(BF)
            scaled = (grad * scale).astype(BF)
            doaug[HD:, cols] = scaled
            dz[HD:, cols] = scaled
            qz[:HD, cols] = rcv[h, j, :HD, :]
            kt[:, cols] = rcv[h, j, HD : 2 * HD, :]

        def back_queries(i, carry, h=h):
            cols = pl.ds(pl.multiple_of(i * TILE, TILE), TILE)
            grads = dot(vaug[h], doaug[:, cols])
            grads = (pt[h, :, cols].astype(F32) * grads).astype(BF)
            dst[:, cols] = grads
            rows = (dot(kt[...], grads) * 0.125).astype(BF)
            for a in range(TILE // F):
                snd2[h, i * (TILE // F) + a, :HD] = rows[:, a * F : (a + 1) * F]
            return carry

        lax.fori_loop(0, S // TILE, back_queries, 0)

        def back_keys(j, carry, h=h):
            rows = pl.ds(pl.multiple_of(j * F, F), F)
            both = dot_nt(dst[rows, :], qz[...]) + dot_nt(pt[h, rows, :], dz[...])
            snd2[h, j, HD:] = both.T.astype(BF)
            return carry

        lax.fori_loop(0, N, back_keys, 0)
        ex_g[h][0]()
        if h == 0:
            point[3]()
            out[1]()
        elif h == 1:
            point[4]()
            out[2]()
        else:
            out[3]()

    for h in range(3):
        ex_g[h][1]()
        for b in range(4):
            cols = slice((4 * h + b) * 128, (4 * h + b + 1) * 128)
            for a, ref in enumerate((gq_ref, gk_ref, gv_ref)):
                part = slice(a * HD, (a + 1) * HD)
                pair = jnp.concatenate([rcv2[h, 2 * b, part], rcv2[h, 2 * b + 1, part]], axis=0)
                ref[:, cols] = pair.T

        if h == 0:
            out[4]()

    point_total = point[5]()
    out_total = out[5]()
    for c in range(NB):
        cols = slice(c * 128, (c + 1) * 128)
        gpw_ref[cols, :] = point_total[:, cols].T[:, :12]
        gow_ref[cols, :] = out_total[:, cols].T[:, :12]
    tail = out_total[:, D:].T
    gker_ref[...] = tail[:KERN, :12]
    gvec_ref[...] = tail[KERN : KERN + 3, :12]
    point[6]()
    out[6]()
    for group in (ex_q, ex_o, ex_d, ex_g):
        for h in range(3):
            group[h][2]()


def fused(lengths, q, k, v, res, go, wo, wp, ng, taps, cb, cg):
    vmem = pl.BlockSpec(memory_space=pltpu.VMEM)
    hbm = pl.BlockSpec(memory_space=pl.ANY)
    smem = pl.BlockSpec(memory_space=pltpu.SMEM)
    rows = jax.ShapeDtypeStruct((F, D), BF)
    dma = pltpu.SemaphoreType.DMA
    scratch = [
        pltpu.VMEM((D, D), BF),
        pltpu.VMEM((D, D), BF),
        pltpu.VMEM((3, N, 3 * HD, F), BF),
        pltpu.VMEM((3, N, 3 * HD, F), BF),
        pltpu.VMEM((S, 128), BF),
        pltpu.VMEM((128, S), BF),
        pltpu.VMEM((HD + 16, S), BF),
        pltpu.VMEM((3, S, 128), BF),
        pltpu.VMEM((3, S, S), BF),
        pltpu.VMEM((3, 1, S), F32),
        pltpu.VMEM((3, N, HD, F), BF),
        pltpu.VMEM((3, N, HD, F), BF),
        pltpu.VMEM((F, D), BF),
        pltpu.VMEM((F, D), F32),
        pltpu.VMEM((F, D), F32),
        pltpu.VMEM((F, 1), F32),
        pltpu.VMEM((F, D), BF),
        pltpu.VMEM((NB, F + 32, 128), F32),
        pltpu.VMEM((F, D), F32),
        pltpu.VMEM((F, D), F32),
        pltpu.VMEM((F, D), BF),
        pltpu.VMEM((F, D), BF),
        pltpu.VMEM((NB, F, 128), F32),
        pltpu.VMEM((F, D), BF),
        pltpu.VMEM((NB, F + 32, 128), F32),
        pltpu.VMEM((3, 8, D), F32),
        pltpu.VMEM((2, 16, D), BF),
        pltpu.VMEM((2, 16, D), BF),
        pltpu.VMEM((3, N, HD, F), BF),
        pltpu.VMEM((3, N, HD, F), BF),
        pltpu.VMEM((128, S), BF),
        pltpu.VMEM((128, S), BF),
        pltpu.VMEM((128, S), BF),
        pltpu.VMEM((HD, S), BF),
        pltpu.VMEM((S, S), BF),
        pltpu.VMEM((3, N, 3 * HD, F), BF),
        pltpu.VMEM((3, N, 3 * HD, F), BF),
        pltpu.VMEM((1, D), F32),
        pltpu.VMEM((1, D), F32),
        pltpu.VMEM((D, 128), BF),
        pltpu.VMEM((D, F), BF),
        *[
            pltpu.VMEM(shape + (width,), BF)
            for width in (D, D + 128)
            for shape in ((2, 8, 96), (8, 96), (2, 96), (2, 2, 96), (96,), (N, 16), (N, 16))
        ],
        pltpu.VMEM((104, D + 128), F32),
        dma((2,)),
        dma((3, N)), dma((3, N)),
        dma((3, N)), dma((3, N)),
        dma((3, N)), dma((3, N)),
        dma((3, N)), dma((3, N)),
        dma((4,)), dma((4,)),
        dma((23,)), dma((23,)),
        dma((23,)), dma((23,)),
    ]
    return pl.pallas_call(
        kernel,
        out_shape=[rows] * 5
        + [
            jax.ShapeDtypeStruct((D, 12), F32),
            jax.ShapeDtypeStruct((D, 12), F32),
            jax.ShapeDtypeStruct((KERN, 12), F32),
            jax.ShapeDtypeStruct((3, 12), F32),
        ],
        in_specs=[smem] + [vmem] * 5 + [hbm] * 2 + [vmem] * 4,
        out_specs=[vmem] * 9,
        scratch_shapes=scratch,
        compiler_params=pltpu.CompilerParams(
            collective_id=0, has_side_effects=True, vmem_limit_bytes=62 * 1024 * 1024
        ),
    )(lengths, q, k, v, res, go, wo, wp, ng, taps, cb, cg)


def local(
    residual_in, query_rows, key_rows, value_rows, lengths, out_weight, norm_gain, conv_kernel,
    conv_bias, conv_gain, point_weight, grad_out,
):
    outs = fused(
        lengths, query_rows[0], key_rows[0], value_rows[0], residual_in[0], grad_out[0],
        out_weight, point_weight, norm_gain.reshape(NB, 128), conv_kernel,
        conv_bias.reshape(NB, 128), conv_gain.reshape(NB, 128),
    )
    return (*[x[None] for x in outs[:5]], *outs[5:])


def solution(mesh):
    rows = P("dp", "ctx", None)
    split = P(None, ("dp", "ctx"))
    in_specs = (rows,) * 4 + (P("dp"),) + (P(),) * 6 + (rows,)
    out_specs = (rows,) * 5 + (split,) * 4
    return jax.shard_map(local, mesh=mesh, in_specs=in_specs, out_specs=out_specs, check_vma=False)
```

```python
import jax
import jax.numpy as jnp
from jax import lax
from jax.experimental import pallas as pl
from jax.experimental.pallas import tpu as pltpu
from jax.sharding import PartitionSpec as P

N = 8
F = 128
D = 1536
S = 1024
HD = 64
KERN = 31
NB = D // 128
TILE = 256
EPSILON = 1e-05
MASKED = -1e30
MESH = pl.DeviceIdType.MESH
BF = jnp.bfloat16
F32 = jnp.float32


def dot(a, b):
    return jnp.dot(a, b, preferred_element_type=F32)


def dot_nt(a, b):
    return lax.dot_general(a, b, (((1,), (1,)), ((), ())), preferred_element_type=F32)


def iota(shape, dim):
    return lax.broadcasted_iota(jnp.int32, shape, dim)


def kernel(
    len_ref, q_hbm, k_hbm, v_hbm, res_hbm, go_hbm, wo_hbm, wp_hbm, ng_ref, taps_ref, cb_ref, cg_ref,
    bo_hbm, gr_hbm, gq_hbm, gk_hbm, gv_hbm, gw_ref, gp_ref,
    q_ref, k_ref, v_ref, res_ref, go_ref, bo_ref, gr_ref, gq_ref, gk_ref, gv_ref, wo, wp, snd, rcv, kaug, qaug, vta, vaug, pt, inv, obuf, att_t, att, mixed, n1, r1, cin, cp, csum,
    gact, gm, act, gc, gcl, gpad, vacc, lh, rh, dsnd, do, doaug, qz, dz, kt, dst, sq, rq, skv, rkv,
    ng, cg, small_t, rows_t, pterm, p1, pa, pb, p3, px, p4, oterm, o1, oa, ob, o3, ox, o4, wide,
    w_sem, i_sem, e_sem, s_q, r_q, s_o, r_o, s_d, r_d, s_g, r_g, s_k, r_k, s_h, r_h, s_p, r_p, s_w, r_w,
):
    me = lax.axis_index("ctx")
    dp = lax.axis_index("dp")
    length = len_ref[0]
    core = lax.rem(dp, 2)
    y = lax.rem(lax.div(dp, 2), 2)
    z = lax.div(dp, 4)
    z_up, z_down, z_far = lax.rem(z + 1, 4), lax.rem(z + 3, 4), lax.rem(z + 2, 4)
    sibling = (dp + 1 - 2 * core, me)
    across = (dp + 2 - 4 * y, me)
    upper = (4 * z_up + 2 * y + core, me)
    lower = (4 * z_down + 2 * y + core, me)

    def at(offset):
        return lax.rem(me + (offset + N), N)

    barrier = pltpu.get_barrier_semaphore()
    for o in range(1, N):
        pl.semaphore_signal(barrier, inc=1, device_id=(dp, at(o)), device_id_type=MESH)
    for peer in (sibling, across, upper, lower):
        pl.semaphore_signal(barrier, inc=1, device_id=peer, device_id_type=MESH)

    loads = [
        pltpu.make_async_copy(source, target, i_sem.at[i])
        for i, (source, target) in enumerate(
            ((q_hbm, q_ref), (k_hbm, k_ref), (v_hbm, v_ref), (go_hbm, go_ref), (res_hbm, res_ref))
        )
    ]
    for load in loads:
        load.start()
    wp_copy = pltpu.make_async_copy(wp_hbm, wp, w_sem.at[0])
    wo_copy = pltpu.make_async_copy(wo_hbm, wo, w_sem.at[1])
    wp_copy.start()
    wo_copy.start()

    def exchange(source, target, send_sem, recv_sem, h):
        def copy(o):
            return pltpu.make_async_remote_copy(
                src_ref=source.at[h, at(o)],
                dst_ref=target.at[h, me],
                send_sem=send_sem.at[h, o],
                recv_sem=recv_sem.at[h, o],
                device_id=(dp, at(o)),
                device_id_type=MESH,
            )

        def arrival(o):
            block = target.at[h, at(-o)]
            return pltpu.make_async_remote_copy(
                src_ref=block,
                dst_ref=block,
                send_sem=send_sem.at[h, o],
                recv_sem=recv_sem.at[h, o],
                device_id=(dp, at(-o)),
                device_id_type=MESH,
            )

        def start():
            for o in (4, 3, 5, 2, 6, 1, 7):
                copy(o).start()
            target[h, me] = source[h, me]

        def start_one(j):
            @pl.when(j != me)
            def _():
                o = lax.rem(j - me + N, N)
                pltpu.make_async_remote_copy(
                    src_ref=source.at[h, j],
                    dst_ref=target.at[h, me],
                    send_sem=send_sem.at[h, o],
                    recv_sem=recv_sem.at[h, o],
                    device_id=(dp, j),
                    device_id_type=MESH,
                ).start()

        def keep():
            target[h, me] = source[h, me]

        def wait():
            for o in range(1, N):
                arrival(o).wait_recv()

        def drain():
            for o in range(1, N):
                copy(o).wait_send()

        return start, wait, drain, start_one, keep

    ex_q = [exchange(snd, rcv, s_q, r_q, h) for h in range(3)]
    ex_o = [exchange(obuf, att_t, s_o, r_o, h) for h in range(3)]
    ex_d = [exchange(dsnd, do, s_d, r_d, h) for h in range(3)]
    ex_g = [exchange(sq, rq, s_g, r_g, h) for h in range(3)]
    ex_k = [exchange(skv, rkv, s_k, r_k, h) for h in range(3)]

    def reducer(term, first, far, near, pair, split, last, send_sem, recv_sem):
        def to(source, target, k, device):
            return pltpu.make_async_remote_copy(
                src_ref=source,
                dst_ref=target,
                send_sem=send_sem.at[k],
                recv_sem=recv_sem.at[k],
                device_id=device,
                device_id_type=MESH,
            )

        def cores(i):
            return to(term.at[1 - core, i], first.at[i], i, sibling)

        far_copies = (
            to(term.at[core, 2 * z_far], far.at[0], 8, upper),
            to(term.at[core, 2 * z_far + 1], far.at[1], 9, lower),
        )
        plain_copies = (
            to(term.at[core, 2 * z_up + 1], near.at[0, 1], 10, upper),
            to(term.at[core, 2 * z_down], near.at[1, 0], 11, lower),
        )
        joint_copies = (
            to(term.at[core, 2 * z_up], near.at[0, 0], 12, upper),
            to(term.at[core, 2 * z_down + 1], near.at[1, 1], 13, lower),
        )
        y_copy = to(term.at[core, 2 * z + 1 - y], pair, 14, across)

        def ctx_copy(o):
            return to(split.at[at(o)], last.at[me], 15 + o, (dp, at(o)))

        def ctx_arrival(o):
            return to(split.at[at(o)], last.at[at(-o)], 15 + o, (dp, at(-o)))

        def start_z():
            def add(i, carry):
                cores(i).wait_recv()
                term[core, i] = term[core, i] + first[i]
                return carry

            lax.fori_loop(0, 8, add, 0)
            for copy in far_copies + plain_copies:
                copy.start()

        def join_z():
            for copy, i in zip(far_copies, (2 * z_up, 2 * z_down + 1)):
                copy.wait_recv()
                term[core, i] = term[core, i] + far[0 if copy is far_copies[0] else 1]
            for copy in joint_copies:
                copy.start()

        def start_y():
            for copy in plain_copies + joint_copies:
                copy.wait_recv()
            for a in (0, 1):
                total = near[0, a].astype(F32) + near[1, a].astype(F32)
                term[core, 2 * z + a] = (term[core, 2 * z + a].astype(F32) + total).astype(BF)
            y_copy.start()

        def start_ctx():
            y_copy.wait_recv()
            width = term.shape[3]
            wide[96:, :width] = jnp.zeros((8, width), F32)
            wide[:96, :width] = term[core, 2 * z + y].astype(F32) + pair[...].astype(F32)
            for j in range(N):
                split[j] = wide[12 * j : 12 * j + 16, :width].astype(BF)
            for o in range(1, N):
                ctx_copy(o).start()
            last[me] = split[me]

        def finish():
            for o in range(1, N):
                ctx_arrival(o).wait_recv()
            total = last[0].astype(F32)
            for j in range(1, N):
                total = total + last[j].astype(F32)
            return total

        def drain():
            for i in range(8):
                cores(i).wait_send()
            for copy in far_copies + plain_copies + joint_copies + (y_copy,):
                copy.wait_send()
            for o in range(1, N):
                ctx_copy(o).wait_send()

        return cores, start_z, join_z, start_y, start_ctx, finish, drain

    point = reducer(pterm, p1, pa, pb, p3, px, p4, s_p, r_p)
    out = reducer(oterm, o1, oa, ob, o3, ox, o4, s_w, r_w)

    def weight_term(rows, others, term, send):
        for c in range(NB):
            rows_t[c * 128 : (c + 1) * 128, :] = rows[:, c * 128 : (c + 1) * 128].T

        def block(i, carry):
            left = rows_t[pl.ds(pl.multiple_of(i * 192, 192), 192), :]
            for n in range(3):
                cols = slice(n * 512, (n + 1) * 512)
                part = dot(left, others[:, cols]).astype(BF)
                term[0, i, :, cols] = part[:96]
                term[1, i, :, cols] = part[96:]
            if term.shape[3] > D:
                for a in range(2):
                    at_rows = pl.ds(pl.multiple_of(i * 192 + a * 96, 96), 96)
                    term[a, i, :, D:] = small_t[at_rows, :]
            send(i).start()
            return carry

        lax.fori_loop(0, 8, block, 0)

    for load in loads[:3]:
        load.wait()
    for h in range(3):
        for b in range(4):
            cols = slice((4 * h + b) * 128, (4 * h + b + 1) * 128)
            for a, ref in enumerate((q_ref, k_ref, v_ref)):
                block = ref[:, cols]
                if a == 0:
                    block = (block.astype(F32) * 0.125).astype(BF)
                block = block.T
                snd[h, 2 * b, a * HD : (a + 1) * HD, :] = block[:HD]
                snd[h, 2 * b + 1, a * HD : (a + 1) * HD, :] = block[HD:]
        if h == 0:
            pl.semaphore_wait(barrier, N + 3)
        ex_q[h][0]()

    for c in range(NB):
        ng[:, c * 128 : (c + 1) * 128] = ng_ref[c : c + 1, :]
        cg[:, c * 128 : (c + 1) * 128] = cg_ref[c : c + 1, :]

    loads[3].wait()
    own_valid = me * F + iota((F, 1), 0) < length
    gm[...] = jnp.where(own_valid, go_ref[...], jnp.zeros_like(go_ref))
    wp_copy.wait()

    def act_grad(c, carry):
        cols = pl.ds(pl.multiple_of(c * 256, 256), 256)
        gact[:, cols] = dot_nt(gm[...], wp[cols, :])
        return carry

    lax.fori_loop(0, D // 256, act_grad, 0)

    qaug[HD:, :] = (iota((HD, S), 0) == 0).astype(F32).astype(BF)
    vta[HD:, :] = (iota((16, S), 0) == 0).astype(F32).astype(BF)
    qz[HD:, :] = jnp.zeros((HD, S), BF)
    dz[:HD, :] = jnp.zeros((HD, S), BF)
    doaug[16:HD, :] = jnp.zeros((HD - 16, S), BF)

    for h in range(3):
        ex_q[h][1]()
        lane = iota((F, 128), 1)
        for j in range(N):
            cols = slice(j * F, (j + 1) * F)
            qaug[:HD, cols] = rcv[h, j, :HD, :]
            vta[:HD, cols] = rcv[h, j, 2 * HD :, :]
            both = rcv[h, j, HD:, :].T
            bias = jnp.where(j * F + iota((F, 128), 0) < length, 0.0, MASKED)
            bias = jnp.where(lane == HD, bias, 0.0).astype(BF)
            ones = jnp.where(lane < 2, 1.0, 0.0).astype(BF)
            kaug[cols, :] = jnp.where(lane < HD, both, bias)
            vaug[h, cols, :] = jnp.where(lane < HD, ones, both)

        def attend(i, carry, h=h):
            cols = pl.ds(pl.multiple_of(i * TILE, TILE), TILE)
            scores = dot(kaug[...], qaug[:, cols])
            top = jnp.max(scores, axis=0, keepdims=True)
            weights = jnp.exp(scores - top).astype(BF)
            pt[h, :, cols] = weights
            summed = dot(vta[...], weights)
            scale = 1.0 / summed[HD : HD + 1, :]
            inv[h, :, cols] = scale
            rows = (summed[:HD] * scale).astype(BF)
            for a in range(TILE // F):
                obuf[h, i * (TILE // F) + a] = rows[:, a * F : (a + 1) * F]
            for a in range(TILE // F):
                ex_o[h][3](i * (TILE // F) + a)
            return carry

        lax.fori_loop(0, S // TILE, attend, 0)
        ex_o[h][4]()

    wo_copy.wait()
    loads[4].wait()
    for h in range(3):
        ex_o[h][1]()
        for b in range(4):
            pair = jnp.concatenate([att_t[h, 2 * b], att_t[h, 2 * b + 1]], axis=0)
            att[:, (4 * h + b) * 128 : (4 * h + b + 1) * 128] = pair.T

        def project(c, carry, h=h):
            cols = pl.ds(pl.multiple_of(c * 256, 256), 256)
            before = res_ref[:, cols].astype(F32) if h == 0 else mixed[:, cols]
            mixed[:, cols] = before + dot(
                att[:, 512 * h : 512 * (h + 1)], wo[512 * h : 512 * (h + 1), cols]
            )
            return carry

        lax.fori_loop(0, D // 256, project, 0)

    def mean_of(x):
        return jnp.sum(x, axis=1, keepdims=True) * (1.0 / D)

    def first_norm(i, carry):
        rows = pl.ds(pl.multiple_of(i * 16, 16), 16)
        x = mixed[rows, :]
        x = x - mean_of(x)
        r = lax.rsqrt(mean_of(x * x) + EPSILON)
        n = x * r
        n1[rows, :] = n
        r1[rows, :] = r
        valid = me * F + i * 16 + iota((16, 1), 0) < length
        low = jnp.where(valid, n * ng[...], 0.0).astype(BF)
        cin[rows, :] = low
        wide = low.astype(F32)
        for c in range(NB):
            cp[c, pl.ds(pl.multiple_of(16 + i * 16, 16), 16), :] = wide[:, c * 128 : (c + 1) * 128]
        return carry

    lax.fori_loop(0, F // 16, first_norm, 0)

    def edges(buffer, k):
        to_right = pltpu.make_async_remote_copy(
            src_ref=buffer.at[pl.ds(F - 16, 16)],
            dst_ref=lh.at[k],
            send_sem=s_h.at[2 * k],
            recv_sem=r_h.at[2 * k],
            device_id=(dp, at(1)),
            device_id_type=MESH,
        )
        to_left = pltpu.make_async_remote_copy(
            src_ref=buffer.at[pl.ds(0, 16)],
            dst_ref=rh.at[k],
            send_sem=s_h.at[2 * k + 1],
            recv_sem=r_h.at[2 * k + 1],
            device_id=(dp, at(-1)),
            device_id_type=MESH,
        )
        return to_right, to_left

    def place_edges(k, padded):
        left = jnp.where(me > 0, lh[k].astype(F32), 0.0)
        right = jnp.where(me < N - 1, rh[k].astype(F32), 0.0)
        for c in range(NB):
            padded[c, 0:16, :] = left[:, c * 128 : (c + 1) * 128]
            padded[c, F + 16 : F + 32, :] = right[:, c * 128 : (c + 1) * 128]

    halo = edges(cin, 0)
    for copy in halo:
        copy.start()
    for copy in halo:
        copy.wait()
    place_edges(0, cp)

    def convolve(c, carry):
        cols = pl.ds(pl.multiple_of(c * 128, 128), 128)
        total = jnp.broadcast_to(cb_ref[pl.ds(c, 1), :], (F, 128))
        for t in range(KERN):
            total = total + cp[c, t + 1 : t + 1 + F, :] * taps_ref[t : t + 1, cols]
        csum[:, cols] = total
        return carry

    lax.fori_loop(0, NB, convolve, 0)

    vacc[...] = jnp.zeros_like(vacc)

    def fold(x):
        return x[:8] + x[8:]

    for i in range(F // 16):
        rows = slice(i * 16, (i + 1) * 16)
        x = csum[rows, :]
        x = x - mean_of(x)
        r = lax.rsqrt(mean_of(x * x) + EPSILON)
        n = x * r
        scaled = n * cg[...]
        g = jax.nn.sigmoid(scaled)
        act[rows, :] = (scaled * g).astype(BF)
        back = gact[rows, :] * g * (1.0 + scaled * (1.0 - g))
        vacc[2] += fold(back * n)
        u = back * cg[...]
        grad = r * (u - mean_of(u) - n * mean_of(u * n))
        vacc[0] += fold(grad)
        low = grad.astype(BF)
        gcl[rows, :] = low
        low_wide = low.astype(F32)
        for c in range(NB):
            cols = slice(c * 128, (c + 1) * 128)
            gc[c, rows, :] = grad[:, cols]
            gpad[c, 16 + i * 16 : 32 + i * 16, :] = low_wide[:, cols]

    halo2 = edges(gcl, 1)
    for copy in halo2:
        copy.start()

    def block_cols(c, carry):
        cols = pl.ds(pl.multiple_of(c * 256, 256), 256)
        bo_ref[:, cols] = (mixed[:, cols] + dot(act[...], wp[:, cols])).astype(BF)
        return carry

    lax.fori_loop(0, D // 256, block_cols, 0)
    stores = [pltpu.make_async_copy(bo_ref, bo_hbm, e_sem.at[0])]
    stores[0].start()

    weight_term(gm, act, pterm, point[0])

    for copy in halo2:
        copy.wait()
    place_edges(1, gpad)

    def convolve_back(c, carry):
        cols = pl.ds(pl.multiple_of(c * 128, 128), 128)
        total = jnp.zeros((F, 128), F32)
        for t in range(KERN):
            total = total + gpad[c, KERN - t : KERN - t + F, :] * taps_ref[t : t + 1, cols]
        csum[:, cols] = jnp.where(me * F + iota((F, 1), 0) < length, total, 0.0)
        return carry

    lax.fori_loop(0, NB, convolve_back, 0)
    point[1]()

    def first_norm_back(i, carry):
        rows = pl.ds(pl.multiple_of(i * 16, 16), 16)
        x = csum[rows, :]
        n = n1[rows, :]
        vacc[1] += fold(x * n)
        u = x * ng[...]
        grad = r1[rows, :] * (u - mean_of(u) - n * mean_of(u * n))
        gr_ref[rows, :] = (gm[rows, :].astype(F32) + grad).astype(BF)
        return carry

    lax.fori_loop(0, F // 16, first_norm_back, 0)
    stores.append(pltpu.make_async_copy(gr_ref, gr_hbm, e_sem.at[1]))
    stores[1].start()

    for h in range(3):

        def attended_rows(j, carry, h=h):
            for a in range(2):
                rows = pl.ds(pl.multiple_of(512 * h + (2 * j + a) * 128, 128), 128)
                part = dot_nt(wo[rows, :], gr_ref[...]).astype(BF)
                dsnd[h, 4 * j + 2 * a] = part[:HD]
                dsnd[h, 4 * j + 2 * a + 1] = part[HD:]
            return carry

        lax.fori_loop(0, 2, attended_rows, 0)
        ex_d[h][0]()

    small = csum

    def tap_rows(c, carry):
        cols = pl.ds(pl.multiple_of(c * 128, 128), 128)
        grad = gc[c]
        for t in range(KERN):
            small[t : t + 1, cols] = jnp.sum(cp[c, t + 1 : t + 1 + F, :] * grad, axis=0, keepdims=True)
        return carry

    lax.fori_loop(0, NB, tap_rows, 0)
    for i in range(3):
        small[KERN + i : KERN + i + 1, :] = jnp.sum(vacc[i], axis=0, keepdims=True)
    small[KERN + 3 :, :] = jnp.zeros((128 - KERN - 3, D), F32)
    for c in range(NB):
        small_t[c * 128 : (c + 1) * 128, :] = small[:, c * 128 : (c + 1) * 128].T.astype(BF)
    weight_term(gr_ref, att, oterm, out[0])
    point[2]()

    for h in range(3):
        ex_d[h][1]()
        row = iota((16, F), 0)
        for j in range(N):
            cols = slice(j * F, (j + 1) * F)
            grad = do[h, j].astype(F32)
            scale = inv[h, :, cols]
            delta = -scale * jnp.sum(grad * obuf[h, j].astype(F32), axis=0, keepdims=True)
            high = delta.astype(BF).astype(F32)
            doaug[:16, cols] = jnp.where(row == 0, high, jnp.where(row == 1, delta - high, 0.0)).astype(BF)
            scaled = (grad * scale).astype(BF)
            doaug[HD:, cols] = scaled
            dz[HD:, cols] = scaled
            qz[:HD, cols] = rcv[h, j, :HD, :]
            kt[:, cols] = rcv[h, j, HD : 2 * HD, :]

        def back_queries(i, carry, h=h):
            cols = pl.ds(pl.multiple_of(i * TILE, TILE), TILE)
            grads = dot(vaug[h], doaug[:, cols])
            grads = (pt[h, :, cols].astype(F32) * grads).astype(BF)
            dst[:, cols] = grads
            rows = (dot(kt[...], grads) * 0.125).astype(BF)
            for a in range(TILE // F):
                sq[h, i * (TILE // F) + a] = rows[:, a * F : (a + 1) * F]
            for a in range(TILE // F):
                ex_g[h][3](i * (TILE // F) + a)
            return carry

        lax.fori_loop(0, S // TILE, back_queries, 0)

        def back_keys(j, carry, h=h):
            rows = pl.ds(pl.multiple_of(j * F, F), F)
            both = dot_nt(dst[rows, :], qz[...]) + dot_nt(pt[h, rows, :], dz[...])
            skv[h, j] = both.T.astype(BF)
            ex_k[h][3](j)
            return carry

        lax.fori_loop(0, N, back_keys, 0)
        ex_g[h][4]()
        ex_k[h][4]()
        if h == 0:
            point[3]()
            out[1]()
        elif h == 1:
            point[4]()
            out[2]()
        else:
            out[3]()

    for h in range(3):
        ex_g[h][1]()
        ex_k[h][1]()
        for b in range(4):
            cols = slice((4 * h + b) * 128, (4 * h + b + 1) * 128)
            for ref, source, part in (
                (gq_ref, rq, slice(0, HD)), (gk_ref, rkv, slice(0, HD)), (gv_ref, rkv, slice(HD, 2 * HD))
            ):
                pair = jnp.concatenate([source[h, 2 * b, part], source[h, 2 * b + 1, part]], axis=0)
                ref[:, cols] = pair.T
        cols = pl.ds(512 * h, 512)
        for a, (ref, hbm) in enumerate(((gq_ref, gq_hbm), (gk_ref, gk_hbm), (gv_ref, gv_hbm))):
            stores.append(pltpu.make_async_copy(ref.at[:, cols], hbm.at[:, cols], e_sem.at[2 + 3 * h + a]))
            stores[-1].start()
        if h == 0:
            out[4]()

    gp_ref[...] = point[5]()
    gw_ref[...] = out[5]()
    point[6]()
    out[6]()
    for group in (ex_q, ex_o, ex_d, ex_g, ex_k):
        for h in range(3):
            group[h][2]()
    for store in stores:
        store.wait()


def fused(lengths, q, k, v, res, go, wo, wp, ng, taps, cb, cg):
    vmem = pl.BlockSpec(memory_space=pltpu.VMEM)
    hbm = pl.BlockSpec(memory_space=pl.ANY)
    smem = pl.BlockSpec(memory_space=pltpu.SMEM)
    rows = jax.ShapeDtypeStruct((F, D), BF)
    dma = pltpu.SemaphoreType.DMA
    scratch = [
        *[pltpu.VMEM((F, D), BF)] * 10,
        pltpu.VMEM((D, D), BF),
        pltpu.VMEM((D, D), BF),
        pltpu.VMEM((3, N, 3 * HD, F), BF),
        pltpu.VMEM((3, N, 3 * HD, F), BF),
        pltpu.VMEM((S, 128), BF),
        pltpu.VMEM((128, S), BF),
        pltpu.VMEM((HD + 16, S), BF),
        pltpu.VMEM((3, S, 128), BF),
        pltpu.VMEM((3, S, S), BF),
        pltpu.VMEM((3, 1, S), F32),
        pltpu.VMEM((3, N, HD, F), BF),
        pltpu.VMEM((3, N, HD, F), BF),
        pltpu.VMEM((F, D), BF),
        pltpu.VMEM((F, D), F32),
        pltpu.VMEM((F, D), F32),
        pltpu.VMEM((F, 1), F32),
        pltpu.VMEM((F, D), BF),
        pltpu.VMEM((NB, F + 32, 128), F32),
        pltpu.VMEM((F, D), F32),
        pltpu.VMEM((F, D), F32),
        pltpu.VMEM((F, D), BF),
        pltpu.VMEM((F, D), BF),
        pltpu.VMEM((NB, F, 128), F32),
        pltpu.VMEM((F, D), BF),
        pltpu.VMEM((NB, F + 32, 128), F32),
        pltpu.VMEM((3, 8, D), F32),
        pltpu.VMEM((2, 16, D), BF),
        pltpu.VMEM((2, 16, D), BF),
        pltpu.VMEM((3, N, HD, F), BF),
        pltpu.VMEM((3, N, HD, F), BF),
        pltpu.VMEM((128, S), BF),
        pltpu.VMEM((128, S), BF),
        pltpu.VMEM((128, S), BF),
        pltpu.VMEM((HD, S), BF),
        pltpu.VMEM((S, S), BF),
        pltpu.VMEM((3, N, HD, F), BF),
        pltpu.VMEM((3, N, HD, F), BF),
        pltpu.VMEM((3, N, 2 * HD, F), BF),
        pltpu.VMEM((3, N, 2 * HD, F), BF),
        pltpu.VMEM((1, D), F32),
        pltpu.VMEM((1, D), F32),
        pltpu.VMEM((D, 128), BF),
        pltpu.VMEM((D, F), BF),
        *[
            pltpu.VMEM(shape + (width,), BF)
            for width in (D, D + 128)
            for shape in ((2, 8, 96), (8, 96), (2, 96), (2, 2, 96), (96,), (N, 16), (N, 16))
        ],
        pltpu.VMEM((104, D + 128), F32),
        dma((2,)),
        dma((5,)),
        dma((11,)),
        dma((3, N)), dma((3, N)),
        dma((3, N)), dma((3, N)),
        dma((3, N)), dma((3, N)),
        dma((3, N)), dma((3, N)),
        dma((3, N)), dma((3, N)),
        dma((4,)), dma((4,)),
        dma((23,)), dma((23,)),
        dma((23,)), dma((23,)),
    ]
    return pl.pallas_call(
        kernel,
        out_shape=[rows] * 5
        + [jax.ShapeDtypeStruct((16, D + 128), F32), jax.ShapeDtypeStruct((16, D), F32)],
        in_specs=[smem] + [hbm] * 7 + [vmem] * 4,
        out_specs=[hbm] * 5 + [vmem] * 2,
        scratch_shapes=scratch,
        compiler_params=pltpu.CompilerParams(
            collective_id=0, has_side_effects=True, vmem_limit_bytes=62 * 1024 * 1024
        ),
    )(lengths, q, k, v, res, go, wo, wp, ng, taps, cb, cg)


def finish(gw_ref, gp_ref, *refs):
    rows, (gow_ref, gpw_ref, gker_ref, gvec_ref), sems = (refs[:5], refs[5:10]), refs[10:14], refs[14]
    copies = [pltpu.make_async_copy(a, b, sems.at[i]) for i, (a, b) in enumerate(zip(*rows))]
    for copy in copies:
        copy.start()
    gow_ref[...] = gw_ref[:12, :D]
    gpw_ref[...] = gp_ref[:12, :]
    gker_ref[...] = gw_ref[:12, D : D + KERN]
    gvec_ref[...] = gw_ref[:, D:].T[KERN : KERN + 3, :12]
    for copy in copies:
        copy.wait()


def finished(rows, gw, gp):
    vmem = pl.BlockSpec(memory_space=pltpu.VMEM)
    hbm = pl.BlockSpec(memory_space=pl.ANY)
    return pl.pallas_call(
        finish,
        out_shape=[jax.ShapeDtypeStruct((F, D), BF)] * 5
        + [jax.ShapeDtypeStruct(shape, F32) for shape in ((12, D), (12, D), (12, KERN), (3, 12))],
        in_specs=[vmem] * 2 + [hbm] * 5,
        out_specs=[hbm] * 5 + [vmem] * 4,
        scratch_shapes=[pltpu.SemaphoreType.DMA((5,))],
        compiler_params=pltpu.CompilerParams(vmem_limit_bytes=62 * 1024 * 1024),
    )(gw, gp, *rows)


def local(
    residual_in, query_rows, key_rows, value_rows, lengths, out_weight, norm_gain, conv_kernel,
    conv_bias, conv_gain, point_weight, grad_out,
):
    outs = fused(
        lengths, query_rows[0], key_rows[0], value_rows[0], residual_in[0], grad_out[0],
        out_weight, point_weight, norm_gain.reshape(NB, 128), conv_kernel,
        conv_bias.reshape(NB, 128), conv_gain.reshape(NB, 128),
    )
    outs = finished(outs[:5], *outs[5:])
    return (*[x[None] for x in outs[:5]], *[x.T for x in outs[5:8]], outs[8])


def solution(mesh):
    rows = P("dp", "ctx", None)
    split = P(None, ("dp", "ctx"))
    in_specs = (rows,) * 4 + (P("dp"),) + (P(),) * 6 + (rows,)
    out_specs = (rows,) * 5 + (split,) * 4
    return jax.shard_map(local, mesh=mesh, in_specs=in_specs, out_specs=out_specs, check_vma=False)
```

```python
import jax
import jax.numpy as jnp
from jax import lax
from jax.experimental import pallas as pl
from jax.experimental.pallas import tpu as pltpu
from jax.sharding import PartitionSpec as P

N = 8
F = 128
D = 1536
S = 1024
HD = 64
KERN = 31
NB = D // 128
TILE = 256
EPSILON = 1e-05
MASKED = -1e30
MESH = pl.DeviceIdType.MESH
BF = jnp.bfloat16
F32 = jnp.float32


def dot(a, b):
    return jnp.dot(a, b, preferred_element_type=F32)


def dot_nt(a, b):
    return lax.dot_general(a, b, (((1,), (1,)), ((), ())), preferred_element_type=F32)


def iota(shape, dim):
    return lax.broadcasted_iota(jnp.int32, shape, dim)


def kernel(
    len_ref, q_hbm, k_hbm, v_hbm, res_hbm, go_hbm, wo_hbm, wp_hbm, ng_ref, taps_ref, cb_ref, cg_ref,
    bo_hbm, gr_hbm, gq_hbm, gk_hbm, gv_hbm, gw_ref, gp_ref,
    q_ref, k_ref, v_ref, res_ref, go_ref, bo_ref, gr_ref, gq_ref, gk_ref, gv_ref, wo, wp, snd, rcv, kaug, qaug, vta, vaug, pt, inv, obuf, att_t, att, mixed, n1, r1, cin, cp, csum,
    gact, gm, act, gc, gcl, gpad, vacc, lh, rh, dsnd, do, doaug, qz, dz, kt, rq, rkv,
    ng, cg, small_t, rows_t, rows_p, *rest,
):
    me = lax.axis_index("ctx")
    dp = lax.axis_index("dp")
    length = len_ref[0]
    sums, rest = [rest[7 * i : 7 * i + 7] for i in range(4)], rest[28:]
    (
        wide, w_sem, i_sem, e_sem, s_q, r_q, s_o, r_o, s_d, r_d, s_g, r_g, s_k, r_k, s_h, r_h, s_r, r_r,
    ) = rest
    dst = wp.at[pl.ds(0, S), pl.ds(0, S)]
    sq, skv = snd.at[:, :, pl.ds(0, HD)], snd.at[:, :, pl.ds(HD, 2 * HD)]
    core = lax.rem(dp, 2)
    y = lax.rem(lax.div(dp, 2), 2)
    z = lax.div(dp, 4)
    def at(offset):
        return lax.rem(me + (offset + N), N)

    x = lax.rem(me, 4)
    y_low = lax.div(me, 4)
    sibling = (dp + 1 - 2 * core, me)

    def in_z(offset):
        return lax.rem(z + (offset + 4), 4)

    def in_x(offset):
        return lax.rem(x + (offset + 4), 4)

    def z_device(offset):
        return (4 * in_z(offset) + 2 * y + core, me)

    def x_device(offset):
        return (dp, 4 * y_low + in_x(offset))

    def y_device(other, offset):
        return (dp + 2 - 4 * y if other else dp, at(offset))

    peers = [sibling] + [z_device(i) for i in (1, 2, 3)]
    peers += [y_device(b, o) for b in range(2) for o in range(N) if b or o]

    barrier = pltpu.get_barrier_semaphore()
    for peer in peers:
        pl.semaphore_signal(barrier, inc=1, device_id=peer, device_id_type=MESH)

    loads = [
        pltpu.make_async_copy(source, target, i_sem.at[i])
        for i, (source, target) in enumerate(
            ((q_hbm, q_ref), (k_hbm, k_ref), (v_hbm, v_ref), (go_hbm, go_ref), (res_hbm, res_ref))
        )
    ]
    for load in loads:
        load.start()
    wp_copy = pltpu.make_async_copy(wp_hbm, wp, w_sem.at[0])
    wo_copy = pltpu.make_async_copy(wo_hbm, wo, w_sem.at[1])
    wp_copy.start()
    wo_copy.start()

    def exchange(source, target, send_sem, recv_sem, h):
        def copy(o):
            return pltpu.make_async_remote_copy(
                src_ref=source.at[h, at(o)],
                dst_ref=target.at[h, me],
                send_sem=send_sem.at[h, o],
                recv_sem=recv_sem.at[h, o],
                device_id=(dp, at(o)),
                device_id_type=MESH,
            )

        def arrival(o):
            block = target.at[h, at(-o)]
            return pltpu.make_async_remote_copy(
                src_ref=block,
                dst_ref=block,
                send_sem=send_sem.at[h, o],
                recv_sem=recv_sem.at[h, o],
                device_id=(dp, at(-o)),
                device_id_type=MESH,
            )

        def start():
            for o in (4, 3, 5, 2, 6, 1, 7):
                copy(o).start()
            target[h, me] = source[h, me]

        def start_one(j):
            @pl.when(j != me)
            def _():
                o = lax.rem(j - me + N, N)
                pltpu.make_async_remote_copy(
                    src_ref=source.at[h, j],
                    dst_ref=target.at[h, me],
                    send_sem=send_sem.at[h, o],
                    recv_sem=recv_sem.at[h, o],
                    device_id=(dp, j),
                    device_id_type=MESH,
                ).start()

        def keep():
            target[h, me] = source[h, me]

        def wait():
            for o in range(1, N):
                arrival(o).wait_recv()

        def drain():
            for o in range(1, N):
                copy(o).wait_send()

        return start, wait, drain, start_one, keep

    ex_q = [exchange(snd, rcv, s_q, r_q, h) for h in range(3)]
    ex_o = [exchange(obuf, att_t, s_o, r_o, h) for h in range(3)]
    ex_d = [exchange(dsnd, do, s_d, r_d, h) for h in range(3)]
    ex_g = [exchange(sq, rq, s_g, r_g, h) for h in range(3)]
    ex_k = [exchange(skv, rkv, s_k, r_k, h) for h in range(3)]

    def ring(k, along, device):
        term, first, far, near = sums[k][:4]
        here = along(0)

        def to(source, target, i, peer):
            return pltpu.make_async_remote_copy(
                src_ref=source,
                dst_ref=target,
                send_sem=s_r.at[k, i],
                recv_sem=r_r.at[k, i],
                device_id=peer,
                device_id_type=MESH,
            )

        up, down = 2 * along(1), 2 * along(-1)
        opposite = 2 * along(2)
        far_copies = (
            to(term.at[core, opposite], far.at[0], 8, device(1)),
            to(term.at[core, opposite + 1], far.at[1], 9, device(-1)),
        )
        plain_copies = (
            to(term.at[core, up + 1], near.at[0, 1], 10, device(1)),
            to(term.at[core, down], near.at[1, 0], 11, device(-1)),
        )
        joint_copies = (
            to(term.at[core, up], near.at[0, 0], 12, device(1)),
            to(term.at[core, down + 1], near.at[1, 1], 13, device(-1)),
        )

        def cores(i):
            return to(term.at[1 - core, i], first.at[i], i, sibling)

        def start():
            order = (opposite, opposite + 1, up + 1, down, up, down + 1, 2 * here, 2 * here + 1)
            for i, copy in zip(order, far_copies + plain_copies + (None,) * 4):
                cores(i).wait_recv()
                term[core, i] = term[core, i] + first[i]
                if copy is not None:
                    copy.start()

        def join():
            for a, (copy, i) in enumerate(zip(far_copies, (up, down + 1))):
                copy.wait_recv()
                term[core, i] = term[core, i] + far[a]
                joint_copies[a].start()

        def total():
            for copy in plain_copies + joint_copies:
                copy.wait_recv()
            parts = []
            for a in range(2):
                part = term[core, 2 * here + a].astype(F32) + near[0, a].astype(F32)
                parts.append(part + near[1, a].astype(F32))
            return parts

        def drain():
            for i in range(8):
                cores(i).wait_send()
            for copy in far_copies + plain_copies + joint_copies:
                copy.wait_send()

        return to, cores, start, join, total, drain

    def slices(part, split, count):
        rows, width = part.shape
        wide[rows : rows + 8, :width] = jnp.zeros((8, width), F32)
        wide[:rows, :width] = part
        for j in range(count):
            split[j] = wide[12 * j : 12 * j + 16, :width].astype(BF)

    def z_reducer(k):
        to, cores, start, join, total, drain_ring = ring(k, in_z, z_device)
        split, last = sums[k][5], sums[k][6]
        others = [(b, o) for b in range(2) for o in range(N) if b or o]

        def sent(b, o):
            side = 1 - y if b else y
            return to(split.at[side, at(o)], last.at[y, me], 14 + N * b + o, y_device(b, o))

        def arrival(b, o):
            block = last.at[1 - y if b else y, at(-o)]
            return to(block, block, 14 + N * b + o, y_device(b, -o))

        def spread():
            for a, part in enumerate(total()):
                slices(part, split.at[a], N)
            for b, o in others:
                sent(b, o).start()
            last[y, me] = split[y, me]

        def finish():
            for b, o in others:
                arrival(b, o).wait_recv()
            result = jnp.zeros(last.shape[2:], F32)
            for b in range(2):
                for j in range(N):
                    result = result + last[b, j].astype(F32)
            return result

        def drain():
            drain_ring()
            for b, o in others:
                sent(b, o).wait_send()

        return cores, start, join, spread, finish, drain

    def x_reducer(k):
        to, cores, start, join, total, drain_ring = ring(k, in_x, x_device)
        term = sums[k][0]
        in_column, split, last = sums[k][4:]

        def column(o):
            c = in_z(o)
            rows = pl.ds(pl.multiple_of(48 * lax.rem(c, 2), 16), 48)
            return to(term.at[core, 2 * x + lax.div(c, 2), rows], in_column.at[z], 13 + o, z_device(o))

        def column_arrival(o):
            block = in_column.at[in_z(-o)]
            return to(block, block, 13 + o, z_device(-o))

        def quad(b):
            low, high = (1 - y_low if b // 2 else y_low), (1 - y if b % 2 else y)
            return 2 * low + high, y_device(b % 2, 4 * (b // 2))

        def sent(b):
            j, peer = quad(b)
            return to(split.at[j], last.at[2 * y_low + y], 16 + b, peer)

        def arrival(b):
            j, peer = quad(b)
            return to(last.at[j], last.at[j], 16 + b, peer)

        def spread_z():
            for a, part in enumerate(total()):
                term[core, 2 * x + a] = part.astype(BF)
            for o in (1, 2, 3):
                column(o).start()

        def spread():
            own = pl.ds(pl.multiple_of(48 * lax.rem(z, 2), 16), 48)
            part = term[core, 2 * x + lax.div(z, 2), own, :].astype(F32)
            for o in (1, 2, 3):
                column_arrival(o).wait_recv()
                part = part + in_column[in_z(-o)].astype(F32)
            slices(part, split, 4)
            for b in (1, 2, 3):
                sent(b).start()
            last[2 * y_low + y] = split[2 * y_low + y]

        def finish():
            for b in (1, 2, 3):
                arrival(b).wait_recv()
            result = last[0].astype(F32)
            for j in (1, 2, 3):
                result = result + last[j].astype(F32)
            return result

        def drain():
            drain_ring()
            for i in (1, 2, 3):
                column(i).wait_send()
                sent(i).wait_send()

        return cores, start, join, spread, finish, drain, spread_z

    point_z, point_x = z_reducer(0), x_reducer(1)
    out_one, out_two = z_reducer(2), z_reducer(3)

    def weight_term(rows, others, begin, width, k, by_z, send):
        term = sums[k][0]

        def block(i, carry):
            for a in range(2):
                if by_z and a:
                    break
                base = 192 * i if by_z else 192 * i + 768 * a
                left = rows[pl.ds(pl.multiple_of(base, 64), 192), :]
                for n in range(width // 256):
                    cols = slice(n * 256, (n + 1) * 256)
                    part = dot(left, others[:, begin + n * 256 : begin + (n + 1) * 256]).astype(BF)
                    if by_z:
                        term[0, i, :, cols] = part[:96]
                        term[1, i, :, cols] = part[96:]
                    else:
                        term[a, 2 * i, :, cols] = part[:96]
                        term[a, 2 * i + 1, :, cols] = part[96:]
            if term.shape[3] > width:
                for a in range(2):
                    at_rows = pl.ds(pl.multiple_of(i * 192 + a * 96, 32), 96)
                    term[a, i, :, width:] = small_t[at_rows, :]
            if by_z:
                send(i).start()
            else:
                send(2 * i).start()
                send(2 * i + 1).start()
            return carry

        lax.fori_loop(0, 8 if by_z else 4, block, 0)

    def turn(rows):
        for c in range(NB):
            rows_t[c * 128 : (c + 1) * 128, :] = rows[:, c * 128 : (c + 1) * 128].T

    for load in loads[:3]:
        load.wait()
    for h in range(3):
        for b in range(4):
            cols = slice((4 * h + b) * 128, (4 * h + b + 1) * 128)
            for a, ref in enumerate((q_ref, k_ref, v_ref)):
                block = ref[:, cols]
                if a == 0:
                    block = (block.astype(F32) * 0.125).astype(BF)
                block = block.T
                snd[h, 2 * b, a * HD : (a + 1) * HD, :] = block[:HD]
                snd[h, 2 * b + 1, a * HD : (a + 1) * HD, :] = block[HD:]
        if h == 0:
            pl.semaphore_wait(barrier, len(peers))
        ex_q[h][0]()

    for c in range(NB):
        ng[:, c * 128 : (c + 1) * 128] = ng_ref[c : c + 1, :]
        cg[:, c * 128 : (c + 1) * 128] = cg_ref[c : c + 1, :]

    loads[3].wait()
    own_valid = me * F + iota((F, 1), 0) < length
    gm[...] = jnp.where(own_valid, go_ref[...], jnp.zeros_like(go_ref))
    wp_copy.wait()

    def act_grad(c, carry):
        cols = pl.ds(pl.multiple_of(c * 256, 256), 256)
        gact[:, cols] = dot_nt(gm[...], wp[cols, :])
        return carry

    lax.fori_loop(0, D // 256, act_grad, 0)

    turn(gm)

    def ordered(b, carry):
        r = iota((192, 1), 0)
        d = 384 * lax.div(r, 48) + 48 * lax.rem(lax.div(r, 24), 2) + 192 * lax.rem(lax.div(r, 12), 2)
        d = d + lax.rem(r, 12) + 96 * lax.div(b, 4) + 12 * lax.rem(b, 4)
        pick = jnp.where(iota((192, D), 1) == d, 1.0, 0.0).astype(BF)
        rows_p[pl.ds(pl.multiple_of(192 * b, 64), 192), :] = dot_nt(pick, gm[...]).astype(BF)
        return carry

    lax.fori_loop(0, 8, ordered, 0)

    qaug[HD:, :] = (iota((HD, S), 0) == 0).astype(F32).astype(BF)
    vta[HD:, :] = (iota((16, S), 0) == 0).astype(F32).astype(BF)
    qz[HD:, :] = jnp.zeros((HD, S), BF)
    dz[:HD, :] = jnp.zeros((HD, S), BF)
    doaug[16:HD, :] = jnp.zeros((HD - 16, S), BF)

    for h in range(3):
        ex_q[h][1]()
        lane = iota((F, 128), 1)
        for j in range(N):
            cols = slice(j * F, (j + 1) * F)
            qaug[:HD, cols] = rcv[h, j, :HD, :]
            vta[:HD, cols] = rcv[h, j, 2 * HD :, :]
            both = rcv[h, j, HD:, :].T
            bias = jnp.where(j * F + iota((F, 128), 0) < length, 0.0, MASKED)
            bias = jnp.where(lane == HD, bias, 0.0).astype(BF)
            ones = jnp.where(lane < 2, 1.0, 0.0).astype(BF)
            kaug[cols, :] = jnp.where(lane < HD, both, bias)
            vaug[h, cols, :] = jnp.where(lane < HD, ones, both)

        def attend(i, carry, h=h):
            cols = pl.ds(pl.multiple_of(i * TILE, TILE), TILE)
            scores = dot(kaug[...], qaug[:, cols])
            top = jnp.max(scores, axis=0, keepdims=True)
            weights = jnp.exp(scores - top).astype(BF)
            pt[h, :, cols] = weights
            summed = dot(vta[...], weights)
            scale = 1.0 / summed[HD : HD + 1, :]
            inv[h, :, cols] = scale
            rows = (summed[:HD] * scale).astype(BF)
            for a in range(TILE // F):
                obuf[h, i * (TILE // F) + a] = rows[:, a * F : (a + 1) * F]
            for a in range(TILE // F):
                ex_o[h][3](i * (TILE // F) + a)
            return carry

        lax.fori_loop(0, S // TILE, attend, 0)
        ex_o[h][4]()

    wo_copy.wait()
    loads[4].wait()
    for h in range(3):
        ex_o[h][1]()
        for b in range(4):
            pair = jnp.concatenate([att_t[h, 2 * b], att_t[h, 2 * b + 1]], axis=0)
            att[:, (4 * h + b) * 128 : (4 * h + b + 1) * 128] = pair.T

        def project(c, carry, h=h):
            cols = pl.ds(pl.multiple_of(c * 256, 256), 256)
            before = res_ref[:, cols].astype(F32) if h == 0 else mixed[:, cols]
            mixed[:, cols] = before + dot(
                att[:, 512 * h : 512 * (h + 1)], wo[512 * h : 512 * (h + 1), cols]
            )
            return carry

        lax.fori_loop(0, D // 256, project, 0)

    def mean_of(x):
        return jnp.sum(x, axis=1, keepdims=True) * (1.0 / D)

    def first_norm(i, carry):
        rows = pl.ds(pl.multiple_of(i * 16, 16), 16)
        x = mixed[rows, :]
        x = x - mean_of(x)
        r = lax.rsqrt(mean_of(x * x) + EPSILON)
        n = x * r
        n1[rows, :] = n
        r1[rows, :] = r
        valid = me * F + i * 16 + iota((16, 1), 0) < length
        low = jnp.where(valid, n * ng[...], 0.0).astype(BF)
        cin[rows, :] = low
        wide = low.astype(F32)
        for c in range(NB):
            cp[c, pl.ds(pl.multiple_of(16 + i * 16, 16), 16), :] = wide[:, c * 128 : (c + 1) * 128]
        return carry

    lax.fori_loop(0, F // 16, first_norm, 0)

    def edges(buffer, k):
        to_right = pltpu.make_async_remote_copy(
            src_ref=buffer.at[pl.ds(F - 16, 16)],
            dst_ref=lh.at[k],
            send_sem=s_h.at[2 * k],
            recv_sem=r_h.at[2 * k],
            device_id=(dp, at(1)),
            device_id_type=MESH,
        )
        to_left = pltpu.make_async_remote_copy(
            src_ref=buffer.at[pl.ds(0, 16)],
            dst_ref=rh.at[k],
            send_sem=s_h.at[2 * k + 1],
            recv_sem=r_h.at[2 * k + 1],
            device_id=(dp, at(-1)),
            device_id_type=MESH,
        )
        return to_right, to_left

    def place_edges(k, padded):
        left = jnp.where(me > 0, lh[k].astype(F32), 0.0)
        right = jnp.where(me < N - 1, rh[k].astype(F32), 0.0)
        for c in range(NB):
            padded[c, 0:16, :] = left[:, c * 128 : (c + 1) * 128]
            padded[c, F + 16 : F + 32, :] = right[:, c * 128 : (c + 1) * 128]

    halo = edges(cin, 0)
    for copy in halo:
        copy.start()
    for copy in halo:
        copy.wait()
    place_edges(0, cp)

    def convolve(c, carry):
        cols = pl.ds(pl.multiple_of(c * 128, 128), 128)
        total = jnp.broadcast_to(cb_ref[pl.ds(c, 1), :], (F, 128))
        for t in range(KERN):
            total = total + cp[c, t + 1 : t + 1 + F, :] * taps_ref[t : t + 1, cols]
        csum[:, cols] = total
        return carry

    lax.fori_loop(0, NB, convolve, 0)

    vacc[...] = jnp.zeros_like(vacc)

    def fold(x):
        return x[:8] + x[8:]

    def second_norm(i):
        rows = slice(i * 16, (i + 1) * 16)
        x = csum[rows, :]
        x = x - mean_of(x)
        r = lax.rsqrt(mean_of(x * x) + EPSILON)
        n = x * r
        scaled = n * cg[...]
        g = jax.nn.sigmoid(scaled)
        act[rows, :] = (scaled * g).astype(BF)
        back = gact[rows, :] * g * (1.0 + scaled * (1.0 - g))
        vacc[2] += fold(back * n)
        u = back * cg[...]
        grad = r * (u - mean_of(u) - n * mean_of(u * n))
        vacc[0] += fold(grad)
        low = grad.astype(BF)
        gcl[rows, :] = low
        low_wide = low.astype(F32)
        for c in range(NB):
            cols = slice(c * 128, (c + 1) * 128)
            gc[c, rows, :] = grad[:, cols]
            gpad[c, 16 + i * 16 : 32 + i * 16, :] = low_wide[:, cols]

    for i in range(F // 16):
        second_norm(i)
    halo2 = edges(gcl, 1)
    for copy in halo2:
        copy.start()

    weight_term(rows_t, act, 0, 768, 0, True, point_z[0])
    weight_term(rows_p, act, 768, 768, 1, False, point_x[0])

    def block_cols(c, carry):
        cols = pl.ds(pl.multiple_of(c * 256, 256), 256)
        bo_ref[:, cols] = (mixed[:, cols] + dot(act[...], wp[:, cols])).astype(BF)
        return carry

    lax.fori_loop(0, D // 256, block_cols, 0)
    stores = [pltpu.make_async_copy(bo_ref, bo_hbm, e_sem.at[0])]
    stores[0].start()

    point_z[1]()
    point_x[1]()

    for copy in halo2:
        copy.wait()
    place_edges(1, gpad)

    def convolve_back(c, carry):
        cols = pl.ds(pl.multiple_of(c * 128, 128), 128)
        total = jnp.zeros((F, 128), F32)
        for t in range(KERN):
            total = total + gpad[c, KERN - t : KERN - t + F, :] * taps_ref[t : t + 1, cols]
        csum[:, cols] = jnp.where(me * F + iota((F, 1), 0) < length, total, 0.0)
        return carry

    lax.fori_loop(0, NB, convolve_back, 0)

    def first_norm_back(i, carry):
        rows = pl.ds(pl.multiple_of(i * 16, 16), 16)
        x = csum[rows, :]
        n = n1[rows, :]
        vacc[1] += fold(x * n)
        u = x * ng[...]
        grad = r1[rows, :] * (u - mean_of(u) - n * mean_of(u * n))
        gr_ref[rows, :] = (gm[rows, :].astype(F32) + grad).astype(BF)
        return carry

    lax.fori_loop(0, F // 16, first_norm_back, 0)
    stores.append(pltpu.make_async_copy(gr_ref, gr_hbm, e_sem.at[1]))
    stores[1].start()

    for h in range(3):

        def attended_rows(j, carry, h=h):
            for a in range(2):
                rows = pl.ds(pl.multiple_of(512 * h + (2 * j + a) * 128, 128), 128)
                part = dot_nt(wo[rows, :], gr_ref[...]).astype(BF)
                dsnd[h, 4 * j + 2 * a] = part[:HD]
                dsnd[h, 4 * j + 2 * a + 1] = part[HD:]
            return carry

        lax.fori_loop(0, 2, attended_rows, 0)
        ex_d[h][0]()

    point_z[2]()
    point_x[2]()
    turn(gr_ref)
    weight_term(rows_t, att, 0, 768, 2, True, out_one[0])
    small = csum

    def tap_rows(c, carry):
        cols = pl.ds(pl.multiple_of(c * 128, 128), 128)
        grad = gc[c]
        for t in range(KERN):
            small[t : t + 1, cols] = jnp.sum(cp[c, t + 1 : t + 1 + F, :] * grad, axis=0, keepdims=True)
        return carry

    lax.fori_loop(0, NB, tap_rows, 0)
    for i in range(3):
        small[KERN + i : KERN + i + 1, :] = jnp.sum(vacc[i], axis=0, keepdims=True)
    small[KERN + 3 :, :] = jnp.zeros((128 - KERN - 3, D), F32)
    for c in range(NB):
        small_t[c * 128 : (c + 1) * 128, :] = small[:, c * 128 : (c + 1) * 128].T.astype(BF)
    weight_term(rows_t, att, 768, 768, 3, True, out_two[0])
    out_one[1]()
    for h in range(3):
        ex_q[h][2]()

    for h in range(3):
        ex_d[h][1]()
        row = iota((16, F), 0)
        for j in range(N):
            cols = slice(j * F, (j + 1) * F)
            grad = do[h, j].astype(F32)
            scale = inv[h, :, cols]
            delta = -scale * jnp.sum(grad * obuf[h, j].astype(F32), axis=0, keepdims=True)
            high = delta.astype(BF).astype(F32)
            doaug[:16, cols] = jnp.where(row == 0, high, jnp.where(row == 1, delta - high, 0.0)).astype(BF)
            scaled = (grad * scale).astype(BF)
            doaug[HD:, cols] = scaled
            dz[HD:, cols] = scaled
            qz[:HD, cols] = rcv[h, j, :HD, :]
            kt[:, cols] = rcv[h, j, HD : 2 * HD, :]

        def back_queries(i, carry, h=h):
            cols = pl.ds(pl.multiple_of(i * TILE, TILE), TILE)
            grads = dot(vaug[h], doaug[:, cols])
            grads = (pt[h, :, cols].astype(F32) * grads).astype(BF)
            dst[:, cols] = grads
            rows = (dot(kt[...], grads) * 0.125).astype(BF)
            for a in range(TILE // F):
                sq[h, i * (TILE // F) + a] = rows[:, a * F : (a + 1) * F]
            for a in range(TILE // F):
                ex_g[h][3](i * (TILE // F) + a)
            return carry

        lax.fori_loop(0, S // TILE, back_queries, 0)

        def back_keys(j, carry, h=h):
            rows = pl.ds(pl.multiple_of(j * F, F), F)
            both = dot_nt(dst[rows, :], qz[...]) + dot_nt(pt[h, rows, :], dz[...])
            skv[h, j] = both.T.astype(BF)
            ex_k[h][3](j)
            return carry

        lax.fori_loop(0, N, back_keys, 0)
        ex_g[h][4]()
        ex_k[h][4]()
        if h == 0:
            out_one[2]()
            out_two[1]()
            point_x[6]()
            point_z[3]()
        elif h == 1:
            point_x[3]()
        else:
            out_one[3]()
            out_two[2]()

    for h in range(3):
        ex_g[h][1]()
        ex_k[h][1]()
        for b in range(4):
            cols = slice((4 * h + b) * 128, (4 * h + b + 1) * 128)
            for ref, source, part in (
                (gq_ref, rq, slice(0, HD)), (gk_ref, rkv, slice(0, HD)), (gv_ref, rkv, slice(HD, 2 * HD))
            ):
                pair = jnp.concatenate([source[h, 2 * b, part], source[h, 2 * b + 1, part]], axis=0)
                ref[:, cols] = pair.T
        cols = pl.ds(512 * h, 512)
        for a, (ref, hbm) in enumerate(((gq_ref, gq_hbm), (gk_ref, gk_hbm), (gv_ref, gv_hbm))):
            stores.append(pltpu.make_async_copy(ref.at[:, cols], hbm.at[:, cols], e_sem.at[2 + 3 * h + a]))
            stores[-1].start()
        if h == 1:
            out_two[3]()

    gp_ref[:, :768] = point_z[4]()
    gp_ref[:, 768:] = point_x[4]()
    gw_ref[:, :768] = out_one[4]()
    gw_ref[:, 768:] = out_two[4]()
    for reducer in (point_z, point_x, out_one, out_two):
        reducer[5]()
    for group in (ex_o, ex_d, ex_g, ex_k):
        for h in range(3):
            group[h][2]()
    for store in stores:
        store.wait()


def fused(lengths, q, k, v, res, go, wo, wp, ng, taps, cb, cg):
    vmem = pl.BlockSpec(memory_space=pltpu.VMEM)
    hbm = pl.BlockSpec(memory_space=pl.ANY)
    smem = pl.BlockSpec(memory_space=pltpu.SMEM)
    rows = jax.ShapeDtypeStruct((F, D), BF)
    dma = pltpu.SemaphoreType.DMA
    scratch = [
        *[pltpu.VMEM((F, D), BF)] * 10,
        pltpu.VMEM((D, D), BF),
        pltpu.VMEM((D, D), BF),
        pltpu.VMEM((3, N, 3 * HD, F), BF),
        pltpu.VMEM((3, N, 3 * HD, F), BF),
        pltpu.VMEM((S, 128), BF),
        pltpu.VMEM((128, S), BF),
        pltpu.VMEM((HD + 16, S), BF),
        pltpu.VMEM((3, S, 128), BF),
        pltpu.VMEM((3, S, S), BF),
        pltpu.VMEM((3, 1, S), F32),
        pltpu.VMEM((3, N, HD, F), BF),
        pltpu.VMEM((3, N, HD, F), BF),
        pltpu.VMEM((F, D), BF),
        pltpu.VMEM((F, D), F32),
        pltpu.VMEM((F, D), F32),
        pltpu.VMEM((F, 1), F32),
        pltpu.VMEM((F, D), BF),
        pltpu.VMEM((NB, F + 32, 128), F32),
        pltpu.VMEM((F, D), F32),
        pltpu.VMEM((F, D), F32),
        pltpu.VMEM((F, D), BF),
        pltpu.VMEM((F, D), BF),
        pltpu.VMEM((NB, F, 128), F32),
        pltpu.VMEM((F, D), BF),
        pltpu.VMEM((NB, F + 32, 128), F32),
        pltpu.VMEM((3, 8, D), F32),
        pltpu.VMEM((2, 16, D), BF),
        pltpu.VMEM((2, 16, D), BF),
        pltpu.VMEM((3, N, HD, F), BF),
        pltpu.VMEM((3, N, HD, F), BF),
        pltpu.VMEM((128, S), BF),
        pltpu.VMEM((128, S), BF),
        pltpu.VMEM((128, S), BF),
        pltpu.VMEM((HD, S), BF),
        pltpu.VMEM((3, N, HD, F), BF),
        pltpu.VMEM((3, N, 2 * HD, F), BF),
        pltpu.VMEM((1, D), F32),
        pltpu.VMEM((1, D), F32),
        pltpu.VMEM((D, 128), BF),
        pltpu.VMEM((D, F), BF),
        pltpu.VMEM((D, F), BF),
        *[
            pltpu.VMEM(shape + (width,), BF)
            for width, by_z in ((768, True), (768, False), (768, True), (896, True))
            for shape in (
                ((2, 8, 96), (8, 96), (2, 96), (2, 2, 96), (8,), (2, N, 16), (2, N, 16))
                if by_z
                else ((2, 8, 96), (8, 96), (2, 96), (2, 2, 96), (4, 48), (4, 16), (4, 16))
            )
        ],
        pltpu.VMEM((104, 896), F32),
        dma((2,)),
        dma((5,)),
        dma((11,)),
        dma((3, N)), dma((3, N)),
        dma((3, N)), dma((3, N)),
        dma((3, N)), dma((3, N)),
        dma((3, N)), dma((3, N)),
        dma((3, N)), dma((3, N)),
        dma((4,)), dma((4,)),
        dma((4, 30)), dma((4, 30)),
    ]
    return pl.pallas_call(
        kernel,
        out_shape=[rows] * 5
        + [jax.ShapeDtypeStruct((16, D + 128), F32), jax.ShapeDtypeStruct((16, D), F32)],
        in_specs=[smem] + [hbm] * 7 + [vmem] * 4,
        out_specs=[hbm] * 5 + [vmem] * 2,
        scratch_shapes=scratch,
        compiler_params=pltpu.CompilerParams(
            collective_id=0, has_side_effects=True, vmem_limit_bytes=62 * 1024 * 1024
        ),
    )(lengths, q, k, v, res, go, wo, wp, ng, taps, cb, cg)


def finish(gw_ref, gp_ref, *refs):
    sources, targets, (gow_ref, gpw_ref, gker_ref, gvec_ref), (held, sems) = refs[:5], refs[5:10], refs[10:14], refs[14:]
    inward = [pltpu.make_async_copy(sources[i], held.at[i], sems.at[0, i]) for i in range(5)]
    outward = [pltpu.make_async_copy(held.at[i], targets[i], sems.at[1, i]) for i in range(5)]
    for copy in inward:
        copy.start()
    for i in range(5):
        inward[i].wait()
        outward[i].start()
    gow_ref[...] = gw_ref[:12, :D]
    gpw_ref[...] = gp_ref[:12, :]
    gker_ref[...] = gw_ref[:12, D : D + KERN]
    gvec_ref[...] = gw_ref[:, D:].T[KERN : KERN + 3, :12]
    for copy in outward:
        copy.wait()


def finished(rows, gw, gp):
    vmem = pl.BlockSpec(memory_space=pltpu.VMEM)
    hbm = pl.BlockSpec(memory_space=pl.ANY)
    return pl.pallas_call(
        finish,
        out_shape=[jax.ShapeDtypeStruct((F, D), BF)] * 5
        + [jax.ShapeDtypeStruct(shape, F32) for shape in ((12, D), (12, D), (12, KERN), (3, 12))],
        in_specs=[vmem] * 2 + [hbm] * 5,
        out_specs=[hbm] * 5 + [vmem] * 4,
        scratch_shapes=[pltpu.VMEM((5, F, D), BF), pltpu.SemaphoreType.DMA((2, 5))],
        compiler_params=pltpu.CompilerParams(vmem_limit_bytes=62 * 1024 * 1024),
    )(gw, gp, *rows)


def local(
    residual_in, query_rows, key_rows, value_rows, lengths, out_weight, norm_gain, conv_kernel,
    conv_bias, conv_gain, point_weight, grad_out,
):
    outs = fused(
        lengths, query_rows[0], key_rows[0], value_rows[0], residual_in[0], grad_out[0],
        out_weight, point_weight, norm_gain.reshape(NB, 128), conv_kernel,
        conv_bias.reshape(NB, 128), conv_gain.reshape(NB, 128),
    )
    outs = finished(outs[:5], *outs[5:])
    return (*[x[None] for x in outs[:5]], *[x.T for x in outs[5:8]], outs[8])


def solution(mesh):
    rows = P("dp", "ctx", None)
    split = P(None, ("dp", "ctx"))
    in_specs = (rows,) * 4 + (P("dp"),) + (P(),) * 6 + (rows,)
    out_specs = (rows,) * 5 + (split,) * 4
    return jax.shard_map(local, mesh=mesh, in_specs=in_specs, out_specs=out_specs, check_vma=False)
```

```python
import jax
import jax.numpy as jnp
from jax import lax
from jax.experimental import pallas as pl
from jax.experimental.pallas import tpu as pltpu
from jax.sharding import PartitionSpec as P

N = 8
F = 128
D = 1536
S = 1024
HD = 64
KERN = 31
NB = D // 128
TILE = 256
EPSILON = 1e-05
MASKED = -1e30
MESH = pl.DeviceIdType.MESH
BF = jnp.bfloat16
F32 = jnp.float32


def dot(a, b):
    return jnp.dot(a, b, preferred_element_type=F32)


def dot_nt(a, b):
    return lax.dot_general(a, b, (((1,), (1,)), ((), ())), preferred_element_type=F32)


def iota(shape, dim):
    return lax.broadcasted_iota(jnp.int32, shape, dim)


def kernel(
    len_ref, q_hbm, k_hbm, v_hbm, res_hbm, go_hbm, wo_hbm, wp_hbm, ng_ref, taps_ref, cb_ref, cg_ref,
    bo_hbm, gr_hbm, gq_hbm, gk_hbm, gv_hbm, gw_ref, gp_ref,
    q_ref, k_ref, v_ref, res_ref, go_ref, bo_ref, gr_ref, gq_ref, gk_ref, gv_ref, wo, wp, snd, rcv, kaug, qaug, vta, vaug, pt, inv, obuf, att_t, att, mixed, n1, r1, cin, cp, csum,
    gact, gm, act, gc, gcl, gpad, vacc, lh, rh, dsnd, do, doaug, qz, dz, kt, rq, rkv,
    ng, cg, small_t, rows_t, rows_p, rows_y, *rest,
):
    me = lax.axis_index("ctx")
    dp = lax.axis_index("dp")
    length = len_ref[0]
    sums, rest = [rest[7 * i : 7 * i + 7] for i in range(5)], rest[35:]
    (
        wide, flat, w_sem, i_sem, e_sem, s_q, r_q, s_o, r_o, s_d, r_d, s_g, r_g, s_k, r_k, s_h, r_h, s_r, r_r,
    ) = rest
    dst = wo.at[pl.ds(0, S), pl.ds(0, S)]
    sq, skv = snd.at[:, :, pl.ds(0, HD)], snd.at[:, :, pl.ds(HD, 2 * HD)]
    core = lax.rem(dp, 2)
    y = lax.rem(lax.div(dp, 2), 2)
    z = lax.div(dp, 4)
    def at(offset):
        return lax.rem(me + (offset + N), N)

    x = lax.rem(me, 4)
    y_low = lax.div(me, 4)
    sibling = (dp + 1 - 2 * core, me)

    def in_z(offset):
        return lax.rem(z + (offset + 4), 4)

    def in_x(offset):
        return lax.rem(x + (offset + 4), 4)

    def z_device(offset):
        return (4 * in_z(offset) + 2 * y + core, me)

    def x_device(offset):
        return (dp, 4 * y_low + in_x(offset))

    def in_y(offset):
        return lax.rem(2 * y + y_low + (offset + 4), 4)

    def side_device(offset):
        return (4 * z + 2 * lax.div(in_y(offset), 2) + core, 4 * lax.rem(in_y(offset), 2) + x)

    def y_device(other, offset):
        return (dp + 2 - 4 * y if other else dp, at(offset))

    peers = [sibling] + [z_device(i) for i in (1, 2, 3)]
    peers += [y_device(b, o) for b in range(2) for o in range(N) if b or o]

    barrier = pltpu.get_barrier_semaphore()
    for peer in peers:
        pl.semaphore_signal(barrier, inc=1, device_id=peer, device_id_type=MESH)

    loads = [
        pltpu.make_async_copy(source, target, i_sem.at[i])
        for i, (source, target) in enumerate(
            ((q_hbm, q_ref), (k_hbm, k_ref), (v_hbm, v_ref), (go_hbm, go_ref), (res_hbm, res_ref))
        )
    ]
    for load in loads:
        load.start()
    wp_copy = pltpu.make_async_copy(wp_hbm, wp, w_sem.at[0])
    wo_copy = pltpu.make_async_copy(wo_hbm, wo, w_sem.at[1])
    wp_copy.start()
    wo_copy.start()

    def exchange(source, target, send_sem, recv_sem, h):
        def copy(o):
            return pltpu.make_async_remote_copy(
                src_ref=source.at[h, at(o)],
                dst_ref=target.at[h, me],
                send_sem=send_sem.at[h, o],
                recv_sem=recv_sem.at[h, o],
                device_id=(dp, at(o)),
                device_id_type=MESH,
            )

        def arrival(o):
            block = target.at[h, at(-o)]
            return pltpu.make_async_remote_copy(
                src_ref=block,
                dst_ref=block,
                send_sem=send_sem.at[h, o],
                recv_sem=recv_sem.at[h, o],
                device_id=(dp, at(-o)),
                device_id_type=MESH,
            )

        def start():
            for o in (4, 3, 5, 2, 6, 1, 7):
                copy(o).start()
            target[h, me] = source[h, me]

        def start_one(j):
            @pl.when(j != me)
            def _():
                o = lax.rem(j - me + N, N)
                pltpu.make_async_remote_copy(
                    src_ref=source.at[h, j],
                    dst_ref=target.at[h, me],
                    send_sem=send_sem.at[h, o],
                    recv_sem=recv_sem.at[h, o],
                    device_id=(dp, j),
                    device_id_type=MESH,
                ).start()

        def keep():
            target[h, me] = source[h, me]

        def wait():
            for o in range(1, N):
                arrival(o).wait_recv()

        def drain():
            for o in range(1, N):
                copy(o).wait_send()

        return start, wait, drain, start_one, keep

    ex_q = [exchange(snd, rcv, s_q, r_q, h) for h in range(3)]
    ex_o = [exchange(obuf, att_t, s_o, r_o, h) for h in range(3)]
    ex_d = [exchange(dsnd, do, s_d, r_d, h) for h in range(3)]
    ex_g = [exchange(sq, rq, s_g, r_g, h) for h in range(3)]
    ex_k = [exchange(skv, rkv, s_k, r_k, h) for h in range(3)]

    def ring(k, along, device):
        term, first, far, near = sums[k][:4]
        here = along(0)

        def to(source, target, i, peer):
            return pltpu.make_async_remote_copy(
                src_ref=source,
                dst_ref=target,
                send_sem=s_r.at[k, i],
                recv_sem=r_r.at[k, i],
                device_id=peer,
                device_id_type=MESH,
            )

        up, down = 2 * along(1), 2 * along(-1)
        opposite = 2 * along(2)
        far_copies = (
            to(term.at[core, opposite], far.at[0], 8, device(1)),
            to(term.at[core, opposite + 1], far.at[1], 9, device(-1)),
        )
        plain_copies = (
            to(term.at[core, up + 1], near.at[0, 1], 10, device(1)),
            to(term.at[core, down], near.at[1, 0], 11, device(-1)),
        )
        joint_copies = (
            to(term.at[core, up], near.at[0, 0], 12, device(1)),
            to(term.at[core, down + 1], near.at[1, 1], 13, device(-1)),
        )

        def cores(i):
            return to(term.at[1 - core, i], first.at[i], i, sibling)

        def begin(blocks, copies):
            for i, copy in zip(blocks, copies):
                cores(i).wait_recv()
                term[core, i] = term[core, i] + first[i]
                if copy is not None:
                    copy.start()

        def start():
            begin((opposite, opposite + 1), far_copies)

        def more():
            blocks = (up + 1, down, up, down + 1, 2 * here, 2 * here + 1)
            begin(blocks, plain_copies + (None,) * 4)

        def join():
            for a, (copy, i) in enumerate(zip(far_copies, (up, down + 1))):
                copy.wait_recv()
                term[core, i] = term[core, i] + far[a]
                joint_copies[a].start()

        def total():
            for copy in plain_copies + joint_copies:
                copy.wait_recv()
            parts = []
            for a in range(2):
                part = term[core, 2 * here + a].astype(F32) + near[0, a].astype(F32)
                parts.append(part + near[1, a].astype(F32))
            return parts

        def drain():
            for i in range(8):
                cores(i).wait_send()
            for copy in far_copies + plain_copies + joint_copies:
                copy.wait_send()

        return to, cores, (start, more), join, total, drain

    def slices(part, split, count, width):
        rows, full = part.shape
        most = 3 * width // 4
        wide[:rows, :full] = part
        for j in range(count):
            flat[:12, :most] = wide[12 * j : 12 * j + 12, :most]
            for g in range(3):
                flat[12:, g * most // 3 : (g + 1) * most // 3] = wide[12 * j + 4 * g : 12 * j + 4 * g + 4, most:width]
            if full > width:
                flat[:12, most : most + full - width] = wide[12 * j : 12 * j + 12, width:full]
            split[j] = flat[:, : most + full - width].astype(BF)

    def unpacked(packed, target, begin, width):
        most = 3 * width // 4
        target[:12, begin : begin + most] = packed[:12, :most]
        for g in range(3):
            block = packed[12:, g * most // 3 : (g + 1) * most // 3]
            target[4 * g : 4 * g + 4, begin + most : begin + width] = block
        rest = packed.shape[1] - most
        if rest:
            target[:12, begin + width : begin + width + rest] = packed[:12, most:]

    def z_reducer(k, width):
        to, cores, start, join, total, drain_ring = ring(k, in_z, z_device)
        split, last = sums[k][5], sums[k][6]
        others = [(b, o) for b in range(2) for o in range(N) if b or o]

        def sent(b, o):
            side = 1 - y if b else y
            return to(split.at[side, at(o)], last.at[y, me], 14 + N * b + o, y_device(b, o))

        def arrival(b, o):
            block = last.at[1 - y if b else y, at(-o)]
            return to(block, block, 14 + N * b + o, y_device(b, -o))

        def spread():
            for a, part in enumerate(total()):
                slices(part, split.at[a], N, width)
            for b, o in others:
                sent(b, o).start()
            last[y, me] = split[y, me]

        def finish():
            for b, o in others:
                arrival(b, o).wait_recv()
            result = jnp.zeros(last.shape[2:], F32)
            for b in range(2):
                for j in range(N):
                    result = result + last[b, j].astype(F32)
            return result

        def drain():
            drain_ring()
            for b, o in others:
                sent(b, o).wait_send()

        return cores, start, join, spread, finish, drain

    def side_reducer(k, width, along, device, across, across_device):
        to, cores, start, join, total, drain_ring = ring(k, along, device)
        here, mine = along(0), across(0)
        term = sums[k][0]
        in_column, split, last = sums[k][4:]

        def column(o):
            c = across(o)
            rows = pl.ds(pl.multiple_of(48 * lax.rem(c, 2), 16), 48)
            block = term.at[core, 2 * here + lax.div(c, 2), rows]
            return to(block, in_column.at[mine], 13 + o, across_device(o))

        def column_arrival(o):
            block = in_column.at[across(-o)]
            return to(block, block, 13 + o, across_device(-o))

        def sent(b):
            return to(split.at[in_z(b)], last.at[z], 16 + b, z_device(b))

        def arrival(b):
            block = last.at[in_z(-b)]
            return to(block, block, 16 + b, z_device(-b))

        def spread_across():
            for a, part in enumerate(total()):
                term[core, 2 * here + a] = part.astype(BF)
            for o in (1, 2, 3):
                column(o).start()

        def spread():
            own = pl.ds(pl.multiple_of(48 * lax.rem(mine, 2), 16), 48)
            part = term[core, 2 * here + lax.div(mine, 2), own, :].astype(F32)
            for o in (1, 2, 3):
                column_arrival(o).wait_recv()
                part = part + in_column[across(-o)].astype(F32)
            slices(part, split, 4, width)
            for b in (1, 2, 3):
                sent(b).start()
            last[z] = split[z]

        def finish():
            for b in (1, 2, 3):
                arrival(b).wait_recv()
            result = last[0].astype(F32)
            for j in (1, 2, 3):
                result = result + last[j].astype(F32)
            return result

        def drain():
            drain_ring()
            for i in (1, 2, 3):
                column(i).wait_send()
                sent(i).wait_send()

        return cores, start, join, spread, finish, drain, spread_across

    point_z = z_reducer(0, 512)
    point_x = side_reducer(1, 512, in_x, x_device, in_y, side_device)
    point_y = side_reducer(2, 512, in_y, side_device, in_x, x_device)
    out_one, out_two = z_reducer(3, 1024), z_reducer(4, 512)

    def weight_term(rows, others, begin, width, k, by_z, send):
        term = sums[k][0]

        def block(i, carry):
            for a in range(2):
                if by_z and a:
                    break
                base = 192 * i if by_z else 192 * i + 768 * a
                left = rows[pl.ds(pl.multiple_of(base, 64), 192), :]
                for n in range(width // 256):
                    cols = slice(n * 256, (n + 1) * 256)
                    part = dot(left, others[:, begin + n * 256 : begin + (n + 1) * 256]).astype(BF)
                    if by_z:
                        term[0, i, :, cols] = part[:96]
                        term[1, i, :, cols] = part[96:]
                    else:
                        term[a, 2 * i, :, cols] = part[:96]
                        term[a, 2 * i + 1, :, cols] = part[96:]
            if term.shape[3] > width:
                for a in range(2):
                    at_rows = pl.ds(pl.multiple_of(i * 192 + a * 96, 32), 96)
                    term[a, i, :, width:] = small_t[at_rows, :]
            if by_z:
                send(i).start()
            else:
                send(2 * i).start()
                send(2 * i + 1).start()
            return carry

        lax.fori_loop(0, 8 if by_z else 4, block, 0)

    def turn(rows):
        for c in range(NB):
            rows_t[c * 128 : (c + 1) * 128, :] = rows[:, c * 128 : (c + 1) * 128].T

    for load in loads[:3]:
        load.wait()
    for h in range(3):
        for b in range(4):
            cols = slice((4 * h + b) * 128, (4 * h + b + 1) * 128)
            for a, ref in enumerate((q_ref, k_ref, v_ref)):
                block = ref[:, cols]
                if a == 0:
                    block = (block.astype(F32) * 0.125).astype(BF)
                block = block.T
                snd[h, 2 * b, a * HD : (a + 1) * HD, :] = block[:HD]
                snd[h, 2 * b + 1, a * HD : (a + 1) * HD, :] = block[HD:]
        if h == 0:
            pl.semaphore_wait(barrier, len(peers))
        ex_q[h][0]()

    for c in range(NB):
        ng[:, c * 128 : (c + 1) * 128] = ng_ref[c : c + 1, :]
        cg[:, c * 128 : (c + 1) * 128] = cg_ref[c : c + 1, :]

    loads[3].wait()
    own_valid = me * F + iota((F, 1), 0) < length
    gm[...] = jnp.where(own_valid, go_ref[...], jnp.zeros_like(go_ref))
    wp_copy.wait()

    def act_grad(c, carry):
        cols = pl.ds(pl.multiple_of(c * 256, 256), 256)
        gact[:, cols] = dot_nt(gm[...], wp[cols, :])
        return carry

    lax.fori_loop(0, D // 256, act_grad, 0)

    turn(gm)

    def ordered(b, carry):
        r = iota((192, 1), 0)
        one, two = lax.div(r, 48), lax.rem(b, 4)
        d = 384 * lax.rem(lax.div(r, 12), 4) + lax.rem(r, 12) + 96 * lax.div(b, 4)
        by_x = 192 * lax.div(one, 2) + 48 * lax.rem(one, 2) + 12 * two
        by_y = 192 * lax.div(two, 2) + 48 * lax.rem(two, 2) + 12 * one
        for ref, more in ((rows_p, by_x), (rows_y, by_y)):
            pick = jnp.where(iota((192, D), 1) == d + more, 1.0, 0.0).astype(BF)
            ref[pl.ds(pl.multiple_of(192 * b, 64), 192), :] = dot_nt(pick, gm[...]).astype(BF)
        return carry

    lax.fori_loop(0, 8, ordered, 0)

    qaug[HD:, :] = (iota((HD, S), 0) == 0).astype(F32).astype(BF)
    vta[HD:, :] = (iota((16, S), 0) == 0).astype(F32).astype(BF)
    qz[HD:, :] = jnp.zeros((HD, S), BF)
    dz[:HD, :] = jnp.zeros((HD, S), BF)
    doaug[16:HD, :] = jnp.zeros((HD - 16, S), BF)

    def turned(i):
        return lax.rem(i + lax.div(me, 2) + 1, 4)

    for h in range(3):
        ex_q[h][1]()
        lane = iota((F, 128), 1)
        for j in range(N):
            cols = slice(j * F, (j + 1) * F)
            qaug[:HD, cols] = rcv[h, j, :HD, :]
            vta[:HD, cols] = rcv[h, j, 2 * HD :, :]
            both = rcv[h, j, HD:, :].T
            bias = jnp.where(j * F + iota((F, 128), 0) < length, 0.0, MASKED)
            bias = jnp.where(lane == HD, bias, 0.0).astype(BF)
            ones = jnp.where(lane < 2, 1.0, 0.0).astype(BF)
            kaug[cols, :] = jnp.where(lane < HD, both, bias)
            vaug[h, cols, :] = jnp.where(lane < HD, ones, both)

        def attend(i, carry, h=h):
            i = turned(i)
            cols = pl.ds(pl.multiple_of(i * TILE, TILE), TILE)
            scores = dot(kaug[...], qaug[:, cols])
            top = jnp.max(scores, axis=0, keepdims=True)
            weights = jnp.exp(scores - top).astype(BF)
            pt[h, :, cols] = weights
            summed = dot(vta[...], weights)
            scale = 1.0 / summed[HD : HD + 1, :]
            inv[h, :, cols] = scale
            rows = (summed[:HD] * scale).astype(BF)
            for a in range(TILE // F):
                obuf[h, i * (TILE // F) + a] = rows[:, a * F : (a + 1) * F]
            for a in range(TILE // F):
                ex_o[h][3](i * (TILE // F) + a)
            return carry

        lax.fori_loop(0, S // TILE, attend, 0)
        ex_o[h][4]()

    wo_copy.wait()
    loads[4].wait()
    for h in range(3):
        ex_o[h][1]()
        for b in range(4):
            pair = jnp.concatenate([att_t[h, 2 * b], att_t[h, 2 * b + 1]], axis=0)
            att[:, (4 * h + b) * 128 : (4 * h + b + 1) * 128] = pair.T

        def project(c, carry, h=h):
            cols = pl.ds(pl.multiple_of(c * 256, 256), 256)
            before = res_ref[:, cols].astype(F32) if h == 0 else mixed[:, cols]
            mixed[:, cols] = before + dot(
                att[:, 512 * h : 512 * (h + 1)], wo[512 * h : 512 * (h + 1), cols]
            )
            return carry

        lax.fori_loop(0, D // 256, project, 0)

    def mean_of(x):
        return jnp.sum(x, axis=1, keepdims=True) * (1.0 / D)

    def first_norm(i):
        rows = slice(i * 16, (i + 1) * 16)
        x = mixed[rows, :]
        x = x - mean_of(x)
        r = lax.rsqrt(mean_of(x * x) + EPSILON)
        n = x * r
        n1[rows, :] = n
        r1[rows, :] = r
        valid = me * F + i * 16 + iota((16, 1), 0) < length
        low = jnp.where(valid, n * ng[...], 0.0).astype(BF)
        cin[rows, :] = low
        low_wide = low.astype(F32)
        for c in range(NB):
            cp[c, 16 + i * 16 : 32 + i * 16, :] = low_wide[:, c * 128 : (c + 1) * 128]

    def edges(buffer, k):
        to_right = pltpu.make_async_remote_copy(
            src_ref=buffer.at[pl.ds(F - 16, 16)],
            dst_ref=lh.at[k],
            send_sem=s_h.at[2 * k],
            recv_sem=r_h.at[2 * k],
            device_id=(dp, at(1)),
            device_id_type=MESH,
        )
        to_left = pltpu.make_async_remote_copy(
            src_ref=buffer.at[pl.ds(0, 16)],
            dst_ref=rh.at[k],
            send_sem=s_h.at[2 * k + 1],
            recv_sem=r_h.at[2 * k + 1],
            device_id=(dp, at(-1)),
            device_id_type=MESH,
        )
        return to_right, to_left

    def place_edges(k, padded):
        left = jnp.where(me > 0, lh[k].astype(F32), 0.0)
        right = jnp.where(me < N - 1, rh[k].astype(F32), 0.0)
        for c in range(NB):
            padded[c, 0:16, :] = left[:, c * 128 : (c + 1) * 128]
            padded[c, F + 16 : F + 32, :] = right[:, c * 128 : (c + 1) * 128]

    ends = (0, F // 16 - 1)
    for i in ends:
        first_norm(i)
    halo = edges(cin, 0)
    for copy in halo:
        copy.start()
    for i in range(1, F // 16 - 1):
        first_norm(i)

    def convolve(c, starts, count):
        cols = pl.ds(pl.multiple_of(c * 128, 128), 128)
        totals = [jnp.broadcast_to(cb_ref[pl.ds(c, 1), :], (count, 128))] * len(starts)
        for t in range(KERN):
            tap = taps_ref[t : t + 1, cols]
            totals = [
                total + cp[c, start + t + 1 : start + t + 1 + count, :] * tap
                for total, start in zip(totals, starts)
            ]
        for total, start in zip(totals, starts):
            csum[start : start + count, cols] = total

    def convolve_inside(c, carry):
        convolve(c, (16,), F - 32)
        return carry

    def convolve_ends(c, carry):
        for a in range(2):
            convolve(2 * c + a, (0, F - 16), 16)
        return carry

    lax.fori_loop(0, NB, convolve_inside, 0)
    for copy in halo:
        copy.wait()
    place_edges(0, cp)
    lax.fori_loop(0, NB // 2, convolve_ends, 0)

    vacc[...] = jnp.zeros_like(vacc)

    def fold(x):
        return x[:8] + x[8:]

    def second_norm(i):
        rows = slice(i * 16, (i + 1) * 16)
        x = csum[rows, :]
        x = x - mean_of(x)
        r = lax.rsqrt(mean_of(x * x) + EPSILON)
        n = x * r
        scaled = n * cg[...]
        g = jax.nn.sigmoid(scaled)
        act[rows, :] = (scaled * g).astype(BF)
        back = gact[rows, :] * g * (1.0 + scaled * (1.0 - g))
        vacc[2] += fold(back * n)
        u = back * cg[...]
        grad = r * (u - mean_of(u) - n * mean_of(u * n))
        vacc[0] += fold(grad)
        low = grad.astype(BF)
        gcl[rows, :] = low
        low_wide = low.astype(F32)
        for c in range(NB):
            cols = slice(c * 128, (c + 1) * 128)
            gc[c, rows, :] = grad[:, cols]
            gpad[c, 16 + i * 16 : 32 + i * 16, :] = low_wide[:, cols]

    for i in range(F // 16):
        second_norm(i)
    halo2 = edges(gcl, 1)
    for copy in halo2:
        copy.start()

    weight_term(rows_t, act, 0, 512, 0, True, point_z[0])
    weight_term(rows_p, act, 512, 512, 1, False, point_x[0])
    weight_term(rows_y, act, 1024, 512, 2, False, point_y[0])

    points = (point_z, point_x, point_y)
    for part in (0, 1):
        for point in points:
            point[1][part]()

    for copy in halo2:
        copy.wait()
    place_edges(1, gpad)

    def convolve_back(c, carry):
        cols = pl.ds(pl.multiple_of(c * 128, 128), 128)
        total = jnp.zeros((F, 128), F32)
        for t in range(KERN):
            total = total + gpad[c, KERN - t : KERN - t + F, :] * taps_ref[t : t + 1, cols]
        csum[:, cols] = jnp.where(me * F + iota((F, 1), 0) < length, total, 0.0)
        return carry

    lax.fori_loop(0, NB, convolve_back, 0)

    def first_norm_back(i, carry):
        rows = pl.ds(pl.multiple_of(i * 16, 16), 16)
        x = csum[rows, :]
        n = n1[rows, :]
        vacc[1] += fold(x * n)
        u = x * ng[...]
        grad = r1[rows, :] * (u - mean_of(u) - n * mean_of(u * n))
        gr_ref[rows, :] = (gm[rows, :].astype(F32) + grad).astype(BF)
        return carry

    lax.fori_loop(0, F // 16, first_norm_back, 0)
    stores = [pltpu.make_async_copy(gr_ref, gr_hbm, e_sem.at[1])]
    stores[0].start()

    for h in range(3):

        def attended_rows(j, carry, h=h):
            for a in range(2):
                rows = pl.ds(pl.multiple_of(512 * h + (2 * j + a) * 128, 128), 128)
                part = dot_nt(wo[rows, :], gr_ref[...]).astype(BF)
                dsnd[h, 4 * j + 2 * a] = part[:HD]
                dsnd[h, 4 * j + 2 * a + 1] = part[HD:]
            return carry

        lax.fori_loop(0, 2, attended_rows, 0)
        ex_d[h][0]()

    turn(gr_ref)
    weight_term(rows_t, att, 0, 1024, 3, True, out_one[0])
    point_z[2]()
    point_x[2]()
    point_y[2]()
    out_one[1][0]()
    small = csum

    def tap_rows(c, carry):
        cols = pl.ds(pl.multiple_of(c * 128, 128), 128)
        grad = gc[c]
        for t in range(KERN):
            small[t : t + 1, cols] = jnp.sum(cp[c, t + 1 : t + 1 + F, :] * grad, axis=0, keepdims=True)
        return carry

    lax.fori_loop(0, NB, tap_rows, 0)
    for i in range(3):
        small[KERN + i : KERN + i + 1, :] = jnp.sum(vacc[i], axis=0, keepdims=True)
    small[KERN + 3 :, :] = jnp.zeros((128 - KERN - 3, D), F32)
    for c in range(NB):
        small_t[c * 128 : (c + 1) * 128, :] = small[:, c * 128 : (c + 1) * 128].T.astype(BF)
    weight_term(rows_t, att, 1024, 512, 4, True, out_two[0])
    out_two[1][0]()
    out_one[1][1]()
    out_two[1][1]()
    point_x[6]()
    point_y[6]()
    for h in range(3):
        ex_q[h][2]()

    for h in range(3):
        ex_d[h][1]()
        row = iota((16, F), 0)
        for j in range(N):
            cols = slice(j * F, (j + 1) * F)
            grad = do[h, j].astype(F32)
            scale = inv[h, :, cols]
            delta = -scale * jnp.sum(grad * obuf[h, j].astype(F32), axis=0, keepdims=True)
            high = delta.astype(BF).astype(F32)
            doaug[:16, cols] = jnp.where(row == 0, high, jnp.where(row == 1, delta - high, 0.0)).astype(BF)
            scaled = (grad * scale).astype(BF)
            doaug[HD:, cols] = scaled
            dz[HD:, cols] = scaled
            qz[:HD, cols] = rcv[h, j, :HD, :]
            kt[:, cols] = rcv[h, j, HD : 2 * HD, :]

        def back_queries(i, carry, h=h):
            i = turned(i)
            cols = pl.ds(pl.multiple_of(i * TILE, TILE), TILE)
            grads = dot(vaug[h], doaug[:, cols])
            grads = (pt[h, :, cols].astype(F32) * grads).astype(BF)
            dst[:, cols] = grads
            rows = (dot(kt[...], grads) * 0.125).astype(BF)
            for a in range(TILE // F):
                sq[h, i * (TILE // F) + a] = rows[:, a * F : (a + 1) * F]
            for a in range(TILE // F):
                ex_g[h][3](i * (TILE // F) + a)
            return carry

        lax.fori_loop(0, S // TILE, back_queries, 0)

        def back_keys(j, carry, h=h):
            j = at(j + 1)
            rows = pl.ds(pl.multiple_of(j * F, F), F)
            both = dot_nt(dst[rows, :], qz[...]) + dot_nt(pt[h, rows, :], dz[...])
            skv[h, j] = both.T.astype(BF)
            ex_k[h][3](j)
            return carry

        lax.fori_loop(0, N, back_keys, 0)
        ex_g[h][4]()
        ex_k[h][4]()
        if h == 0:
            out_one[2]()
            point_z[3]()
        elif h == 1:
            out_two[2]()
            point_x[3]()
            point_y[3]()

    def block_cols(c, carry):
        cols = pl.ds(pl.multiple_of(c * 256, 256), 256)
        bo_ref[:, cols] = (mixed[:, cols] + dot(act[...], wp[:, cols])).astype(BF)
        return carry

    lax.fori_loop(0, D // 256, block_cols, 0)
    stores.append(pltpu.make_async_copy(bo_ref, bo_hbm, e_sem.at[0]))
    stores[-1].start()

    for h in range(3):
        ex_g[h][1]()
        ex_k[h][1]()
        for b in range(4):
            cols = slice((4 * h + b) * 128, (4 * h + b + 1) * 128)
            for ref, source, part in (
                (gq_ref, rq, slice(0, HD)), (gk_ref, rkv, slice(0, HD)), (gv_ref, rkv, slice(HD, 2 * HD))
            ):
                pair = jnp.concatenate([source[h, 2 * b, part], source[h, 2 * b + 1, part]], axis=0)
                ref[:, cols] = pair.T
        cols = pl.ds(512 * h, 512)
        for a, (ref, hbm) in enumerate(((gq_ref, gq_hbm), (gk_ref, gk_hbm), (gv_ref, gv_hbm))):
            stores.append(pltpu.make_async_copy(ref.at[:, cols], hbm.at[:, cols], e_sem.at[2 + 3 * h + a]))
            stores[-1].start()
        if h == 1:
            out_one[3]()
        elif h == 2:
            out_two[3]()

    gp_ref[12:, :] = jnp.zeros((4, D), F32)
    gw_ref[12:, :] = jnp.zeros((4, D + 128), F32)
    unpacked(point_z[4](), gp_ref, 0, 512)
    unpacked(point_x[4](), gp_ref, 512, 512)
    unpacked(point_y[4](), gp_ref, 1024, 512)
    unpacked(out_one[4](), gw_ref, 0, 1024)
    unpacked(out_two[4](), gw_ref, 1024, 512)
    for reducer in (point_z, point_x, point_y, out_one, out_two):
        reducer[5]()
    for group in (ex_o, ex_d, ex_g, ex_k):
        for h in range(3):
            group[h][2]()
    for store in stores:
        store.wait()


def fused(lengths, q, k, v, res, go, wo, wp, ng, taps, cb, cg):
    vmem = pl.BlockSpec(memory_space=pltpu.VMEM)
    hbm = pl.BlockSpec(memory_space=pl.ANY)
    smem = pl.BlockSpec(memory_space=pltpu.SMEM)
    rows = jax.ShapeDtypeStruct((F, D), BF)
    dma = pltpu.SemaphoreType.DMA
    scratch = [
        *[pltpu.VMEM((F, D), BF)] * 10,
        pltpu.VMEM((D, D), BF),
        pltpu.VMEM((D, D), BF),
        pltpu.VMEM((3, N, 3 * HD, F), BF),
        pltpu.VMEM((3, N, 3 * HD, F), BF),
        pltpu.VMEM((S, 128), BF),
        pltpu.VMEM((128, S), BF),
        pltpu.VMEM((HD + 16, S), BF),
        pltpu.VMEM((3, S, 128), BF),
        pltpu.VMEM((3, S, S), BF),
        pltpu.VMEM((3, 1, S), F32),
        pltpu.VMEM((3, N, HD, F), BF),
        pltpu.VMEM((3, N, HD, F), BF),
        pltpu.VMEM((F, D), BF),
        pltpu.VMEM((F, D), F32),
        pltpu.VMEM((F, D), F32),
        pltpu.VMEM((F, 1), F32),
        pltpu.VMEM((F, D), BF),
        pltpu.VMEM((NB, F + 32, 128), F32),
        pltpu.VMEM((F, D), F32),
        pltpu.VMEM((F, D), F32),
        pltpu.VMEM((F, D), BF),
        pltpu.VMEM((F, D), BF),
        pltpu.VMEM((NB, F, 128), F32),
        pltpu.VMEM((F, D), BF),
        pltpu.VMEM((NB, F + 32, 128), F32),
        pltpu.VMEM((3, 8, D), F32),
        pltpu.VMEM((2, 16, D), BF),
        pltpu.VMEM((2, 16, D), BF),
        pltpu.VMEM((3, N, HD, F), BF),
        pltpu.VMEM((3, N, HD, F), BF),
        pltpu.VMEM((128, S), BF),
        pltpu.VMEM((128, S), BF),
        pltpu.VMEM((128, S), BF),
        pltpu.VMEM((HD, S), BF),
        pltpu.VMEM((3, N, HD, F), BF),
        pltpu.VMEM((3, N, 2 * HD, F), BF),
        pltpu.VMEM((1, D), F32),
        pltpu.VMEM((1, D), F32),
        pltpu.VMEM((D, 128), BF),
        pltpu.VMEM((D, F), BF),
        pltpu.VMEM((D, F), BF),
        pltpu.VMEM((D, F), BF),
        *[
            pltpu.VMEM(shape, BF)
            for w, last, by_z in (
                (512, 384, True), (512, 384, False), (512, 384, False), (1024, 768, True), (640, 512, True)
            )
            for shape in (
                (2, 8, 96, w),
                (8, 96, w),
                (2, 96, w),
                (2, 2, 96, w),
                (8, w) if by_z else (4, 48, w),
                (2, N, 16, last) if by_z else (4, 16, last),
                (2, N, 16, last) if by_z else (4, 16, last),
            )
        ],
        pltpu.VMEM((96, 1024), F32),
        pltpu.VMEM((16, 768), F32),
        dma((2,)),
        dma((5,)),
        dma((11,)),
        dma((3, N)), dma((3, N)),
        dma((3, N)), dma((3, N)),
        dma((3, N)), dma((3, N)),
        dma((3, N)), dma((3, N)),
        dma((3, N)), dma((3, N)),
        dma((4,)), dma((4,)),
        dma((5, 30)), dma((5, 30)),
    ]
    return pl.pallas_call(
        kernel,
        out_shape=[rows] * 5
        + [jax.ShapeDtypeStruct((16, D + 128), F32), jax.ShapeDtypeStruct((16, D), F32)],
        in_specs=[smem] + [hbm] * 7 + [vmem] * 4,
        out_specs=[hbm] * 5 + [vmem] * 2,
        scratch_shapes=scratch,
        compiler_params=pltpu.CompilerParams(
            collective_id=0, has_side_effects=True, vmem_limit_bytes=62 * 1024 * 1024
        ),
    )(lengths, q, k, v, res, go, wo, wp, ng, taps, cb, cg)


def finish(gw_ref, gp_ref, *refs):
    sources, targets, (gow_ref, gpw_ref, gker_ref, gvec_ref), (held, sems) = refs[:5], refs[5:10], refs[10:14], refs[14:]
    inward = [pltpu.make_async_copy(sources[i], held.at[i], sems.at[0, i]) for i in range(5)]
    outward = [pltpu.make_async_copy(held.at[i], targets[i], sems.at[1, i]) for i in range(5)]
    for copy in inward:
        copy.start()
    for i in range(5):
        inward[i].wait()
        outward[i].start()
    gow_ref[...] = gw_ref[:12, :D]
    gpw_ref[...] = gp_ref[:12, :]
    gker_ref[...] = gw_ref[:12, D : D + KERN]
    gvec_ref[...] = gw_ref[:, D:].T[KERN : KERN + 3, :12]
    for copy in outward:
        copy.wait()


def finished(rows, gw, gp):
    vmem = pl.BlockSpec(memory_space=pltpu.VMEM)
    hbm = pl.BlockSpec(memory_space=pl.ANY)
    return pl.pallas_call(
        finish,
        out_shape=[jax.ShapeDtypeStruct((F, D), BF)] * 5
        + [jax.ShapeDtypeStruct(shape, F32) for shape in ((12, D), (12, D), (12, KERN), (3, 12))],
        in_specs=[vmem] * 2 + [hbm] * 5,
        out_specs=[hbm] * 5 + [vmem] * 4,
        scratch_shapes=[pltpu.VMEM((5, F, D), BF), pltpu.SemaphoreType.DMA((2, 5))],
        compiler_params=pltpu.CompilerParams(vmem_limit_bytes=62 * 1024 * 1024),
    )(gw, gp, *rows)


def local(
    residual_in, query_rows, key_rows, value_rows, lengths, out_weight, norm_gain, conv_kernel,
    conv_bias, conv_gain, point_weight, grad_out,
):
    outs = fused(
        lengths, query_rows[0], key_rows[0], value_rows[0], residual_in[0], grad_out[0],
        out_weight, point_weight, norm_gain.reshape(NB, 128), conv_kernel,
        conv_bias.reshape(NB, 128), conv_gain.reshape(NB, 128),
    )
    outs = finished(outs[:5], *outs[5:])
    return (*[x[None] for x in outs[:5]], *[x.T for x in outs[5:8]], outs[8])


def solution(mesh):
    rows = P("dp", "ctx", None)
    split = P(None, ("dp", "ctx"))
    in_specs = (rows,) * 4 + (P("dp"),) + (P(),) * 6 + (rows,)
    out_specs = (rows,) * 5 + (split,) * 4
    return jax.shard_map(local, mesh=mesh, in_specs=in_specs, out_specs=out_specs, check_vma=False)
```

```python
import jax
import jax.numpy as jnp
from jax import lax
from jax.experimental import pallas as pl
from jax.experimental.pallas import tpu as pltpu
from jax.sharding import PartitionSpec as P

N = 8
F = 128
D = 1536
S = 1024
HD = 64
KERN = 31
NB = D // 128
TILE = 256
EPSILON = 1e-05
MASKED = -1e30
MESH = pl.DeviceIdType.MESH
BF = jnp.bfloat16
F32 = jnp.float32


def dot(a, b):
    return jnp.dot(a, b, preferred_element_type=F32)


def dot_nt(a, b):
    return lax.dot_general(a, b, (((1,), (1,)), ((), ())), preferred_element_type=F32)


def iota(shape, dim):
    return lax.broadcasted_iota(jnp.int32, shape, dim)


def kernel(
    len_hbm, q_hbm, k_hbm, v_hbm, res_hbm, go_hbm, wo_hbm, wp_hbm, ng_hbm, taps_hbm, cb_hbm, cg_hbm,
    bo_hbm, gr_hbm, gq_hbm, gk_hbm, gv_hbm, gw_hbm, gp_hbm,
    len_ref, ng_ref, taps_ref, cb_ref, cg_ref, gw_ref, gp_ref,
    q_ref, k_ref, v_ref, res_ref, go_ref, bo_ref, gr_ref, gq_ref, gk_ref, gv_ref, wo, wp, snd, rcv, kaug, qaug, vta, vaug, pt, inv, obuf, att_t, att, mixed, n1, r1, cin, cp, csum,
    gact, gm, act, gc, gcl, gpad, vacc, lh, rh, dsnd, do, doaug, qz, dz, kt, rq, rkv,
    ng, cg, small_t, rows_t, rows_p, rows_y, *rest,
):
    me = lax.axis_index("ctx")
    dp = lax.axis_index("dp")
    sums, rest = [rest[7 * i : 7 * i + 7] for i in range(5)], rest[35:]
    (
        wide, flat, w_sem, i_sem, e_sem, s_q, r_q, s_v, r_v, s_o, r_o, s_d, r_d, s_g, r_g, s_k, r_k, s_h, r_h, s_r, r_r,
    ) = rest
    dst = wo.at[pl.ds(0, S), pl.ds(0, S)]
    sq, skv = snd.at[:, :, pl.ds(0, HD)], snd.at[:, :, pl.ds(HD, 2 * HD)]
    core = lax.rem(dp, 2)
    y = lax.rem(lax.div(dp, 2), 2)
    z = lax.div(dp, 4)
    def at(offset):
        return lax.rem(me + (offset + N), N)

    x = lax.rem(me, 4)
    y_low = lax.div(me, 4)
    sibling = (dp + 1 - 2 * core, me)

    def in_z(offset):
        return lax.rem(z + (offset + 4), 4)

    def in_x(offset):
        return lax.rem(x + (offset + 4), 4)

    def z_device(offset):
        return (4 * in_z(offset) + 2 * y + core, me)

    def x_device(offset):
        return (dp, 4 * y_low + in_x(offset))

    def in_y(offset):
        return lax.rem(2 * y + y_low + (offset + 4), 4)

    def side_device(offset):
        return (4 * z + 2 * lax.div(in_y(offset), 2) + core, 4 * lax.rem(in_y(offset), 2) + x)

    def y_device(other, offset):
        return (dp + 2 - 4 * y if other else dp, at(offset))

    peers = [sibling] + [z_device(i) for i in (1, 2, 3)]
    peers += [y_device(b, o) for b in range(2) for o in range(N) if b or o]

    barrier = pltpu.get_barrier_semaphore()
    for peer in peers:
        pl.semaphore_signal(barrier, inc=1, device_id=peer, device_id_type=MESH)

    loads = [
        pltpu.make_async_copy(source, target, i_sem.at[i])
        for i, (source, target) in enumerate((
            (q_hbm, q_ref), (k_hbm, k_ref), (v_hbm, v_ref), (go_hbm, go_ref), (res_hbm, res_ref),
            (len_hbm, len_ref), (ng_hbm, ng_ref), (taps_hbm, taps_ref), (cb_hbm, cb_ref), (cg_hbm, cg_ref),
        ))
    ]
    for load in loads:
        load.start()
    wp_copy = pltpu.make_async_copy(wp_hbm, wp, w_sem.at[0])
    wo_copy = pltpu.make_async_copy(wo_hbm, wo, w_sem.at[1])
    wp_copy.start()
    wo_copy.start()

    def exchange(source, target, send_sem, recv_sem, h):
        def copy(o):
            return pltpu.make_async_remote_copy(
                src_ref=source.at[h, at(o)],
                dst_ref=target.at[h, me],
                send_sem=send_sem.at[h, o],
                recv_sem=recv_sem.at[h, o],
                device_id=(dp, at(o)),
                device_id_type=MESH,
            )

        def arrival(o):
            block = target.at[h, at(-o)]
            return pltpu.make_async_remote_copy(
                src_ref=block,
                dst_ref=block,
                send_sem=send_sem.at[h, o],
                recv_sem=recv_sem.at[h, o],
                device_id=(dp, at(-o)),
                device_id_type=MESH,
            )

        def start():
            for o in (4, 3, 5, 2, 6, 1, 7):
                copy(o).start()
            target[h, me] = source[h, me]

        def start_one(j):
            @pl.when(j != me)
            def _():
                o = lax.rem(j - me + N, N)
                pltpu.make_async_remote_copy(
                    src_ref=source.at[h, j],
                    dst_ref=target.at[h, me],
                    send_sem=send_sem.at[h, o],
                    recv_sem=recv_sem.at[h, o],
                    device_id=(dp, j),
                    device_id_type=MESH,
                ).start()

        def keep():
            target[h, me] = source[h, me]

        def wait_one(j):
            @pl.when(j != me)
            def _():
                arrival(lax.rem(me - j + N, N)).wait_recv()

        def wait():
            for o in range(1, N):
                arrival(o).wait_recv()

        def drain():
            for o in range(1, N):
                copy(o).wait_send()

        return start, wait, drain, start_one, keep, wait_one

    ex_q = [exchange(snd.at[:, :, pl.ds(0, HD)], rcv.at[:, :, pl.ds(0, HD)], s_q, r_q, h) for h in range(3)]
    ex_v = [
        exchange(snd.at[:, :, pl.ds(HD, 2 * HD)], rcv.at[:, :, pl.ds(HD, 2 * HD)], s_v, r_v, h) for h in range(3)
    ]
    ex_o = [exchange(obuf, att_t, s_o, r_o, h) for h in range(3)]
    ex_d = [exchange(dsnd, do, s_d, r_d, h) for h in range(3)]
    ex_g = [exchange(sq, rq, s_g, r_g, h) for h in range(3)]
    ex_k = [exchange(skv, rkv, s_k, r_k, h) for h in range(3)]

    def ring(k, along, device):
        term, first, far, near = sums[k][:4]
        here = along(0)

        def to(source, target, i, peer):
            return pltpu.make_async_remote_copy(
                src_ref=source,
                dst_ref=target,
                send_sem=s_r.at[k, i],
                recv_sem=r_r.at[k, i],
                device_id=peer,
                device_id_type=MESH,
            )

        up, down = 2 * along(1), 2 * along(-1)
        opposite = 2 * along(2)
        far_copies = (
            to(term.at[core, opposite], far.at[0], 8, device(1)),
            to(term.at[core, opposite + 1], far.at[1], 9, device(-1)),
        )
        plain_copies = (
            to(term.at[core, up + 1], near.at[0, 1], 10, device(1)),
            to(term.at[core, down], near.at[1, 0], 11, device(-1)),
        )
        joint_copies = (
            to(term.at[core, up], near.at[0, 0], 12, device(1)),
            to(term.at[core, down + 1], near.at[1, 1], 13, device(-1)),
        )

        def cores(i):
            return to(term.at[1 - core, i], first.at[i], i, sibling)

        def begin(blocks, copies):
            for i, copy in zip(blocks, copies):
                cores(i).wait_recv()
                term[core, i] = term[core, i] + first[i]
                if copy is not None:
                    copy.start()

        def start():
            begin((opposite, opposite + 1), far_copies)

        def more():
            blocks = (up + 1, down, up, down + 1, 2 * here, 2 * here + 1)
            begin(blocks, plain_copies + (None,) * 4)

        def join():
            for a, (copy, i) in enumerate(zip(far_copies, (up, down + 1))):
                copy.wait_recv()
                term[core, i] = term[core, i] + far[a]
                joint_copies[a].start()

        def total():
            for copy in plain_copies + joint_copies:
                copy.wait_recv()
            parts = []
            for a in range(2):
                part = term[core, 2 * here + a].astype(F32) + near[0, a].astype(F32)
                parts.append(part + near[1, a].astype(F32))
            return parts

        def drain():
            for i in range(8):
                cores(i).wait_send()
            for copy in far_copies + plain_copies + joint_copies:
                copy.wait_send()

        return to, cores, (start, more), join, total, drain

    def slices(part, split, count, width):
        rows, full = part.shape
        most = 3 * width // 4
        wide[:rows, :full] = part
        for j in range(count):
            flat[:12, :most] = wide[12 * j : 12 * j + 12, :most]
            for g in range(3):
                flat[12:, g * most // 3 : (g + 1) * most // 3] = wide[12 * j + 4 * g : 12 * j + 4 * g + 4, most:width]
            if full > width:
                flat[:12, most : most + full - width] = wide[12 * j : 12 * j + 12, width:full]
            split[j] = flat[:, : most + full - width].astype(BF)

    def unpacked(packed, target, begin, width):
        most = 3 * width // 4
        target[:12, begin : begin + most] = packed[:12, :most]
        for g in range(3):
            block = packed[12:, g * most // 3 : (g + 1) * most // 3]
            target[4 * g : 4 * g + 4, begin + most : begin + width] = block
        rest = packed.shape[1] - most
        if rest:
            target[:12, begin + width : begin + width + rest] = packed[:12, most:]

    def z_reducer(k, width):
        to, cores, start, join, total, drain_ring = ring(k, in_z, z_device)
        split, last = sums[k][5], sums[k][6]
        others = [(b, o) for b in range(2) for o in range(N) if b or o]

        def sent(b, o):
            side = 1 - y if b else y
            return to(split.at[side, at(o)], last.at[y, me], 14 + N * b + o, y_device(b, o))

        def arrival(b, o):
            block = last.at[1 - y if b else y, at(-o)]
            return to(block, block, 14 + N * b + o, y_device(b, -o))

        def spread():
            for a, part in enumerate(total()):
                slices(part, split.at[a], N, width)
            for b, o in others:
                sent(b, o).start()
            last[y, me] = split[y, me]

        def finish():
            for b, o in others:
                arrival(b, o).wait_recv()
            result = jnp.zeros(last.shape[2:], F32)
            for b in range(2):
                for j in range(N):
                    result = result + last[b, j].astype(F32)
            return result

        def drain():
            drain_ring()
            for b, o in others:
                sent(b, o).wait_send()

        return cores, start, join, spread, finish, drain

    def side_reducer(k, width, along, device, across, across_device):
        to, cores, start, join, total, drain_ring = ring(k, along, device)
        here, mine = along(0), across(0)
        term = sums[k][0]
        in_column, split, last = sums[k][4:]

        def column(o):
            c = across(o)
            rows = pl.ds(pl.multiple_of(48 * lax.rem(c, 2), 16), 48)
            block = term.at[core, 2 * here + lax.div(c, 2), rows]
            return to(block, in_column.at[mine], 13 + o, across_device(o))

        def column_arrival(o):
            block = in_column.at[across(-o)]
            return to(block, block, 13 + o, across_device(-o))

        def sent(b):
            return to(split.at[in_z(b)], last.at[z], 16 + b, z_device(b))

        def arrival(b):
            block = last.at[in_z(-b)]
            return to(block, block, 16 + b, z_device(-b))

        def spread_across():
            for a, part in enumerate(total()):
                term[core, 2 * here + a] = part.astype(BF)
            for o in (1, 2, 3):
                column(o).start()

        def spread():
            own = pl.ds(pl.multiple_of(48 * lax.rem(mine, 2), 16), 48)
            part = term[core, 2 * here + lax.div(mine, 2), own, :].astype(F32)
            for o in (1, 2, 3):
                column_arrival(o).wait_recv()
                part = part + in_column[across(-o)].astype(F32)
            slices(part, split, 4, width)
            for b in (1, 2, 3):
                sent(b).start()
            last[z] = split[z]

        def finish():
            for b in (1, 2, 3):
                arrival(b).wait_recv()
            result = last[0].astype(F32)
            for j in (1, 2, 3):
                result = result + last[j].astype(F32)
            return result

        def drain():
            drain_ring()
            for i in (1, 2, 3):
                column(i).wait_send()
                sent(i).wait_send()

        return cores, start, join, spread, finish, drain, spread_across

    point_z = z_reducer(0, 512)
    point_x = side_reducer(1, 512, in_x, x_device, in_y, side_device)
    point_y = side_reducer(2, 512, in_y, side_device, in_x, x_device)
    out_one, out_two = z_reducer(3, 1024), z_reducer(4, 512)

    def weight_term(rows, others, begin, width, k, by_z, along, send):
        term = sums[k][0]

        def block(i, carry):
            i = lax.rem(i + 2 * along(2), 8) if by_z else lax.rem(i + along(2), 4)
            for a in range(2):
                if by_z and a:
                    break
                base = 192 * i if by_z else 192 * i + 768 * a
                left = rows[pl.ds(pl.multiple_of(base, 64), 192), :]
                for n in range(width // 256):
                    cols = slice(n * 256, (n + 1) * 256)
                    part = dot(left, others[:, begin + n * 256 : begin + (n + 1) * 256]).astype(BF)
                    if by_z:
                        term[0, i, :, cols] = part[:96]
                        term[1, i, :, cols] = part[96:]
                    else:
                        term[a, 2 * i, :, cols] = part[:96]
                        term[a, 2 * i + 1, :, cols] = part[96:]
            if term.shape[3] > width:
                for a in range(2):
                    at_rows = pl.ds(pl.multiple_of(i * 192 + a * 96, 32), 96)
                    term[a, i, :, width:] = small_t[at_rows, :]
            if by_z:
                send(i).start()
            else:
                send(2 * i).start()
                send(2 * i + 1).start()
            return carry

        lax.fori_loop(0, 8 if by_z else 4, block, 0)

    def turn(rows):
        for c in range(NB):
            rows_t[c * 128 : (c + 1) * 128, :] = rows[:, c * 128 : (c + 1) * 128].T

    for load in loads[:3]:
        load.wait()
    for h in range(3):
        for b in range(4):
            cols = slice((4 * h + b) * 128, (4 * h + b + 1) * 128)
            for a, ref in enumerate((q_ref, k_ref, v_ref)):
                block = ref[:, cols]
                if a == 0:
                    block = (block.astype(F32) * 0.125).astype(BF)
                block = block.T
                snd[h, 2 * b, a * HD : (a + 1) * HD, :] = block[:HD]
                snd[h, 2 * b + 1, a * HD : (a + 1) * HD, :] = block[HD:]
        if h == 0:
            pl.semaphore_wait(barrier, len(peers))
        ex_v[h][0]()
        ex_q[h][0]()

    for load in loads[5:]:
        load.wait()
    length = len_ref[0]
    for c in range(NB):
        ng[:, c * 128 : (c + 1) * 128] = ng_ref[c : c + 1, :]
        cg[:, c * 128 : (c + 1) * 128] = cg_ref[c : c + 1, :]

    loads[3].wait()
    own_valid = me * F + iota((F, 1), 0) < length
    gm[...] = jnp.where(own_valid, go_ref[...], jnp.zeros_like(go_ref))
    wp_copy.wait()

    def act_grad(c, carry):
        cols = pl.ds(pl.multiple_of(c * 256, 256), 256)
        gact[:, cols] = dot_nt(gm[...], wp[cols, :])
        return carry

    lax.fori_loop(0, D // 256, act_grad, 0)

    turn(gm)

    def ordered(b, carry):
        r = iota((192, 1), 0)
        one, two = lax.div(r, 48), lax.rem(b, 4)
        d = 384 * lax.rem(lax.div(r, 12), 4) + lax.rem(r, 12) + 96 * lax.div(b, 4)
        by_x = 192 * lax.div(one, 2) + 48 * lax.rem(one, 2) + 12 * two
        by_y = 192 * lax.div(two, 2) + 48 * lax.rem(two, 2) + 12 * one
        for ref, more in ((rows_p, by_x), (rows_y, by_y)):
            pick = jnp.where(iota((192, D), 1) == d + more, 1.0, 0.0).astype(BF)
            ref[pl.ds(pl.multiple_of(192 * b, 64), 192), :] = dot_nt(pick, gm[...]).astype(BF)
        return carry

    lax.fori_loop(0, 8, ordered, 0)

    qaug[HD:, :] = (iota((HD, S), 0) == 0).astype(F32).astype(BF)
    vta[HD:, :] = (iota((16, S), 0) == 0).astype(F32).astype(BF)
    qz[HD:, :] = jnp.zeros((HD, S), BF)
    dz[:HD, :] = jnp.zeros((HD, S), BF)
    doaug[16:HD, :] = jnp.zeros((HD - 16, S), BF)

    def turned(i):
        return lax.rem(i + lax.div(me, 2) + 1, 4)

    for h in range(3):
        ex_v[h][1]()
        lane = iota((F, 128), 1)
        for j in range(N):
            cols = slice(j * F, (j + 1) * F)
            vta[:HD, cols] = rcv[h, j, 2 * HD :, :]
            both = rcv[h, j, HD:, :].T
            bias = jnp.where(j * F + iota((F, 128), 0) < length, 0.0, MASKED)
            bias = jnp.where(lane == HD, bias, 0.0).astype(BF)
            ones = jnp.where(lane < 2, 1.0, 0.0).astype(BF)
            kaug[cols, :] = jnp.where(lane < HD, both, bias)
            vaug[h, cols, :] = jnp.where(lane < HD, ones, both)

        def attend(i, carry, h=h):
            i = turned(i)
            cols = pl.ds(pl.multiple_of(i * TILE, TILE), TILE)
            for a in range(TILE // F):
                j = i * (TILE // F) + a
                ex_q[h][5](j)
                qaug[:HD, pl.ds(pl.multiple_of(j * F, F), F)] = rcv[h, j, :HD, :]
            scores = dot(kaug[...], qaug[:, cols])
            top = jnp.max(scores, axis=0, keepdims=True)
            weights = jnp.exp(scores - top).astype(BF)
            pt[h, :, cols] = weights
            summed = dot(vta[...], weights)
            scale = 1.0 / summed[HD : HD + 1, :]
            inv[h, :, cols] = scale
            rows = (summed[:HD] * scale).astype(BF)
            for a in range(TILE // F):
                obuf[h, i * (TILE // F) + a] = rows[:, a * F : (a + 1) * F]
            for a in range(TILE // F):
                ex_o[h][3](i * (TILE // F) + a)
            return carry

        lax.fori_loop(0, S // TILE, attend, 0)
        ex_o[h][4]()

    wo_copy.wait()
    loads[4].wait()
    for h in range(3):
        ex_o[h][1]()
        for b in range(4):
            pair = jnp.concatenate([att_t[h, 2 * b], att_t[h, 2 * b + 1]], axis=0)
            att[:, (4 * h + b) * 128 : (4 * h + b + 1) * 128] = pair.T

        def project(c, carry, h=h):
            cols = pl.ds(pl.multiple_of(c * 256, 256), 256)
            before = res_ref[:, cols].astype(F32) if h == 0 else mixed[:, cols]
            mixed[:, cols] = before + dot(
                att[:, 512 * h : 512 * (h + 1)], wo[512 * h : 512 * (h + 1), cols]
            )
            return carry

        lax.fori_loop(0, D // 256, project, 0)

    def mean_of(x):
        return jnp.sum(x, axis=1, keepdims=True) * (1.0 / D)

    def first_norm(i):
        rows = slice(i * 16, (i + 1) * 16)
        x = mixed[rows, :]
        x = x - mean_of(x)
        r = lax.rsqrt(mean_of(x * x) + EPSILON)
        n = x * r
        n1[rows, :] = n
        r1[rows, :] = r
        valid = me * F + i * 16 + iota((16, 1), 0) < length
        low = jnp.where(valid, n * ng[...], 0.0).astype(BF)
        cin[rows, :] = low
        low_wide = low.astype(F32)
        for c in range(NB):
            cp[c, 16 + i * 16 : 32 + i * 16, :] = low_wide[:, c * 128 : (c + 1) * 128]

    def edges(buffer, k):
        to_right = pltpu.make_async_remote_copy(
            src_ref=buffer.at[pl.ds(F - 16, 16)],
            dst_ref=lh.at[k],
            send_sem=s_h.at[2 * k],
            recv_sem=r_h.at[2 * k],
            device_id=(dp, at(1)),
            device_id_type=MESH,
        )
        to_left = pltpu.make_async_remote_copy(
            src_ref=buffer.at[pl.ds(0, 16)],
            dst_ref=rh.at[k],
            send_sem=s_h.at[2 * k + 1],
            recv_sem=r_h.at[2 * k + 1],
            device_id=(dp, at(-1)),
            device_id_type=MESH,
        )
        return to_right, to_left

    def place_edges(k, padded):
        left = jnp.where(me > 0, lh[k].astype(F32), 0.0)
        right = jnp.where(me < N - 1, rh[k].astype(F32), 0.0)
        for c in range(NB):
            padded[c, 0:16, :] = left[:, c * 128 : (c + 1) * 128]
            padded[c, F + 16 : F + 32, :] = right[:, c * 128 : (c + 1) * 128]

    ends = (0, F // 16 - 1)
    for i in ends:
        first_norm(i)
    halo = edges(cin, 0)
    for copy in halo:
        copy.start()
    for i in range(1, F // 16 - 1):
        first_norm(i)

    def convolve(c, starts, count):
        cols = pl.ds(pl.multiple_of(c * 128, 128), 128)
        totals = [jnp.broadcast_to(cb_ref[pl.ds(c, 1), :], (count, 128))] * len(starts)
        for t in range(KERN):
            tap = taps_ref[t : t + 1, cols]
            totals = [
                total + cp[c, start + t + 1 : start + t + 1 + count, :] * tap
                for total, start in zip(totals, starts)
            ]
        for total, start in zip(totals, starts):
            csum[start : start + count, cols] = total

    def convolve_inside(c, carry):
        convolve(c, (16,), F - 32)
        return carry

    def convolve_ends(c, carry):
        for a in range(2):
            convolve(2 * c + a, (0, F - 16), 16)
        return carry

    lax.fori_loop(0, NB, convolve_inside, 0)
    for copy in halo:
        copy.wait()
    place_edges(0, cp)
    lax.fori_loop(0, NB // 2, convolve_ends, 0)

    vacc[...] = jnp.zeros_like(vacc)

    def fold(x):
        return x[:8] + x[8:]

    def second_norm(i):
        rows = slice(i * 16, (i + 1) * 16)
        x = csum[rows, :]
        x = x - mean_of(x)
        r = lax.rsqrt(mean_of(x * x) + EPSILON)
        n = x * r
        scaled = n * cg[...]
        g = jax.nn.sigmoid(scaled)
        act[rows, :] = (scaled * g).astype(BF)
        back = gact[rows, :] * g * (1.0 + scaled * (1.0 - g))
        vacc[2] += fold(back * n)
        u = back * cg[...]
        grad = r * (u - mean_of(u) - n * mean_of(u * n))
        vacc[0] += fold(grad)
        low = grad.astype(BF)
        gcl[rows, :] = low
        low_wide = low.astype(F32)
        for c in range(NB):
            cols = slice(c * 128, (c + 1) * 128)
            gc[c, rows, :] = grad[:, cols]
            gpad[c, 16 + i * 16 : 32 + i * 16, :] = low_wide[:, cols]

    for i in range(F // 16):
        second_norm(i)
    halo2 = edges(gcl, 1)
    for copy in halo2:
        copy.start()

    weight_term(rows_t, act, 0, 512, 0, True, in_z, point_z[0])
    weight_term(rows_p, act, 512, 512, 1, False, in_x, point_x[0])
    weight_term(rows_y, act, 1024, 512, 2, False, in_y, point_y[0])

    points = (point_z, point_x, point_y)
    for part in (0, 1):
        for point in points:
            point[1][part]()

    for copy in halo2:
        copy.wait()
    place_edges(1, gpad)

    def convolve_back(c, carry):
        cols = pl.ds(pl.multiple_of(c * 128, 128), 128)
        total = jnp.zeros((F, 128), F32)
        for t in range(KERN):
            total = total + gpad[c, KERN - t : KERN - t + F, :] * taps_ref[t : t + 1, cols]
        csum[:, cols] = jnp.where(me * F + iota((F, 1), 0) < length, total, 0.0)
        return carry

    lax.fori_loop(0, NB, convolve_back, 0)

    def first_norm_back(i):
        rows = slice(i * 16, (i + 1) * 16)
        x = csum[rows, :]
        n = n1[rows, :]
        vacc[1] += fold(x * n)
        u = x * ng[...]
        grad = r1[rows, :] * (u - mean_of(u) - n * mean_of(u * n))
        gr_ref[rows, :] = (gm[rows, :].astype(F32) + grad).astype(BF)

    for i in range(F // 16):
        first_norm_back(i)
    stores = [pltpu.make_async_copy(gr_ref, gr_hbm, e_sem.at[1])]
    stores[0].start()

    for h in range(3):

        def attended_rows(j, carry, h=h):
            for a in range(2):
                rows = pl.ds(pl.multiple_of(512 * h + (2 * j + a) * 128, 128), 128)
                part = dot_nt(wo[rows, :], gr_ref[...]).astype(BF)
                dsnd[h, 4 * j + 2 * a] = part[:HD]
                dsnd[h, 4 * j + 2 * a + 1] = part[HD:]
            return carry

        lax.fori_loop(0, 2, attended_rows, 0)
        ex_d[h][0]()

    turn(gr_ref)
    weight_term(rows_t, att, 0, 1024, 3, True, in_z, out_one[0])
    point_z[2]()
    point_x[2]()
    point_y[2]()
    out_one[1][0]()
    small = csum

    def tap_rows(c, carry):
        cols = pl.ds(pl.multiple_of(c * 128, 128), 128)
        grad = gc[c]
        for t in range(KERN):
            small[t : t + 1, cols] = jnp.sum(cp[c, t + 1 : t + 1 + F, :] * grad, axis=0, keepdims=True)
        return carry

    lax.fori_loop(0, NB, tap_rows, 0)
    for i in range(3):
        small[KERN + i : KERN + i + 1, :] = jnp.sum(vacc[i], axis=0, keepdims=True)
    small[KERN + 3 :, :] = jnp.zeros((128 - KERN - 3, D), F32)
    for c in range(NB):
        small_t[c * 128 : (c + 1) * 128, :] = small[:, c * 128 : (c + 1) * 128].T.astype(BF)
    weight_term(rows_t, att, 1024, 512, 4, True, in_z, out_two[0])
    out_two[1][0]()
    out_one[1][1]()
    out_two[1][1]()
    point_x[6]()
    point_y[6]()
    for h in range(3):
        ex_q[h][2]()
        ex_v[h][2]()

    for h in range(3):
        ex_d[h][1]()
        row = iota((16, F), 0)
        for j in range(N):
            cols = slice(j * F, (j + 1) * F)
            grad = do[h, j].astype(F32)
            scale = inv[h, :, cols]
            delta = -scale * jnp.sum(grad * obuf[h, j].astype(F32), axis=0, keepdims=True)
            high = delta.astype(BF).astype(F32)
            doaug[:16, cols] = jnp.where(row == 0, high, jnp.where(row == 1, delta - high, 0.0)).astype(BF)
            scaled = (grad * scale).astype(BF)
            doaug[HD:, cols] = scaled
            dz[HD:, cols] = scaled
            qz[:HD, cols] = rcv[h, j, :HD, :]
            kt[:, cols] = rcv[h, j, HD : 2 * HD, :]

        def back_queries(i, carry, h=h):
            i = turned(i)
            cols = pl.ds(pl.multiple_of(i * TILE, TILE), TILE)
            grads = dot(vaug[h], doaug[:, cols])
            grads = (pt[h, :, cols].astype(F32) * grads).astype(BF)
            dst[:, cols] = grads
            rows = (dot(kt[...], grads) * 0.125).astype(BF)
            for a in range(TILE // F):
                sq[h, i * (TILE // F) + a] = rows[:, a * F : (a + 1) * F]
            for a in range(TILE // F):
                ex_g[h][3](i * (TILE // F) + a)
            return carry

        lax.fori_loop(0, S // TILE, back_queries, 0)

        def back_keys(j, carry, h=h):
            j = at(j + 1)
            rows = pl.ds(pl.multiple_of(j * F, F), F)
            both = dot_nt(dst[rows, :], qz[...]) + dot_nt(pt[h, rows, :], dz[...])
            skv[h, j] = both.T.astype(BF)
            ex_k[h][3](j)
            return carry

        lax.fori_loop(0, N, back_keys, 0)
        ex_g[h][4]()
        ex_k[h][4]()
        if h == 0:
            out_one[2]()
            point_z[3]()
        elif h == 1:
            out_two[2]()
            point_x[3]()
            point_y[3]()

    def block_cols(c, carry):
        cols = pl.ds(pl.multiple_of(c * 256, 256), 256)
        bo_ref[:, cols] = (mixed[:, cols] + dot(act[...], wp[:, cols])).astype(BF)
        return carry

    lax.fori_loop(0, D // 256, block_cols, 0)
    stores.append(pltpu.make_async_copy(bo_ref, bo_hbm, e_sem.at[0]))
    stores[-1].start()

    for h in range(3):
        ex_g[h][1]()
        ex_k[h][1]()
        for b in range(4):
            cols = slice((4 * h + b) * 128, (4 * h + b + 1) * 128)
            for ref, source, part in (
                (gq_ref, rq, slice(0, HD)), (gk_ref, rkv, slice(0, HD)), (gv_ref, rkv, slice(HD, 2 * HD))
            ):
                pair = jnp.concatenate([source[h, 2 * b, part], source[h, 2 * b + 1, part]], axis=0)
                ref[:, cols] = pair.T
        cols = pl.ds(512 * h, 512)
        for a, (ref, hbm) in enumerate(((gq_ref, gq_hbm), (gk_ref, gk_hbm), (gv_ref, gv_hbm))):
            stores.append(pltpu.make_async_copy(ref.at[:, cols], hbm.at[:, cols], e_sem.at[2 + 3 * h + a]))
            stores[-1].start()
        if h == 1:
            out_one[3]()
        elif h == 2:
            out_two[3]()

    gp_ref[12:, :] = jnp.zeros((4, D), F32)
    gw_ref[12:, :] = jnp.zeros((4, D + 128), F32)
    unpacked(point_z[4](), gp_ref, 0, 512)
    unpacked(point_x[4](), gp_ref, 512, 512)
    unpacked(point_y[4](), gp_ref, 1024, 512)
    unpacked(out_one[4](), gw_ref, 0, 1024)
    unpacked(out_two[4](), gw_ref, 1024, 512)
    for i, (ref, hbm) in enumerate(((gw_ref, gw_hbm), (gp_ref, gp_hbm))):
        stores.append(pltpu.make_async_copy(ref, hbm, e_sem.at[11 + i]))
        stores[-1].start()
    for reducer in (point_z, point_x, point_y, out_one, out_two):
        reducer[5]()
    for group in (ex_o, ex_d, ex_g, ex_k):
        for h in range(3):
            group[h][2]()
    for store in stores:
        store.wait()


def fused(lengths, q, k, v, res, go, wo, wp, ng, taps, cb, cg):
    hbm = pl.BlockSpec(memory_space=pl.ANY)
    rows = jax.ShapeDtypeStruct((F, D), BF)
    dma = pltpu.SemaphoreType.DMA
    scratch = [
        pltpu.SMEM((1,), jnp.int32),
        pltpu.VMEM((NB, 128), F32),
        pltpu.VMEM((KERN, D), F32),
        pltpu.VMEM((NB, 128), F32),
        pltpu.VMEM((NB, 128), F32),
        pltpu.VMEM((16, D + 128), F32),
        pltpu.VMEM((16, D), F32),
        *[pltpu.VMEM((F, D), BF)] * 10,
        pltpu.VMEM((D, D), BF),
        pltpu.VMEM((D, D), BF),
        pltpu.VMEM((3, N, 3 * HD, F), BF),
        pltpu.VMEM((3, N, 3 * HD, F), BF),
        pltpu.VMEM((S, 128), BF),
        pltpu.VMEM((128, S), BF),
        pltpu.VMEM((HD + 16, S), BF),
        pltpu.VMEM((3, S, 128), BF),
        pltpu.VMEM((3, S, S), BF),
        pltpu.VMEM((3, 1, S), F32),
        pltpu.VMEM((3, N, HD, F), BF),
        pltpu.VMEM((3, N, HD, F), BF),
        pltpu.VMEM((F, D), BF),
        pltpu.VMEM((F, D), F32),
        pltpu.VMEM((F, D), F32),
        pltpu.VMEM((F, 1), F32),
        pltpu.VMEM((F, D), BF),
        pltpu.VMEM((NB, F + 32, 128), F32),
        pltpu.VMEM((F, D), F32),
        pltpu.VMEM((F, D), F32),
        pltpu.VMEM((F, D), BF),
        pltpu.VMEM((F, D), BF),
        pltpu.VMEM((NB, F, 128), F32),
        pltpu.VMEM((F, D), BF),
        pltpu.VMEM((NB, F + 32, 128), F32),
        pltpu.VMEM((3, 8, D), F32),
        pltpu.VMEM((2, 16, D), BF),
        pltpu.VMEM((2, 16, D), BF),
        pltpu.VMEM((3, N, HD, F), BF),
        pltpu.VMEM((3, N, HD, F), BF),
        pltpu.VMEM((128, S), BF),
        pltpu.VMEM((128, S), BF),
        pltpu.VMEM((128, S), BF),
        pltpu.VMEM((HD, S), BF),
        pltpu.VMEM((3, N, HD, F), BF),
        pltpu.VMEM((3, N, 2 * HD, F), BF),
        pltpu.VMEM((1, D), F32),
        pltpu.VMEM((1, D), F32),
        pltpu.VMEM((D, 128), BF),
        pltpu.VMEM((D, F), BF),
        pltpu.VMEM((D, F), BF),
        pltpu.VMEM((D, F), BF),
        *[
            pltpu.VMEM(shape, BF)
            for w, last, by_z in (
                (512, 384, True), (512, 384, False), (512, 384, False), (1024, 768, True), (640, 512, True)
            )
            for shape in (
                (2, 8, 96, w),
                (8, 96, w),
                (2, 96, w),
                (2, 2, 96, w),
                (8, w) if by_z else (4, 48, w),
                (2, N, 16, last) if by_z else (4, 16, last),
                (2, N, 16, last) if by_z else (4, 16, last),
            )
        ],
        pltpu.VMEM((96, 1024), F32),
        pltpu.VMEM((16, 768), F32),
        dma((2,)),
        dma((10,)),
        dma((13,)),
        dma((3, N)), dma((3, N)),
        dma((3, N)), dma((3, N)),
        dma((3, N)), dma((3, N)),
        dma((3, N)), dma((3, N)),
        dma((3, N)), dma((3, N)),
        dma((3, N)), dma((3, N)),
        dma((4,)), dma((4,)),
        dma((5, 30)), dma((5, 30)),
    ]
    return pl.pallas_call(
        kernel,
        out_shape=[rows] * 5
        + [jax.ShapeDtypeStruct((16, D + 128), F32), jax.ShapeDtypeStruct((16, D), F32)],
        in_specs=[hbm] * 12,
        out_specs=[hbm] * 7,
        scratch_shapes=scratch,
        compiler_params=pltpu.CompilerParams(
            collective_id=0, has_side_effects=True, vmem_limit_bytes=62 * 1024 * 1024
        ),
    )(lengths, q, k, v, res, go, wo, wp, ng, taps, cb, cg)


def finish(*refs):
    sources, targets, held, results, sems = refs[:7], refs[7:16], refs[16:23], refs[23:27], refs[27]
    inward = [pltpu.make_async_copy(sources[i], held[i], sems.at[0, i]) for i in range(7)]
    outward = [pltpu.make_async_copy(held[i], targets[i], sems.at[1, i]) for i in range(5)]
    outward += [pltpu.make_async_copy(results[i], targets[5 + i], sems.at[1, 5 + i]) for i in range(4)]
    for copy in inward:
        copy.start()
    for i in range(5):
        inward[i].wait()
        outward[i].start()
    inward[5].wait()
    inward[6].wait()
    gw_ref, gp_ref = held[5:]
    results[0][...] = gw_ref[:12, :D]
    results[1][...] = gp_ref[:12, :]
    results[2][...] = gw_ref[:12, D : D + KERN]
    results[3][...] = gw_ref[:, D:].T[KERN : KERN + 3, :12]
    for copy in outward[5:]:
        copy.start()
    for copy in outward:
        copy.wait()


def finished(rows, gw, gp):
    hbm = pl.BlockSpec(memory_space=pl.ANY)
    shapes = ((12, D), (12, D), (12, KERN), (3, 12))
    return pl.pallas_call(
        finish,
        out_shape=[jax.ShapeDtypeStruct((F, D), BF)] * 5 + [jax.ShapeDtypeStruct(shape, F32) for shape in shapes],
        in_specs=[hbm] * 7,
        out_specs=[hbm] * 9,
        scratch_shapes=[
            *[pltpu.VMEM((F, D), BF)] * 5,
            *[pltpu.VMEM(shape, F32) for shape in ((16, D + 128), (16, D), *shapes)],
            pltpu.SemaphoreType.DMA((2, 9)),
        ],
        compiler_params=pltpu.CompilerParams(vmem_limit_bytes=62 * 1024 * 1024),
    )(*rows, gw, gp)


def local(
    residual_in, query_rows, key_rows, value_rows, lengths, out_weight, norm_gain, conv_kernel,
    conv_bias, conv_gain, point_weight, grad_out,
):
    outs = fused(
        lengths, query_rows[0], key_rows[0], value_rows[0], residual_in[0], grad_out[0],
        out_weight, point_weight, norm_gain.reshape(NB, 128), conv_kernel,
        conv_bias.reshape(NB, 128), conv_gain.reshape(NB, 128),
    )
    outs = finished(outs[:5], *outs[5:])
    return (*[x[None] for x in outs[:5]], *[x.T for x in outs[5:8]], outs[8])


def solution(mesh):
    rows = P("dp", "ctx", None)
    split = P(None, ("dp", "ctx"))
    in_specs = (rows,) * 4 + (P("dp"),) + (P(),) * 6 + (rows,)
    out_specs = (rows,) * 5 + (split,) * 4
    return jax.shard_map(local, mesh=mesh, in_specs=in_specs, out_specs=out_specs, check_vma=False)
```

```python
import jax
import jax.numpy as jnp
from jax import lax
from jax.experimental import pallas as pl
from jax.experimental.pallas import tpu as pltpu
from jax.sharding import PartitionSpec as P

N = 8
F = 128
D = 1536
S = 1024
HD = 64
KERN = 31
NB = D // 128
TILE = 512
EPSILON = 1e-05
MASKED = -1e30
MESH = pl.DeviceIdType.MESH
BF = jnp.bfloat16
F32 = jnp.float32


def dot(a, b):
    return jnp.dot(a, b, preferred_element_type=F32)


def dot_nt(a, b):
    return lax.dot_general(a, b, (((1,), (1,)), ((), ())), preferred_element_type=F32)


def iota(shape, dim):
    return lax.broadcasted_iota(jnp.int32, shape, dim)


def kernel(
    len_hbm, q_hbm, k_hbm, v_hbm, res_hbm, go_hbm, wo_hbm, wp_hbm, ng_hbm, taps_hbm, cb_hbm, cg_hbm,
    bo_hbm, gr_hbm, gq_hbm, gk_hbm, gv_hbm, gw_hbm, gp_hbm,
    len_ref, ng_ref, taps_ref, cb_ref, cg_ref, gw_ref, gp_ref,
    q_ref, k_ref, v_ref, res_ref, go_ref, bo_ref, gr_ref, gq_ref, gk_ref, gv_ref, wo, wp, snd, rcv, kaug, qaug, vta, vaug, pt, inv, obuf, att_t, att, mixed, n1, r1, cin, cp, csum,
    gact, gm, act, gc, gcl, gpad, vacc, lh, rh, dsnd, do, doaug, qz, dz, kt, rq, rkv,
    ng, cg, small_t, rows_t, rows_p, rows_y, *rest,
):
    me = lax.axis_index("ctx")
    dp = lax.axis_index("dp")
    sums, rest = [rest[7 * i : 7 * i + 7] for i in range(5)], rest[35:]
    (
        wide, flat, w_sem, i_sem, e_sem, s_q, r_q, s_v, r_v, s_o, r_o, s_d, r_d, s_g, r_g, s_k, r_k, s_h, r_h, s_r, r_r,
    ) = rest
    dst = wo.at[pl.ds(0, S), pl.ds(0, S)]
    sq, skv = snd.at[:, :, pl.ds(0, HD)], snd.at[:, :, pl.ds(HD, 2 * HD)]
    core = lax.rem(dp, 2)
    y = lax.rem(lax.div(dp, 2), 2)
    z = lax.div(dp, 4)
    def at(offset):
        return lax.rem(me + (offset + N), N)

    x = lax.rem(me, 4)
    y_low = lax.div(me, 4)
    sibling = (dp + 1 - 2 * core, me)

    def in_z(offset):
        return lax.rem(z + (offset + 4), 4)

    def in_x(offset):
        return lax.rem(x + (offset + 4), 4)

    def z_device(offset):
        return (4 * in_z(offset) + 2 * y + core, me)

    def x_device(offset):
        return (dp, 4 * y_low + in_x(offset))

    def in_y(offset):
        return lax.rem(2 * y + y_low + (offset + 4), 4)

    def side_device(offset):
        return (4 * z + 2 * lax.div(in_y(offset), 2) + core, 4 * lax.rem(in_y(offset), 2) + x)

    def y_device(other, offset):
        return (dp + 2 - 4 * y if other else dp, at(offset))

    peers = [sibling] + [z_device(i) for i in (1, 2, 3)]
    peers += [y_device(b, o) for b in range(2) for o in range(N) if b or o]

    barrier = pltpu.get_barrier_semaphore()
    for peer in peers:
        pl.semaphore_signal(barrier, inc=1, device_id=peer, device_id_type=MESH)

    loads = [
        pltpu.make_async_copy(source, target, i_sem.at[i])
        for i, (source, target) in enumerate((
            (q_hbm, q_ref), (k_hbm, k_ref), (v_hbm, v_ref), (go_hbm, go_ref), (res_hbm, res_ref),
            (len_hbm, len_ref), (ng_hbm, ng_ref), (taps_hbm, taps_ref), (cb_hbm, cb_ref), (cg_hbm, cg_ref),
        ))
    ]
    for load in loads:
        load.start()
    wp_copy = pltpu.make_async_copy(wp_hbm, wp, w_sem.at[0])
    wo_copy = pltpu.make_async_copy(wo_hbm, wo, w_sem.at[1])
    wp_copy.start()
    wo_copy.start()

    def exchange(source, target, send_sem, recv_sem, h):
        def copy(o):
            return pltpu.make_async_remote_copy(
                src_ref=source.at[h, at(o)],
                dst_ref=target.at[h, me],
                send_sem=send_sem.at[h, o],
                recv_sem=recv_sem.at[h, o],
                device_id=(dp, at(o)),
                device_id_type=MESH,
            )

        def arrival(o):
            block = target.at[h, at(-o)]
            return pltpu.make_async_remote_copy(
                src_ref=block,
                dst_ref=block,
                send_sem=send_sem.at[h, o],
                recv_sem=recv_sem.at[h, o],
                device_id=(dp, at(-o)),
                device_id_type=MESH,
            )

        def start():
            for o in (4, 3, 5, 2, 6, 1, 7):
                copy(o).start()
            target[h, me] = source[h, me]

        def start_one(j):
            @pl.when(j != me)
            def _():
                o = lax.rem(j - me + N, N)
                pltpu.make_async_remote_copy(
                    src_ref=source.at[h, j],
                    dst_ref=target.at[h, me],
                    send_sem=send_sem.at[h, o],
                    recv_sem=recv_sem.at[h, o],
                    device_id=(dp, j),
                    device_id_type=MESH,
                ).start()

        def keep():
            target[h, me] = source[h, me]

        def wait_one(j):
            @pl.when(j != me)
            def _():
                arrival(lax.rem(me - j + N, N)).wait_recv()

        def wait():
            for o in range(1, N):
                arrival(o).wait_recv()

        def drain():
            for o in range(1, N):
                copy(o).wait_send()

        return start, wait, drain, start_one, keep, wait_one

    ex_q = [exchange(snd.at[:, :, pl.ds(0, HD)], rcv.at[:, :, pl.ds(0, HD)], s_q, r_q, h) for h in range(3)]
    ex_v = [
        exchange(snd.at[:, :, pl.ds(HD, 2 * HD)], rcv.at[:, :, pl.ds(HD, 2 * HD)], s_v, r_v, h) for h in range(3)
    ]
    ex_o = [exchange(obuf, att_t, s_o, r_o, h) for h in range(3)]
    ex_d = [exchange(dsnd, do, s_d, r_d, h) for h in range(3)]
    ex_g = [exchange(sq, rq, s_g, r_g, h) for h in range(3)]
    ex_k = [exchange(skv, rkv, s_k, r_k, h) for h in range(3)]

    def ring(k, along, device):
        term, first, far, near = sums[k][:4]
        here = along(0)

        def to(source, target, i, peer):
            return pltpu.make_async_remote_copy(
                src_ref=source,
                dst_ref=target,
                send_sem=s_r.at[k, i],
                recv_sem=r_r.at[k, i],
                device_id=peer,
                device_id_type=MESH,
            )

        up, down = 2 * along(1), 2 * along(-1)
        opposite = 2 * along(2)
        far_copies = (
            to(term.at[core, opposite], far.at[0], 8, device(1)),
            to(term.at[core, opposite + 1], far.at[1], 9, device(-1)),
        )
        plain_copies = (
            to(term.at[core, up + 1], near.at[0, 1], 10, device(1)),
            to(term.at[core, down], near.at[1, 0], 11, device(-1)),
        )
        joint_copies = (
            to(term.at[core, up], near.at[0, 0], 12, device(1)),
            to(term.at[core, down + 1], near.at[1, 1], 13, device(-1)),
        )

        def cores(i):
            return to(term.at[1 - core, i], first.at[i], i, sibling)

        def begin(blocks, copies):
            for i, copy in zip(blocks, copies):
                cores(i).wait_recv()
                term[core, i] = term[core, i] + first[i]
                if copy is not None:
                    copy.start()

        def start():
            begin((opposite, opposite + 1), far_copies)

        def more():
            blocks = (up + 1, down, up, down + 1, 2 * here, 2 * here + 1)
            begin(blocks, plain_copies + (None,) * 4)

        def join():
            for a, (copy, i) in enumerate(zip(far_copies, (up, down + 1))):
                copy.wait_recv()
                term[core, i] = term[core, i] + far[a]
                joint_copies[a].start()

        def total():
            for copy in plain_copies + joint_copies:
                copy.wait_recv()
            parts = []
            for a in range(2):
                part = term[core, 2 * here + a].astype(F32) + near[0, a].astype(F32)
                parts.append(part + near[1, a].astype(F32))
            return parts

        def drain():
            for i in range(8):
                cores(i).wait_send()
            for copy in far_copies + plain_copies + joint_copies:
                copy.wait_send()

        return to, cores, (start, more), join, total, drain

    def slices(part, split, count, width):
        rows, full = part.shape
        most = 3 * width // 4
        wide[:rows, :full] = part
        for j in range(count):
            flat[:12, :most] = wide[12 * j : 12 * j + 12, :most]
            for g in range(3):
                flat[12:, g * most // 3 : (g + 1) * most // 3] = wide[12 * j + 4 * g : 12 * j + 4 * g + 4, most:width]
            if full > width:
                flat[:12, most : most + full - width] = wide[12 * j : 12 * j + 12, width:full]
            split[j] = flat[:, : most + full - width].astype(BF)

    def unpacked(packed, target, begin, width):
        most = 3 * width // 4
        target[:12, begin : begin + most] = packed[:12, :most]
        for g in range(3):
            block = packed[12:, g * most // 3 : (g + 1) * most // 3]
            target[4 * g : 4 * g + 4, begin + most : begin + width] = block
        rest = packed.shape[1] - most
        if rest:
            target[:12, begin + width : begin + width + rest] = packed[:12, most:]

    def z_reducer(k, width):
        to, cores, start, join, total, drain_ring = ring(k, in_z, z_device)
        split, last = sums[k][5], sums[k][6]
        others = [(b, o) for b in range(2) for o in range(N) if b or o]

        def sent(b, o):
            side = 1 - y if b else y
            return to(split.at[side, at(o)], last.at[y, me], 14 + N * b + o, y_device(b, o))

        def arrival(b, o):
            block = last.at[1 - y if b else y, at(-o)]
            return to(block, block, 14 + N * b + o, y_device(b, -o))

        def spread():
            for a, part in enumerate(total()):
                slices(part, split.at[a], N, width)
            for b, o in others:
                sent(b, o).start()
            last[y, me] = split[y, me]

        def finish():
            for b, o in others:
                arrival(b, o).wait_recv()
            result = jnp.zeros(last.shape[2:], F32)
            for b in range(2):
                for j in range(N):
                    result = result + last[b, j].astype(F32)
            return result

        def drain():
            drain_ring()
            for b, o in others:
                sent(b, o).wait_send()

        return cores, start, join, spread, finish, drain

    def side_reducer(k, width, along, device, across, across_device):
        to, cores, start, join, total, drain_ring = ring(k, along, device)
        here, mine = along(0), across(0)
        term = sums[k][0]
        in_column, split, last = sums[k][4:]

        def column(o):
            c = across(o)
            rows = pl.ds(pl.multiple_of(48 * lax.rem(c, 2), 16), 48)
            block = term.at[core, 2 * here + lax.div(c, 2), rows]
            return to(block, in_column.at[mine], 13 + o, across_device(o))

        def column_arrival(o):
            block = in_column.at[across(-o)]
            return to(block, block, 13 + o, across_device(-o))

        def sent(b):
            return to(split.at[in_z(b)], last.at[z], 16 + b, z_device(b))

        def arrival(b):
            block = last.at[in_z(-b)]
            return to(block, block, 16 + b, z_device(-b))

        def spread_across():
            for a, part in enumerate(total()):
                term[core, 2 * here + a] = part.astype(BF)
            for o in (1, 2, 3):
                column(o).start()

        def spread():
            own = pl.ds(pl.multiple_of(48 * lax.rem(mine, 2), 16), 48)
            part = term[core, 2 * here + lax.div(mine, 2), own, :].astype(F32)
            for o in (1, 2, 3):
                column_arrival(o).wait_recv()
                part = part + in_column[across(-o)].astype(F32)
            slices(part, split, 4, width)
            for b in (1, 2, 3):
                sent(b).start()
            last[z] = split[z]

        def finish():
            for b in (1, 2, 3):
                arrival(b).wait_recv()
            result = last[0].astype(F32)
            for j in (1, 2, 3):
                result = result + last[j].astype(F32)
            return result

        def drain():
            drain_ring()
            for i in (1, 2, 3):
                column(i).wait_send()
                sent(i).wait_send()

        return cores, start, join, spread, finish, drain, spread_across

    point_z = z_reducer(0, 512)
    point_x = side_reducer(1, 512, in_x, x_device, in_y, side_device)
    point_y = side_reducer(2, 512, in_y, side_device, in_x, x_device)
    out_one, out_two = z_reducer(3, 1024), z_reducer(4, 512)

    def weight_term(rows, others, begin, width, k, by_z, along, send):
        term = sums[k][0]

        def block(i, carry):
            i = lax.rem(i + 2 * along(2), 8) if by_z else lax.rem(i + along(2), 4)
            for a in range(2):
                if by_z and a:
                    break
                base = 192 * i if by_z else 192 * i + 768 * a
                left = rows[pl.ds(pl.multiple_of(base, 64), 192), :]
                for n in range(width // 256):
                    cols = slice(n * 256, (n + 1) * 256)
                    part = dot(left, others[:, begin + n * 256 : begin + (n + 1) * 256]).astype(BF)
                    if by_z:
                        term[0, i, :, cols] = part[:96]
                        term[1, i, :, cols] = part[96:]
                    else:
                        term[a, 2 * i, :, cols] = part[:96]
                        term[a, 2 * i + 1, :, cols] = part[96:]
            if term.shape[3] > width:
                for a in range(2):
                    at_rows = pl.ds(pl.multiple_of(i * 192 + a * 96, 32), 96)
                    term[a, i, :, width:] = small_t[at_rows, :]
            if by_z:
                send(i).start()
            else:
                send(2 * i).start()
                send(2 * i + 1).start()
            return carry

        lax.fori_loop(0, 8 if by_z else 4, block, 0)

    def turn(rows):
        for c in range(NB):
            rows_t[c * 128 : (c + 1) * 128, :] = rows[:, c * 128 : (c + 1) * 128].T

    for load in loads[:3]:
        load.wait()
    for h in range(3):
        for b in range(4):
            cols = slice((4 * h + b) * 128, (4 * h + b + 1) * 128)
            for a, ref in enumerate((q_ref, k_ref, v_ref)):
                block = ref[:, cols]
                if a == 0:
                    block = (block.astype(F32) * 0.125).astype(BF)
                block = block.T
                snd[h, 2 * b, a * HD : (a + 1) * HD, :] = block[:HD]
                snd[h, 2 * b + 1, a * HD : (a + 1) * HD, :] = block[HD:]
        if h == 0:
            pl.semaphore_wait(barrier, len(peers))
        ex_v[h][0]()
        ex_q[h][0]()

    for load in loads[5:]:
        load.wait()
    length = len_ref[0]
    for c in range(NB):
        ng[:, c * 128 : (c + 1) * 128] = ng_ref[c : c + 1, :]
        cg[:, c * 128 : (c + 1) * 128] = cg_ref[c : c + 1, :]

    loads[3].wait()
    own_valid = me * F + iota((F, 1), 0) < length
    gm[...] = jnp.where(own_valid, go_ref[...], jnp.zeros_like(go_ref))
    wp_copy.wait()

    def act_grad(c, carry):
        cols = pl.ds(pl.multiple_of(c * 256, 256), 256)
        gact[:, cols] = dot_nt(gm[...], wp[cols, :])
        return carry

    lax.fori_loop(0, D // 256, act_grad, 0)

    turn(gm)

    def ordered(b, carry):
        r = iota((192, 1), 0)
        one, two = lax.div(r, 48), lax.rem(b, 4)
        d = 384 * lax.rem(lax.div(r, 12), 4) + lax.rem(r, 12) + 96 * lax.div(b, 4)
        by_x = 192 * lax.div(one, 2) + 48 * lax.rem(one, 2) + 12 * two
        by_y = 192 * lax.div(two, 2) + 48 * lax.rem(two, 2) + 12 * one
        for ref, more in ((rows_p, by_x), (rows_y, by_y)):
            pick = jnp.where(iota((192, D), 1) == d + more, 1.0, 0.0).astype(BF)
            ref[pl.ds(pl.multiple_of(192 * b, 64), 192), :] = dot_nt(pick, gm[...]).astype(BF)
        return carry

    lax.fori_loop(0, 8, ordered, 0)

    qaug[HD:, :] = (iota((HD, S), 0) == 0).astype(F32).astype(BF)
    vta[HD:, :] = (iota((16, S), 0) == 0).astype(F32).astype(BF)
    qz[HD:, :] = jnp.zeros((HD, S), BF)
    dz[:HD, :] = jnp.zeros((HD, S), BF)
    doaug[16:HD, :] = jnp.zeros((HD - 16, S), BF)

    def turned(i):
        return lax.rem(i + lax.div(me, TILE // F) + 1, S // TILE)

    for h in range(3):
        ex_v[h][1]()
        lane = iota((F, 128), 1)
        for j in range(N):
            cols = slice(j * F, (j + 1) * F)
            vta[:HD, cols] = rcv[h, j, 2 * HD :, :]
            both = rcv[h, j, HD:, :].T
            bias = jnp.where(j * F + iota((F, 128), 0) < length, 0.0, MASKED)
            bias = jnp.where(lane == HD, bias, 0.0).astype(BF)
            ones = jnp.where(lane < 2, 1.0, 0.0).astype(BF)
            kaug[cols, :] = jnp.where(lane < HD, both, bias)
            vaug[h, cols, :] = jnp.where(lane < HD, ones, both)

        def attend(i, carry, h=h):
            i = turned(i)
            cols = pl.ds(pl.multiple_of(i * TILE, TILE), TILE)
            for a in range(TILE // F):
                j = i * (TILE // F) + a
                ex_q[h][5](j)
                qaug[:HD, pl.ds(pl.multiple_of(j * F, F), F)] = rcv[h, j, :HD, :]
            scores = dot(kaug[...], qaug[:, cols])
            top = jnp.max(scores, axis=0, keepdims=True)
            weights = jnp.exp(scores - top).astype(BF)
            pt[h, :, cols] = weights
            summed = dot(vta[...], weights)
            scale = 1.0 / summed[HD : HD + 1, :]
            inv[h, :, cols] = scale
            rows = (summed[:HD] * scale).astype(BF)
            for a in range(TILE // F):
                obuf[h, i * (TILE // F) + a] = rows[:, a * F : (a + 1) * F]
            for a in range(TILE // F):
                ex_o[h][3](i * (TILE // F) + a)
            return carry

        lax.fori_loop(0, S // TILE, attend, 0)
        ex_o[h][4]()

    wo_copy.wait()
    loads[4].wait()
    for h in range(3):
        ex_o[h][1]()
        for b in range(4):
            pair = jnp.concatenate([att_t[h, 2 * b], att_t[h, 2 * b + 1]], axis=0)
            att[:, (4 * h + b) * 128 : (4 * h + b + 1) * 128] = pair.T

        def project(c, carry, h=h):
            cols = pl.ds(pl.multiple_of(c * 256, 256), 256)
            before = res_ref[:, cols].astype(F32) if h == 0 else mixed[:, cols]
            mixed[:, cols] = before + dot(
                att[:, 512 * h : 512 * (h + 1)], wo[512 * h : 512 * (h + 1), cols]
            )
            return carry

        lax.fori_loop(0, D // 256, project, 0)

    def mean_of(x):
        return jnp.sum(x, axis=1, keepdims=True) * (1.0 / D)

    def first_norm(i):
        rows = slice(i * 16, (i + 1) * 16)
        x = mixed[rows, :]
        x = x - mean_of(x)
        r = lax.rsqrt(mean_of(x * x) + EPSILON)
        n = x * r
        n1[rows, :] = n
        r1[rows, :] = r
        valid = me * F + i * 16 + iota((16, 1), 0) < length
        low = jnp.where(valid, n * ng[...], 0.0).astype(BF)
        cin[rows, :] = low
        low_wide = low.astype(F32)
        for c in range(NB):
            cp[c, 16 + i * 16 : 32 + i * 16, :] = low_wide[:, c * 128 : (c + 1) * 128]

    def edges(buffer, k):
        to_right = pltpu.make_async_remote_copy(
            src_ref=buffer.at[pl.ds(F - 16, 16)],
            dst_ref=lh.at[k],
            send_sem=s_h.at[2 * k],
            recv_sem=r_h.at[2 * k],
            device_id=(dp, at(1)),
            device_id_type=MESH,
        )
        to_left = pltpu.make_async_remote_copy(
            src_ref=buffer.at[pl.ds(0, 16)],
            dst_ref=rh.at[k],
            send_sem=s_h.at[2 * k + 1],
            recv_sem=r_h.at[2 * k + 1],
            device_id=(dp, at(-1)),
            device_id_type=MESH,
        )
        return to_right, to_left

    def place_edges(k, padded):
        left = jnp.where(me > 0, lh[k].astype(F32), 0.0)
        right = jnp.where(me < N - 1, rh[k].astype(F32), 0.0)
        for c in range(NB):
            padded[c, 0:16, :] = left[:, c * 128 : (c + 1) * 128]
            padded[c, F + 16 : F + 32, :] = right[:, c * 128 : (c + 1) * 128]

    ends = (0, F // 16 - 1)
    for i in ends:
        first_norm(i)
    halo = edges(cin, 0)
    for copy in halo:
        copy.start()
    for i in range(1, F // 16 - 1):
        first_norm(i)

    def convolve(c, starts, count):
        cols = pl.ds(pl.multiple_of(c * 128, 128), 128)
        totals = [jnp.broadcast_to(cb_ref[pl.ds(c, 1), :], (count, 128))] * len(starts)
        for t in range(KERN):
            tap = taps_ref[t : t + 1, cols]
            totals = [
                total + cp[c, start + t + 1 : start + t + 1 + count, :] * tap
                for total, start in zip(totals, starts)
            ]
        for total, start in zip(totals, starts):
            csum[start : start + count, cols] = total

    def convolve_inside(c, carry):
        convolve(c, (16,), F - 32)
        return carry

    def convolve_ends(c, carry):
        for a in range(2):
            convolve(2 * c + a, (0, F - 16), 16)
        return carry

    lax.fori_loop(0, NB, convolve_inside, 0)
    for copy in halo:
        copy.wait()
    place_edges(0, cp)
    lax.fori_loop(0, NB // 2, convolve_ends, 0)

    vacc[...] = jnp.zeros_like(vacc)

    def fold(x):
        return x[:8] + x[8:]

    def second_norm(i):
        rows = slice(i * 16, (i + 1) * 16)
        x = csum[rows, :]
        x = x - mean_of(x)
        r = lax.rsqrt(mean_of(x * x) + EPSILON)
        n = x * r
        scaled = n * cg[...]
        g = jax.nn.sigmoid(scaled)
        act[rows, :] = (scaled * g).astype(BF)
        back = gact[rows, :] * g * (1.0 + scaled * (1.0 - g))
        vacc[2] += fold(back * n)
        u = back * cg[...]
        grad = r * (u - mean_of(u) - n * mean_of(u * n))
        vacc[0] += fold(grad)
        low = grad.astype(BF)
        gcl[rows, :] = low
        low_wide = low.astype(F32)
        for c in range(NB):
            cols = slice(c * 128, (c + 1) * 128)
            gc[c, rows, :] = grad[:, cols]
            gpad[c, 16 + i * 16 : 32 + i * 16, :] = low_wide[:, cols]

    for i in range(F // 16):
        second_norm(i)
    halo2 = edges(gcl, 1)
    for copy in halo2:
        copy.start()

    weight_term(rows_t, act, 0, 512, 0, True, in_z, point_z[0])
    weight_term(rows_p, act, 512, 512, 1, False, in_x, point_x[0])
    weight_term(rows_y, act, 1024, 512, 2, False, in_y, point_y[0])

    points = (point_z, point_x, point_y)
    for part in (0, 1):
        for point in points:
            point[1][part]()

    for copy in halo2:
        copy.wait()
    place_edges(1, gpad)

    def convolve_back(c, carry):
        cols = pl.ds(pl.multiple_of(c * 128, 128), 128)
        total = jnp.zeros((F, 128), F32)
        for t in range(KERN):
            total = total + gpad[c, KERN - t : KERN - t + F, :] * taps_ref[t : t + 1, cols]
        csum[:, cols] = jnp.where(me * F + iota((F, 1), 0) < length, total, 0.0)
        return carry

    lax.fori_loop(0, NB, convolve_back, 0)

    def first_norm_back(i):
        rows = slice(i * 16, (i + 1) * 16)
        x = csum[rows, :]
        n = n1[rows, :]
        vacc[1] += fold(x * n)
        u = x * ng[...]
        grad = r1[rows, :] * (u - mean_of(u) - n * mean_of(u * n))
        gr_ref[rows, :] = (gm[rows, :].astype(F32) + grad).astype(BF)

    for i in range(F // 16):
        first_norm_back(i)
    stores = [pltpu.make_async_copy(gr_ref, gr_hbm, e_sem.at[1])]
    stores[0].start()

    for h in range(3):

        def attended_rows(j, carry, h=h):
            for a in range(2):
                rows = pl.ds(pl.multiple_of(512 * h + (2 * j + a) * 128, 128), 128)
                part = dot_nt(wo[rows, :], gr_ref[...]).astype(BF)
                dsnd[h, 4 * j + 2 * a] = part[:HD]
                dsnd[h, 4 * j + 2 * a + 1] = part[HD:]
            return carry

        lax.fori_loop(0, 2, attended_rows, 0)
        ex_d[h][0]()

    point_z[2]()
    point_x[2]()
    point_y[2]()
    turn(gr_ref)
    weight_term(rows_t, att, 0, 1024, 3, True, in_z, out_one[0])
    out_one[1][0]()
    small = csum

    def tap_rows(c, carry):
        cols = pl.ds(pl.multiple_of(c * 128, 128), 128)
        grad = gc[c]
        for t in range(KERN):
            small[t : t + 1, cols] = jnp.sum(cp[c, t + 1 : t + 1 + F, :] * grad, axis=0, keepdims=True)
        return carry

    lax.fori_loop(0, NB, tap_rows, 0)
    for i in range(3):
        small[KERN + i : KERN + i + 1, :] = jnp.sum(vacc[i], axis=0, keepdims=True)
    small[KERN + 3 :, :] = jnp.zeros((128 - KERN - 3, D), F32)
    for c in range(NB):
        small_t[c * 128 : (c + 1) * 128, :] = small[:, c * 128 : (c + 1) * 128].T.astype(BF)
    weight_term(rows_t, att, 1024, 512, 4, True, in_z, out_two[0])
    out_two[1][0]()
    out_one[1][1]()
    out_two[1][1]()
    point_x[6]()
    point_y[6]()
    for h in range(3):
        ex_q[h][2]()
        ex_v[h][2]()

    for h in range(3):
        ex_d[h][1]()
        row = iota((16, F), 0)
        for j in range(N):
            cols = slice(j * F, (j + 1) * F)
            grad = do[h, j].astype(F32)
            scale = inv[h, :, cols]
            delta = -scale * jnp.sum(grad * obuf[h, j].astype(F32), axis=0, keepdims=True)
            high = delta.astype(BF).astype(F32)
            doaug[:16, cols] = jnp.where(row == 0, high, jnp.where(row == 1, delta - high, 0.0)).astype(BF)
            scaled = (grad * scale).astype(BF)
            doaug[HD:, cols] = scaled
            dz[HD:, cols] = scaled
            qz[:HD, cols] = rcv[h, j, :HD, :]
            kt[:, cols] = rcv[h, j, HD : 2 * HD, :]

        def back_queries(i, carry, h=h):
            i = turned(i)
            cols = pl.ds(pl.multiple_of(i * TILE, TILE), TILE)
            grads = dot(vaug[h], doaug[:, cols])
            grads = (pt[h, :, cols].astype(F32) * grads).astype(BF)
            dst[:, cols] = grads
            rows = (dot(kt[...], grads) * 0.125).astype(BF)
            for a in range(TILE // F):
                sq[h, i * (TILE // F) + a] = rows[:, a * F : (a + 1) * F]
            for a in range(TILE // F):
                ex_g[h][3](i * (TILE // F) + a)
            return carry

        lax.fori_loop(0, S // TILE, back_queries, 0)

        def back_keys(j, carry, h=h):
            j = lax.rem(j + lax.div(me, 2) + 1, 4)
            rows = pl.ds(pl.multiple_of(j * 2 * F, 2 * F), 2 * F)
            both = dot_nt(dst[rows, :], qz[...]) + dot_nt(pt[h, rows, :], dz[...])
            for a in range(2):
                skv[h, 2 * j + a] = both[a * F : (a + 1) * F].T.astype(BF)
                ex_k[h][3](2 * j + a)
            return carry

        lax.fori_loop(0, N // 2, back_keys, 0)
        ex_g[h][4]()
        ex_k[h][4]()
        if h == 0:
            out_one[2]()
            point_z[3]()
        elif h == 1:
            out_two[2]()
            point_x[3]()
            point_y[3]()

    def block_cols(c, carry):
        cols = pl.ds(pl.multiple_of(c * 256, 256), 256)
        bo_ref[:, cols] = (mixed[:, cols] + dot(act[...], wp[:, cols])).astype(BF)
        return carry

    lax.fori_loop(0, D // 256, block_cols, 0)
    stores.append(pltpu.make_async_copy(bo_ref, bo_hbm, e_sem.at[0]))
    stores[-1].start()

    for h in range(3):
        ex_g[h][1]()
        ex_k[h][1]()
        for b in range(4):
            cols = slice((4 * h + b) * 128, (4 * h + b + 1) * 128)
            for ref, source, part in (
                (gq_ref, rq, slice(0, HD)), (gk_ref, rkv, slice(0, HD)), (gv_ref, rkv, slice(HD, 2 * HD))
            ):
                pair = jnp.concatenate([source[h, 2 * b, part], source[h, 2 * b + 1, part]], axis=0)
                ref[:, cols] = pair.T
        cols = pl.ds(512 * h, 512)
        for a, (ref, hbm) in enumerate(((gq_ref, gq_hbm), (gk_ref, gk_hbm), (gv_ref, gv_hbm))):
            stores.append(pltpu.make_async_copy(ref.at[:, cols], hbm.at[:, cols], e_sem.at[2 + 3 * h + a]))
            stores[-1].start()
        if h == 1:
            out_one[3]()
        elif h == 2:
            out_two[3]()

    gp_ref[12:, :] = jnp.zeros((4, D), F32)
    gw_ref[12:, :] = jnp.zeros((4, D + 128), F32)
    unpacked(point_z[4](), gp_ref, 0, 512)
    unpacked(point_x[4](), gp_ref, 512, 512)
    unpacked(point_y[4](), gp_ref, 1024, 512)
    unpacked(out_one[4](), gw_ref, 0, 1024)
    unpacked(out_two[4](), gw_ref, 1024, 512)
    for i, (ref, hbm) in enumerate(((gw_ref, gw_hbm), (gp_ref, gp_hbm))):
        stores.append(pltpu.make_async_copy(ref, hbm, e_sem.at[11 + i]))
        stores[-1].start()
    for reducer in (point_z, point_x, point_y, out_one, out_two):
        reducer[5]()
    for group in (ex_o, ex_d, ex_g, ex_k):
        for h in range(3):
            group[h][2]()
    for store in stores:
        store.wait()


def fused(lengths, q, k, v, res, go, wo, wp, ng, taps, cb, cg):
    hbm = pl.BlockSpec(memory_space=pl.ANY)
    rows = jax.ShapeDtypeStruct((F, D), BF)
    dma = pltpu.SemaphoreType.DMA
    scratch = [
        pltpu.SMEM((1,), jnp.int32),
        pltpu.VMEM((NB, 128), F32),
        pltpu.VMEM((KERN, D), F32),
        pltpu.VMEM((NB, 128), F32),
        pltpu.VMEM((NB, 128), F32),
        pltpu.VMEM((16, D + 128), F32),
        pltpu.VMEM((16, D), F32),
        *[pltpu.VMEM((F, D), BF)] * 10,
        pltpu.VMEM((D, D), BF),
        pltpu.VMEM((D, D), BF),
        pltpu.VMEM((3, N, 3 * HD, F), BF),
        pltpu.VMEM((3, N, 3 * HD, F), BF),
        pltpu.VMEM((S, 128), BF),
        pltpu.VMEM((128, S), BF),
        pltpu.VMEM((HD + 16, S), BF),
        pltpu.VMEM((3, S, 128), BF),
        pltpu.VMEM((3, S, S), BF),
        pltpu.VMEM((3, 1, S), F32),
        pltpu.VMEM((3, N, HD, F), BF),
        pltpu.VMEM((3, N, HD, F), BF),
        pltpu.VMEM((F, D), BF),
        pltpu.VMEM((F, D), F32),
        pltpu.VMEM((F, D), F32),
        pltpu.VMEM((F, 1), F32),
        pltpu.VMEM((F, D), BF),
        pltpu.VMEM((NB, F + 32, 128), F32),
        pltpu.VMEM((F, D), F32),
        pltpu.VMEM((F, D), F32),
        pltpu.VMEM((F, D), BF),
        pltpu.VMEM((F, D), BF),
        pltpu.VMEM((NB, F, 128), F32),
        pltpu.VMEM((F, D), BF),
        pltpu.VMEM((NB, F + 32, 128), F32),
        pltpu.VMEM((3, 8, D), F32),
        pltpu.VMEM((2, 16, D), BF),
        pltpu.VMEM((2, 16, D), BF),
        pltpu.VMEM((3, N, HD, F), BF),
        pltpu.VMEM((3, N, HD, F), BF),
        pltpu.VMEM((128, S), BF),
        pltpu.VMEM((128, S), BF),
        pltpu.VMEM((128, S), BF),
        pltpu.VMEM((HD, S), BF),
        pltpu.VMEM((3, N, HD, F), BF),
        pltpu.VMEM((3, N, 2 * HD, F), BF),
        pltpu.VMEM((1, D), F32),
        pltpu.VMEM((1, D), F32),
        pltpu.VMEM((D, 128), BF),
        pltpu.VMEM((D, F), BF),
        pltpu.VMEM((D, F), BF),
        pltpu.VMEM((D, F), BF),
        *[
            pltpu.VMEM(shape, BF)
            for w, last, by_z in (
                (512, 384, True), (512, 384, False), (512, 384, False), (1024, 768, True), (640, 512, True)
            )
            for shape in (
                (2, 8, 96, w),
                (8, 96, w),
                (2, 96, w),
                (2, 2, 96, w),
                (8, w) if by_z else (4, 48, w),
                (2, N, 16, last) if by_z else (4, 16, last),
                (2, N, 16, last) if by_z else (4, 16, last),
            )
        ],
        pltpu.VMEM((96, 1024), F32),
        pltpu.VMEM((16, 768), F32),
        dma((2,)),
        dma((10,)),
        dma((13,)),
        dma((3, N)), dma((3, N)),
        dma((3, N)), dma((3, N)),
        dma((3, N)), dma((3, N)),
        dma((3, N)), dma((3, N)),
        dma((3, N)), dma((3, N)),
        dma((3, N)), dma((3, N)),
        dma((4,)), dma((4,)),
        dma((5, 30)), dma((5, 30)),
    ]
    return pl.pallas_call(
        kernel,
        out_shape=[rows] * 5
        + [jax.ShapeDtypeStruct((16, D + 128), F32), jax.ShapeDtypeStruct((16, D), F32)],
        in_specs=[hbm] * 12,
        out_specs=[hbm] * 7,
        scratch_shapes=scratch,
        compiler_params=pltpu.CompilerParams(
            collective_id=0, has_side_effects=True, vmem_limit_bytes=62 * 1024 * 1024
        ),
    )(lengths, q, k, v, res, go, wo, wp, ng, taps, cb, cg)


def finish(*refs):
    sources, targets, held, results, sems = refs[:7], refs[7:16], refs[16:23], refs[23:27], refs[27]
    inward = [pltpu.make_async_copy(sources[i], held[i], sems.at[0, i]) for i in range(7)]
    outward = [pltpu.make_async_copy(held[i], targets[i], sems.at[1, i]) for i in range(5)]
    outward += [pltpu.make_async_copy(results[i], targets[5 + i], sems.at[1, 5 + i]) for i in range(4)]
    for copy in inward:
        copy.start()
    for i in range(5):
        inward[i].wait()
        outward[i].start()
    inward[5].wait()
    inward[6].wait()
    gw_ref, gp_ref = held[5:]
    results[0][...] = gw_ref[:12, :D]
    results[1][...] = gp_ref[:12, :]
    results[2][...] = gw_ref[:12, D : D + KERN]
    results[3][...] = gw_ref[:, D:].T[KERN : KERN + 3, :12]
    for copy in outward[5:]:
        copy.start()
    for copy in outward:
        copy.wait()


def finished(rows, gw, gp):
    hbm = pl.BlockSpec(memory_space=pl.ANY)
    shapes = ((12, D), (12, D), (12, KERN), (3, 12))
    return pl.pallas_call(
        finish,
        out_shape=[jax.ShapeDtypeStruct((F, D), BF)] * 5 + [jax.ShapeDtypeStruct(shape, F32) for shape in shapes],
        in_specs=[hbm] * 7,
        out_specs=[hbm] * 9,
        scratch_shapes=[
            *[pltpu.VMEM((F, D), BF)] * 5,
            *[pltpu.VMEM(shape, F32) for shape in ((16, D + 128), (16, D), *shapes)],
            pltpu.SemaphoreType.DMA((2, 9)),
        ],
        compiler_params=pltpu.CompilerParams(vmem_limit_bytes=62 * 1024 * 1024),
    )(*rows, gw, gp)


def local(
    residual_in, query_rows, key_rows, value_rows, lengths, out_weight, norm_gain, conv_kernel,
    conv_bias, conv_gain, point_weight, grad_out,
):
    outs = fused(
        lengths, query_rows[0], key_rows[0], value_rows[0], residual_in[0], grad_out[0],
        out_weight, point_weight, norm_gain.reshape(NB, 128), conv_kernel,
        conv_bias.reshape(NB, 128), conv_gain.reshape(NB, 128),
    )
    outs = finished(outs[:5], *outs[5:])
    return (*[x[None] for x in outs[:5]], *[x.T for x in outs[5:8]], outs[8])


def solution(mesh):
    rows = P("dp", "ctx", None)
    split = P(None, ("dp", "ctx"))
    in_specs = (rows,) * 4 + (P("dp"),) + (P(),) * 6 + (rows,)
    out_specs = (rows,) * 5 + (split,) * 4
    return jax.shard_map(local, mesh=mesh, in_specs=in_specs, out_specs=out_specs, check_vma=False)
```

```python
import jax
import jax.numpy as jnp
from jax import lax
from jax.experimental import pallas as pl
from jax.experimental.pallas import tpu as pltpu
from jax.sharding import PartitionSpec as P

N = 8
F = 128
D = 1536
S = 1024
HD = 64
KERN = 31
NB = D // 128
TILE = 512
EPSILON = 1e-05
MASKED = -1e30
MESH = pl.DeviceIdType.MESH
BF = jnp.bfloat16
F32 = jnp.float32


def dot(a, b):
    return jnp.dot(a, b, preferred_element_type=F32)


def dot_nt(a, b):
    return lax.dot_general(a, b, (((1,), (1,)), ((), ())), preferred_element_type=F32)


def iota(shape, dim):
    return lax.broadcasted_iota(jnp.int32, shape, dim)


def kernel(
    len_hbm, q_hbm, k_hbm, v_hbm, res_hbm, go_hbm, wo_hbm, wp_hbm, ng_hbm, taps_hbm, cb_hbm, cg_hbm,
    bo_hbm, gr_hbm, gq_hbm, gk_hbm, gv_hbm, gw_hbm, gp_hbm,
    len_ref, ng_ref, taps_ref, cb_ref, cg_ref, gw_ref, gp_ref,
    q_ref, k_ref, v_ref, res_ref, go_ref, bo_ref, gr_ref, gq_ref, gk_ref, gv_ref, wo, wp, snd, rcv, kaug, qaug, vta, vaug, pt, inv, obuf, att_t, att, mixed, n1, r1, cin, cp, csum,
    gact, gm, act, gc, gcl, gpad, vacc, lh, rh, dsnd, do, doaug, qz, dz, kt, rq, rkv,
    ng, cg, small_t, rows_t, rows_p, rows_y, *rest,
):
    me = lax.axis_index("ctx")
    dp = lax.axis_index("dp")
    sums, rest = [rest[7 * i : 7 * i + 7] for i in range(5)], rest[35:]
    (
        wide, flat, w_sem, i_sem, e_sem, s_q, r_q, s_v, r_v, s_o, r_o, s_d, r_d, s_g, r_g, s_k, r_k, s_h, r_h, s_r, r_r,
    ) = rest
    dst = wo.at[pl.ds(0, S), pl.ds(0, S)]
    sq, skv = snd.at[:, :, pl.ds(0, HD)], snd.at[:, :, pl.ds(HD, 2 * HD)]
    core = lax.rem(dp, 2)
    y = lax.rem(lax.div(dp, 2), 2)
    z = lax.div(dp, 4)
    def at(offset):
        return lax.rem(me + (offset + N), N)

    x = lax.rem(me, 4)
    y_low = lax.div(me, 4)
    sibling = (dp + 1 - 2 * core, me)

    def in_z(offset):
        return lax.rem(z + (offset + 4), 4)

    def in_x(offset):
        return lax.rem(x + (offset + 4), 4)

    def z_device(offset):
        return (4 * in_z(offset) + 2 * y + core, me)

    def x_device(offset):
        return (dp, 4 * y_low + in_x(offset))

    def in_y(offset):
        return lax.rem(2 * y + y_low + (offset + 4), 4)

    def side_device(offset):
        return (4 * z + 2 * lax.div(in_y(offset), 2) + core, 4 * lax.rem(in_y(offset), 2) + x)

    def y_device(other, offset):
        return (dp + 2 - 4 * y if other else dp, at(offset))

    peers = [sibling] + [z_device(i) for i in (1, 2, 3)]
    peers += [y_device(b, o) for b in range(2) for o in range(N) if b or o]

    barrier = pltpu.get_barrier_semaphore()
    for peer in peers:
        pl.semaphore_signal(barrier, inc=1, device_id=peer, device_id_type=MESH)

    loads = [
        pltpu.make_async_copy(source, target, i_sem.at[i])
        for i, (source, target) in enumerate((
            (q_hbm, q_ref), (k_hbm, k_ref), (v_hbm, v_ref), (go_hbm, go_ref), (res_hbm, res_ref),
            (len_hbm, len_ref), (ng_hbm, ng_ref), (taps_hbm, taps_ref), (cb_hbm, cb_ref), (cg_hbm, cg_ref),
        ))
    ]
    for load in loads:
        load.start()
    wp_copy = pltpu.make_async_copy(wp_hbm, wp, w_sem.at[0])
    wo_copy = pltpu.make_async_copy(wo_hbm, wo, w_sem.at[1])
    wp_copy.start()
    wo_copy.start()

    def exchange(source, target, send_sem, recv_sem, h):
        def copy(o):
            return pltpu.make_async_remote_copy(
                src_ref=source.at[h, at(o)],
                dst_ref=target.at[h, me],
                send_sem=send_sem.at[h, o],
                recv_sem=recv_sem.at[h, o],
                device_id=(dp, at(o)),
                device_id_type=MESH,
            )

        def arrival(o):
            block = target.at[h, at(-o)]
            return pltpu.make_async_remote_copy(
                src_ref=block,
                dst_ref=block,
                send_sem=send_sem.at[h, o],
                recv_sem=recv_sem.at[h, o],
                device_id=(dp, at(-o)),
                device_id_type=MESH,
            )

        def start():
            for o in (4, 3, 5, 2, 6, 1, 7):
                copy(o).start()
            target[h, me] = source[h, me]

        def start_one(j):
            @pl.when(j != me)
            def _():
                o = lax.rem(j - me + N, N)
                pltpu.make_async_remote_copy(
                    src_ref=source.at[h, j],
                    dst_ref=target.at[h, me],
                    send_sem=send_sem.at[h, o],
                    recv_sem=recv_sem.at[h, o],
                    device_id=(dp, j),
                    device_id_type=MESH,
                ).start()

        def keep():
            target[h, me] = source[h, me]

        def wait_one(j):
            @pl.when(j != me)
            def _():
                arrival(lax.rem(me - j + N, N)).wait_recv()

        def wait():
            for o in range(1, N):
                arrival(o).wait_recv()

        def drain():
            for o in range(1, N):
                copy(o).wait_send()

        return start, wait, drain, start_one, keep, wait_one

    ex_q = [exchange(snd.at[:, :, pl.ds(0, HD)], rcv.at[:, :, pl.ds(0, HD)], s_q, r_q, h) for h in range(3)]
    ex_v = [
        exchange(snd.at[:, :, pl.ds(HD, 2 * HD)], rcv.at[:, :, pl.ds(HD, 2 * HD)], s_v, r_v, h) for h in range(3)
    ]
    ex_o = [exchange(obuf, att_t, s_o, r_o, h) for h in range(3)]
    ex_d = [exchange(dsnd, do, s_d, r_d, h) for h in range(3)]
    ex_g = [exchange(sq, rq, s_g, r_g, h) for h in range(3)]
    ex_k = [exchange(skv, rkv, s_k, r_k, h) for h in range(3)]

    def ring(k, along, device):
        term, first, far, near = sums[k][:4]
        here = along(0)

        def to(source, target, i, peer):
            return pltpu.make_async_remote_copy(
                src_ref=source,
                dst_ref=target,
                send_sem=s_r.at[k, i],
                recv_sem=r_r.at[k, i],
                device_id=peer,
                device_id_type=MESH,
            )

        up, down = 2 * along(1), 2 * along(-1)
        opposite = 2 * along(2)
        far_copies = (
            to(term.at[core, opposite], far.at[0], 8, device(1)),
            to(term.at[core, opposite + 1], far.at[1], 9, device(-1)),
        )
        plain_copies = (
            to(term.at[core, up + 1], near.at[0, 1], 10, device(1)),
            to(term.at[core, down], near.at[1, 0], 11, device(-1)),
        )
        joint_copies = (
            to(term.at[core, up], near.at[0, 0], 12, device(1)),
            to(term.at[core, down + 1], near.at[1, 1], 13, device(-1)),
        )

        def cores(i):
            return to(term.at[1 - core, i], first.at[i], i, sibling)

        def begin(blocks, copies):
            for i, copy in zip(blocks, copies):
                cores(i).wait_recv()
                term[core, i] = term[core, i] + first[i]
                if copy is not None:
                    copy.start()

        def start():
            begin((opposite, opposite + 1), far_copies)

        def more():
            blocks = (up + 1, down, up, down + 1, 2 * here, 2 * here + 1)
            begin(blocks, plain_copies + (None,) * 4)

        def join():
            for a, (copy, i) in enumerate(zip(far_copies, (up, down + 1))):
                copy.wait_recv()
                term[core, i] = term[core, i] + far[a]
                joint_copies[a].start()

        def total():
            for copy in plain_copies + joint_copies:
                copy.wait_recv()
            parts = []
            for a in range(2):
                part = term[core, 2 * here + a].astype(F32) + near[0, a].astype(F32)
                parts.append(part + near[1, a].astype(F32))
            return parts

        def drain():
            for i in range(8):
                cores(i).wait_send()
            for copy in far_copies + plain_copies + joint_copies:
                copy.wait_send()

        return to, cores, (start, more), join, total, drain

    def slices(part, split, count, width):
        rows, full = part.shape
        most = 3 * width // 4
        wide[:rows, :full] = part
        for j in range(count):
            flat[:12, :most] = wide[12 * j : 12 * j + 12, :most]
            for g in range(3):
                flat[12:, g * most // 3 : (g + 1) * most // 3] = wide[12 * j + 4 * g : 12 * j + 4 * g + 4, most:width]
            if full > width:
                flat[:12, most : most + full - width] = wide[12 * j : 12 * j + 12, width:full]
            split[j] = flat[:, : most + full - width].astype(BF)

    def unpacked(packed, target, begin, width):
        most = 3 * width // 4
        target[:12, begin : begin + most] = packed[:12, :most]
        for g in range(3):
            block = packed[12:, g * most // 3 : (g + 1) * most // 3]
            target[4 * g : 4 * g + 4, begin + most : begin + width] = block
        rest = packed.shape[1] - most
        if rest:
            target[:12, begin + width : begin + width + rest] = packed[:12, most:]

    def z_reducer(k, width):
        to, cores, start, join, total, drain_ring = ring(k, in_z, z_device)
        split, last = sums[k][5], sums[k][6]
        others = [(b, o) for b in range(2) for o in range(N) if b or o]

        def sent(b, o):
            side = 1 - y if b else y
            return to(split.at[side, at(o)], last.at[y, me], 14 + N * b + o, y_device(b, o))

        def arrival(b, o):
            block = last.at[1 - y if b else y, at(-o)]
            return to(block, block, 14 + N * b + o, y_device(b, -o))

        def spread():
            for a, part in enumerate(total()):
                slices(part, split.at[a], N, width)
            for b, o in others:
                sent(b, o).start()
            last[y, me] = split[y, me]

        def finish():
            for b, o in others:
                arrival(b, o).wait_recv()
            result = jnp.zeros(last.shape[2:], F32)
            for b in range(2):
                for j in range(N):
                    result = result + last[b, j].astype(F32)
            return result

        def drain():
            drain_ring()
            for b, o in others:
                sent(b, o).wait_send()

        return cores, start, join, spread, finish, drain

    def side_reducer(k, width, along, device, across, across_device):
        to, cores, start, join, total, drain_ring = ring(k, along, device)
        here, mine = along(0), across(0)
        term = sums[k][0]
        in_column, split, last = sums[k][4:]

        def column(o):
            c = across(o)
            rows = pl.ds(pl.multiple_of(48 * lax.rem(c, 2), 16), 48)
            block = term.at[core, 2 * here + lax.div(c, 2), rows]
            return to(block, in_column.at[mine], 13 + o, across_device(o))

        def column_arrival(o):
            block = in_column.at[across(-o)]
            return to(block, block, 13 + o, across_device(-o))

        def sent(b):
            return to(split.at[in_z(b)], last.at[z], 16 + b, z_device(b))

        def arrival(b):
            block = last.at[in_z(-b)]
            return to(block, block, 16 + b, z_device(-b))

        def spread_across():
            for a, part in enumerate(total()):
                term[core, 2 * here + a] = part.astype(BF)
            for o in (1, 2, 3):
                column(o).start()

        def spread():
            own = pl.ds(pl.multiple_of(48 * lax.rem(mine, 2), 16), 48)
            part = term[core, 2 * here + lax.div(mine, 2), own, :].astype(F32)
            for o in (1, 2, 3):
                column_arrival(o).wait_recv()
                part = part + in_column[across(-o)].astype(F32)
            slices(part, split, 4, width)
            for b in (1, 2, 3):
                sent(b).start()
            last[z] = split[z]

        def finish():
            for b in (1, 2, 3):
                arrival(b).wait_recv()
            result = last[0].astype(F32)
            for j in (1, 2, 3):
                result = result + last[j].astype(F32)
            return result

        def drain():
            drain_ring()
            for i in (1, 2, 3):
                column(i).wait_send()
                sent(i).wait_send()

        return cores, start, join, spread, finish, drain, spread_across

    point_z = z_reducer(0, 512)
    point_x = side_reducer(1, 512, in_x, x_device, in_y, side_device)
    point_y = side_reducer(2, 512, in_y, side_device, in_x, x_device)
    out_one, out_two = z_reducer(3, 1024), z_reducer(4, 512)

    def weight_term(rows, others, begin, width, k, by_z, along, send):
        term = sums[k][0]

        def block(i, carry):
            i = lax.rem(i + 2 * along(2), 8) if by_z else lax.rem(i + along(2), 4)
            for a in range(2):
                if by_z and a:
                    break
                base = 192 * i if by_z else 192 * i + 768 * a
                left = rows[pl.ds(pl.multiple_of(base, 64), 192), :]
                for n in range(width // 256):
                    cols = slice(n * 256, (n + 1) * 256)
                    part = dot(left, others[:, begin + n * 256 : begin + (n + 1) * 256]).astype(BF)
                    if by_z:
                        term[0, i, :, cols] = part[:96]
                        term[1, i, :, cols] = part[96:]
                    else:
                        term[a, 2 * i, :, cols] = part[:96]
                        term[a, 2 * i + 1, :, cols] = part[96:]
            if term.shape[3] > width:
                for a in range(2):
                    at_rows = pl.ds(pl.multiple_of(i * 192 + a * 96, 32), 96)
                    term[a, i, :, width:] = small_t[at_rows, :]
            if by_z:
                send(i).start()
            else:
                send(2 * i).start()
                send(2 * i + 1).start()
            return carry

        lax.fori_loop(0, 8 if by_z else 4, block, 0)

    def turn(rows):
        for c in range(NB):
            rows_t[c * 128 : (c + 1) * 128, :] = rows[:, c * 128 : (c + 1) * 128].T

    for load in loads[:3]:
        load.wait()
    for h in range(3):
        for b in range(4):
            cols = slice((4 * h + b) * 128, (4 * h + b + 1) * 128)
            for a, ref in enumerate((q_ref, k_ref, v_ref)):
                block = ref[:, cols]
                if a == 0:
                    block = (block.astype(F32) * 0.125).astype(BF)
                block = block.T
                snd[h, 2 * b, a * HD : (a + 1) * HD, :] = block[:HD]
                snd[h, 2 * b + 1, a * HD : (a + 1) * HD, :] = block[HD:]
        if h == 0:
            pl.semaphore_wait(barrier, len(peers))
        ex_v[h][0]()
        ex_q[h][0]()

    for load in loads[5:]:
        load.wait()
    length = len_ref[0]
    for c in range(NB):
        ng[:, c * 128 : (c + 1) * 128] = ng_ref[c : c + 1, :]
        cg[:, c * 128 : (c + 1) * 128] = cg_ref[c : c + 1, :]

    loads[3].wait()
    own_valid = me * F + iota((F, 1), 0) < length
    gm[...] = jnp.where(own_valid, go_ref[...], jnp.zeros_like(go_ref))
    wp_copy.wait()

    def act_grad(c, carry):
        cols = pl.ds(pl.multiple_of(c * 256, 256), 256)
        gact[:, cols] = dot_nt(gm[...], wp[cols, :])
        return carry

    lax.fori_loop(0, D // 256, act_grad, 0)

    turn(gm)

    def ordered(b, carry):
        r = iota((192, 1), 0)
        one, two = lax.div(r, 48), lax.rem(b, 4)
        d = 384 * lax.rem(lax.div(r, 12), 4) + lax.rem(r, 12) + 96 * lax.div(b, 4)
        by_x = 192 * lax.div(one, 2) + 48 * lax.rem(one, 2) + 12 * two
        by_y = 192 * lax.div(two, 2) + 48 * lax.rem(two, 2) + 12 * one
        for ref, more in ((rows_p, by_x), (rows_y, by_y)):
            pick = jnp.where(iota((192, D), 1) == d + more, 1.0, 0.0).astype(BF)
            ref[pl.ds(pl.multiple_of(192 * b, 64), 192), :] = dot_nt(pick, gm[...]).astype(BF)
        return carry

    lax.fori_loop(0, 8, ordered, 0)

    qaug[HD:, :] = (iota((HD, S), 0) == 0).astype(F32).astype(BF)
    vta[HD:, :] = (iota((16, S), 0) == 0).astype(F32).astype(BF)
    qz[HD:, :] = jnp.zeros((HD, S), BF)
    dz[:HD, :] = jnp.zeros((HD, S), BF)
    doaug[16:HD, :] = jnp.zeros((HD - 16, S), BF)

    def turned(i):
        return lax.rem(i + lax.div(me, TILE // F) + 1, S // TILE)

    for h in range(3):
        ex_v[h][1]()
        lane = iota((F, 128), 1)
        for j in range(N):
            cols = slice(j * F, (j + 1) * F)
            vta[:HD, cols] = rcv[h, j, 2 * HD :, :]
            both = rcv[h, j, HD:, :].T
            bias = jnp.where(j * F + iota((F, 128), 0) < length, 0.0, MASKED)
            bias = jnp.where(lane == HD, bias, 0.0).astype(BF)
            ones = jnp.where(lane < 2, 1.0, 0.0).astype(BF)
            kaug[cols, :] = jnp.where(lane < HD, both, bias)
            vaug[h, cols, :] = jnp.where(lane < HD, ones, both)

        def attend(i, carry, h=h):
            i = turned(i)
            cols = pl.ds(pl.multiple_of(i * TILE, TILE), TILE)
            for a in range(TILE // F):
                j = i * (TILE // F) + a
                ex_q[h][5](j)
                qaug[:HD, pl.ds(pl.multiple_of(j * F, F), F)] = rcv[h, j, :HD, :]
            scores = dot(kaug[...], qaug[:, cols])
            top = jnp.max(scores, axis=0, keepdims=True)
            weights = jnp.exp(scores - top).astype(BF)
            pt[h, :, cols] = weights
            summed = dot(vta[...], weights)
            scale = 1.0 / summed[HD : HD + 1, :]
            inv[h, :, cols] = scale
            rows = (summed[:HD] * scale).astype(BF)
            for a in range(TILE // F):
                obuf[h, i * (TILE // F) + a] = rows[:, a * F : (a + 1) * F]
            for a in range(TILE // F):
                ex_o[h][3](i * (TILE // F) + a)
            return carry

        lax.fori_loop(0, S // TILE, attend, 0)
        ex_o[h][4]()

    wo_copy.wait()
    loads[4].wait()
    for h in range(3):
        ex_o[h][1]()
        for b in range(4):
            pair = jnp.concatenate([att_t[h, 2 * b], att_t[h, 2 * b + 1]], axis=0)
            att[:, (4 * h + b) * 128 : (4 * h + b + 1) * 128] = pair.T

        def project(c, carry, h=h):
            cols = pl.ds(pl.multiple_of(c * 256, 256), 256)
            before = res_ref[:, cols].astype(F32) if h == 0 else mixed[:, cols]
            mixed[:, cols] = before + dot(
                att[:, 512 * h : 512 * (h + 1)], wo[512 * h : 512 * (h + 1), cols]
            )
            return carry

        lax.fori_loop(0, D // 256, project, 0)

    def mean_of(x):
        return jnp.sum(x, axis=1, keepdims=True) * (1.0 / D)

    def first_norm(i):
        rows = slice(i * 16, (i + 1) * 16)
        x = mixed[rows, :]
        x = x - mean_of(x)
        r = lax.rsqrt(mean_of(x * x) + EPSILON)
        n = x * r
        n1[rows, :] = n
        r1[rows, :] = r
        valid = me * F + i * 16 + iota((16, 1), 0) < length
        low = jnp.where(valid, n * ng[...], 0.0).astype(BF)
        cin[rows, :] = low
        low_wide = low.astype(F32)
        for c in range(NB):
            cp[c, 16 + i * 16 : 32 + i * 16, :] = low_wide[:, c * 128 : (c + 1) * 128]

    def edges(buffer, k):
        to_right = pltpu.make_async_remote_copy(
            src_ref=buffer.at[pl.ds(F - 16, 16)],
            dst_ref=lh.at[k],
            send_sem=s_h.at[2 * k],
            recv_sem=r_h.at[2 * k],
            device_id=(dp, at(1)),
            device_id_type=MESH,
        )
        to_left = pltpu.make_async_remote_copy(
            src_ref=buffer.at[pl.ds(0, 16)],
            dst_ref=rh.at[k],
            send_sem=s_h.at[2 * k + 1],
            recv_sem=r_h.at[2 * k + 1],
            device_id=(dp, at(-1)),
            device_id_type=MESH,
        )
        return to_right, to_left

    def place_edges(k, padded):
        left = jnp.where(me > 0, lh[k].astype(F32), 0.0)
        right = jnp.where(me < N - 1, rh[k].astype(F32), 0.0)
        for c in range(NB):
            padded[c, 0:16, :] = left[:, c * 128 : (c + 1) * 128]
            padded[c, F + 16 : F + 32, :] = right[:, c * 128 : (c + 1) * 128]

    ends = (0, F // 16 - 1)
    for i in ends:
        first_norm(i)
    halo = edges(cin, 0)
    for copy in halo:
        copy.start()
    for i in range(1, F // 16 - 1):
        first_norm(i)

    def convolve(c, starts, count):
        cols = pl.ds(pl.multiple_of(c * 128, 128), 128)
        totals = [jnp.broadcast_to(cb_ref[pl.ds(c, 1), :], (count, 128))] * len(starts)
        for t in range(KERN):
            tap = taps_ref[t : t + 1, cols]
            totals = [
                total + cp[c, start + t + 1 : start + t + 1 + count, :] * tap
                for total, start in zip(totals, starts)
            ]
        for total, start in zip(totals, starts):
            csum[start : start + count, cols] = total

    def convolve_inside(c, carry):
        convolve(c, (16,), F - 32)
        return carry

    def convolve_ends(c, carry):
        for a in range(2):
            convolve(2 * c + a, (0, F - 16), 16)
        return carry

    lax.fori_loop(0, NB, convolve_inside, 0)
    for copy in halo:
        copy.wait()
    place_edges(0, cp)
    lax.fori_loop(0, NB // 2, convolve_ends, 0)

    vacc[...] = jnp.zeros_like(vacc)

    def fold(x):
        return x[:8] + x[8:]

    def second_norm(i):
        rows = slice(i * 16, (i + 1) * 16)
        x = csum[rows, :]
        x = x - mean_of(x)
        r = lax.rsqrt(mean_of(x * x) + EPSILON)
        n = x * r
        scaled = n * cg[...]
        g = jax.nn.sigmoid(scaled)
        act[rows, :] = (scaled * g).astype(BF)
        back = gact[rows, :] * g * (1.0 + scaled * (1.0 - g))
        vacc[2] += fold(back * n)
        u = back * cg[...]
        grad = r * (u - mean_of(u) - n * mean_of(u * n))
        vacc[0] += fold(grad)
        low = grad.astype(BF)
        gcl[rows, :] = low
        low_wide = low.astype(F32)
        for c in range(NB):
            cols = slice(c * 128, (c + 1) * 128)
            gc[c, rows, :] = grad[:, cols]
            gpad[c, 16 + i * 16 : 32 + i * 16, :] = low_wide[:, cols]

    for i in range(F // 16):
        second_norm(i)
    halo2 = edges(gcl, 1)
    for copy in halo2:
        copy.start()

    weight_term(rows_t, act, 0, 512, 0, True, in_z, point_z[0])
    weight_term(rows_p, act, 512, 512, 1, False, in_x, point_x[0])
    weight_term(rows_y, act, 1024, 512, 2, False, in_y, point_y[0])

    points = (point_z, point_x, point_y)
    for part in (0, 1):
        for point in points:
            point[1][part]()

    for copy in halo2:
        copy.wait()
    place_edges(1, gpad)

    def convolve_back(c, carry):
        cols = pl.ds(pl.multiple_of(c * 128, 128), 128)
        total = jnp.zeros((F, 128), F32)
        for t in range(KERN):
            total = total + gpad[c, KERN - t : KERN - t + F, :] * taps_ref[t : t + 1, cols]
        csum[:, cols] = jnp.where(me * F + iota((F, 1), 0) < length, total, 0.0)
        return carry

    lax.fori_loop(0, NB, convolve_back, 0)

    def first_norm_back(i):
        rows = slice(i * 16, (i + 1) * 16)
        x = csum[rows, :]
        n = n1[rows, :]
        vacc[1] += fold(x * n)
        u = x * ng[...]
        grad = r1[rows, :] * (u - mean_of(u) - n * mean_of(u * n))
        gr_ref[rows, :] = (gm[rows, :].astype(F32) + grad).astype(BF)

    for i in range(F // 16):
        first_norm_back(i)
    stores = [pltpu.make_async_copy(gr_ref, gr_hbm, e_sem.at[1])]
    stores[0].start()

    for h in range(3):

        def attended_rows(j, carry, h=h):
            for a in range(2):
                rows = pl.ds(pl.multiple_of(512 * h + (2 * j + a) * 128, 128), 128)
                part = dot_nt(wo[rows, :], gr_ref[...]).astype(BF)
                dsnd[h, 4 * j + 2 * a] = part[:HD]
                dsnd[h, 4 * j + 2 * a + 1] = part[HD:]
            return carry

        lax.fori_loop(0, 2, attended_rows, 0)
        ex_d[h][0]()

    point_z[2]()
    point_x[2]()
    point_y[2]()
    turn(gr_ref)
    weight_term(rows_t, att, 0, 1024, 3, True, in_z, out_one[0])
    out_one[1][0]()
    small = csum

    def tap_rows(c, carry):
        cols = pl.ds(pl.multiple_of(c * 128, 128), 128)
        grad = gc[c]
        for t in range(KERN):
            small[t : t + 1, cols] = jnp.sum(cp[c, t + 1 : t + 1 + F, :] * grad, axis=0, keepdims=True)
        return carry

    lax.fori_loop(0, NB, tap_rows, 0)
    for i in range(3):
        small[KERN + i : KERN + i + 1, :] = jnp.sum(vacc[i], axis=0, keepdims=True)
    small[KERN + 3 :, :] = jnp.zeros((128 - KERN - 3, D), F32)
    for c in range(NB):
        small_t[c * 128 : (c + 1) * 128, :] = small[:, c * 128 : (c + 1) * 128].T.astype(BF)
    weight_term(rows_t, att, 1024, 512, 4, True, in_z, out_two[0])
    out_two[1][0]()
    out_one[1][1]()
    out_two[1][1]()
    point_x[6]()
    point_y[6]()
    for h in range(3):
        ex_q[h][2]()
        ex_v[h][2]()

    for h in range(3):
        ex_d[h][1]()
        row = iota((16, F), 0)
        for j in range(N):
            cols = slice(j * F, (j + 1) * F)
            grad = do[h, j].astype(F32)
            scale = inv[h, :, cols]
            delta = -scale * jnp.sum(grad * obuf[h, j].astype(F32), axis=0, keepdims=True)
            high = delta.astype(BF).astype(F32)
            doaug[:16, cols] = jnp.where(row == 0, high, jnp.where(row == 1, delta - high, 0.0)).astype(BF)
            scaled = (grad * scale).astype(BF)
            doaug[HD:, cols] = scaled
            dz[HD:, cols] = scaled
            qz[:HD, cols] = rcv[h, j, :HD, :]
            kt[:, cols] = rcv[h, j, HD : 2 * HD, :]

        def back_queries(i, carry, h=h):
            i = turned(i)
            cols = pl.ds(pl.multiple_of(i * TILE, TILE), TILE)
            grads = dot(vaug[h], doaug[:, cols])
            grads = (pt[h, :, cols].astype(F32) * grads).astype(BF)
            dst[:, cols] = grads
            rows = (dot(kt[...], grads) * 0.125).astype(BF)
            for a in range(TILE // F):
                sq[h, i * (TILE // F) + a] = rows[:, a * F : (a + 1) * F]
            for a in range(TILE // F):
                ex_g[h][3](i * (TILE // F) + a)
            return carry

        lax.fori_loop(0, S // TILE, back_queries, 0)

        def back_keys(j, carry, h=h):
            j = lax.rem(j + lax.div(me, 2) + 1, 4)
            rows = pl.ds(pl.multiple_of(j * 2 * F, 2 * F), 2 * F)
            both = dot_nt(dst[rows, :], qz[...]) + dot_nt(pt[h, rows, :], dz[...])
            for a in range(2):
                skv[h, 2 * j + a] = both[a * F : (a + 1) * F].T.astype(BF)
                ex_k[h][3](2 * j + a)
            return carry

        lax.fori_loop(0, N // 2, back_keys, 0)
        ex_g[h][4]()
        ex_k[h][4]()
        if h == 0:
            out_one[2]()
            point_z[3]()
        elif h == 1:
            out_two[2]()
            point_x[3]()
            point_y[3]()

    def block_cols(c, carry):
        cols = pl.ds(pl.multiple_of(c * 256, 256), 256)
        bo_ref[:, cols] = (mixed[:, cols] + dot(act[...], wp[:, cols])).astype(BF)
        return carry

    lax.fori_loop(0, D // 256, block_cols, 0)
    stores.append(pltpu.make_async_copy(bo_ref, bo_hbm, e_sem.at[0]))
    stores[-1].start()

    for h in range(3):
        ex_g[h][1]()
        ex_k[h][1]()
        for b in range(4):
            cols = slice((4 * h + b) * 128, (4 * h + b + 1) * 128)
            for ref, source, part in (
                (gq_ref, rq, slice(0, HD)), (gk_ref, rkv, slice(0, HD)), (gv_ref, rkv, slice(HD, 2 * HD))
            ):
                pair = jnp.concatenate([source[h, 2 * b, part], source[h, 2 * b + 1, part]], axis=0)
                ref[:, cols] = pair.T
        cols = pl.ds(512 * h, 512)
        for a, (ref, hbm) in enumerate(((gq_ref, gq_hbm), (gk_ref, gk_hbm), (gv_ref, gv_hbm))):
            stores.append(pltpu.make_async_copy(ref.at[:, cols], hbm.at[:, cols], e_sem.at[2 + 3 * h + a]))
            stores[-1].start()
        if h == 0:
            out_one[3]()
        elif h == 1:
            out_two[3]()

    gp_ref[12:, :] = jnp.zeros((4, D), F32)
    gw_ref[12:, :] = jnp.zeros((4, D + 128), F32)
    unpacked(point_z[4](), gp_ref, 0, 512)
    unpacked(point_x[4](), gp_ref, 512, 512)
    unpacked(point_y[4](), gp_ref, 1024, 512)
    unpacked(out_one[4](), gw_ref, 0, 1024)
    unpacked(out_two[4](), gw_ref, 1024, 512)
    for i, (ref, hbm) in enumerate(((gw_ref, gw_hbm), (gp_ref, gp_hbm))):
        stores.append(pltpu.make_async_copy(ref, hbm, e_sem.at[11 + i]))
        stores[-1].start()
    for reducer in (point_z, point_x, point_y, out_one, out_two):
        reducer[5]()
    for group in (ex_o, ex_d, ex_g, ex_k):
        for h in range(3):
            group[h][2]()
    for store in stores:
        store.wait()


def fused(lengths, q, k, v, res, go, wo, wp, ng, taps, cb, cg):
    hbm = pl.BlockSpec(memory_space=pl.ANY)
    rows = jax.ShapeDtypeStruct((F, D), BF)
    dma = pltpu.SemaphoreType.DMA
    scratch = [
        pltpu.SMEM((1,), jnp.int32),
        pltpu.VMEM((NB, 128), F32),
        pltpu.VMEM((KERN, D), F32),
        pltpu.VMEM((NB, 128), F32),
        pltpu.VMEM((NB, 128), F32),
        pltpu.VMEM((16, D + 128), F32),
        pltpu.VMEM((16, D), F32),
        *[pltpu.VMEM((F, D), BF)] * 10,
        pltpu.VMEM((D, D), BF),
        pltpu.VMEM((D, D), BF),
        pltpu.VMEM((3, N, 3 * HD, F), BF),
        pltpu.VMEM((3, N, 3 * HD, F), BF),
        pltpu.VMEM((S, 128), BF),
        pltpu.VMEM((128, S), BF),
        pltpu.VMEM((HD + 16, S), BF),
        pltpu.VMEM((3, S, 128), BF),
        pltpu.VMEM((3, S, S), BF),
        pltpu.VMEM((3, 1, S), F32),
        pltpu.VMEM((3, N, HD, F), BF),
        pltpu.VMEM((3, N, HD, F), BF),
        pltpu.VMEM((F, D), BF),
        pltpu.VMEM((F, D), F32),
        pltpu.VMEM((F, D), F32),
        pltpu.VMEM((F, 1), F32),
        pltpu.VMEM((F, D), BF),
        pltpu.VMEM((NB, F + 32, 128), F32),
        pltpu.VMEM((F, D), F32),
        pltpu.VMEM((F, D), F32),
        pltpu.VMEM((F, D), BF),
        pltpu.VMEM((F, D), BF),
        pltpu.VMEM((NB, F, 128), F32),
        pltpu.VMEM((F, D), BF),
        pltpu.VMEM((NB, F + 32, 128), F32),
        pltpu.VMEM((3, 8, D), F32),
        pltpu.VMEM((2, 16, D), BF),
        pltpu.VMEM((2, 16, D), BF),
        pltpu.VMEM((3, N, HD, F), BF),
        pltpu.VMEM((3, N, HD, F), BF),
        pltpu.VMEM((128, S), BF),
        pltpu.VMEM((128, S), BF),
        pltpu.VMEM((128, S), BF),
        pltpu.VMEM((HD, S), BF),
        pltpu.VMEM((3, N, HD, F), BF),
        pltpu.VMEM((3, N, 2 * HD, F), BF),
        pltpu.VMEM((1, D), F32),
        pltpu.VMEM((1, D), F32),
        pltpu.VMEM((D, 128), BF),
        pltpu.VMEM((D, F), BF),
        pltpu.VMEM((D, F), BF),
        pltpu.VMEM((D, F), BF),
        *[
            pltpu.VMEM(shape, BF)
            for w, last, by_z in (
                (512, 384, True), (512, 384, False), (512, 384, False), (1024, 768, True), (640, 512, True)
            )
            for shape in (
                (2, 8, 96, w),
                (8, 96, w),
                (2, 96, w),
                (2, 2, 96, w),
                (8, w) if by_z else (4, 48, w),
                (2, N, 16, last) if by_z else (4, 16, last),
                (2, N, 16, last) if by_z else (4, 16, last),
            )
        ],
        pltpu.VMEM((96, 1024), F32),
        pltpu.VMEM((16, 768), F32),
        dma((2,)),
        dma((10,)),
        dma((13,)),
        dma((3, N)), dma((3, N)),
        dma((3, N)), dma((3, N)),
        dma((3, N)), dma((3, N)),
        dma((3, N)), dma((3, N)),
        dma((3, N)), dma((3, N)),
        dma((3, N)), dma((3, N)),
        dma((4,)), dma((4,)),
        dma((5, 30)), dma((5, 30)),
    ]
    return pl.pallas_call(
        kernel,
        out_shape=[rows] * 5
        + [jax.ShapeDtypeStruct((16, D + 128), F32), jax.ShapeDtypeStruct((16, D), F32)],
        in_specs=[hbm] * 12,
        out_specs=[hbm] * 7,
        scratch_shapes=scratch,
        compiler_params=pltpu.CompilerParams(
            collective_id=0, has_side_effects=True, vmem_limit_bytes=62 * 1024 * 1024
        ),
    )(lengths, q, k, v, res, go, wo, wp, ng, taps, cb, cg)


def finish(*refs):
    sources, targets, held, results, sems = refs[:7], refs[7:16], refs[16:23], refs[23:27], refs[27]
    inward = [pltpu.make_async_copy(sources[i], held[i], sems.at[0, i]) for i in range(7)]
    outward = [pltpu.make_async_copy(held[i], targets[i], sems.at[1, i]) for i in range(5)]
    outward += [pltpu.make_async_copy(results[i], targets[5 + i], sems.at[1, 5 + i]) for i in range(4)]
    for copy in inward:
        copy.start()
    for i in range(5):
        inward[i].wait()
        outward[i].start()
    inward[5].wait()
    inward[6].wait()
    gw_ref, gp_ref = held[5:]
    results[0][...] = gw_ref[:12, :D]
    results[1][...] = gp_ref[:12, :]
    results[2][...] = gw_ref[:12, D : D + KERN]
    results[3][...] = gw_ref[:, D:].T[KERN : KERN + 3, :12]
    for copy in outward[5:]:
        copy.start()
    for copy in outward:
        copy.wait()


def finished(rows, gw, gp):
    hbm = pl.BlockSpec(memory_space=pl.ANY)
    shapes = ((12, D), (12, D), (12, KERN), (3, 12))
    return pl.pallas_call(
        finish,
        out_shape=[jax.ShapeDtypeStruct((F, D), BF)] * 5 + [jax.ShapeDtypeStruct(shape, F32) for shape in shapes],
        in_specs=[hbm] * 7,
        out_specs=[hbm] * 9,
        scratch_shapes=[
            *[pltpu.VMEM((F, D), BF)] * 5,
            *[pltpu.VMEM(shape, F32) for shape in ((16, D + 128), (16, D), *shapes)],
            pltpu.SemaphoreType.DMA((2, 9)),
        ],
        compiler_params=pltpu.CompilerParams(vmem_limit_bytes=62 * 1024 * 1024),
    )(*rows, gw, gp)


def local(
    residual_in, query_rows, key_rows, value_rows, lengths, out_weight, norm_gain, conv_kernel,
    conv_bias, conv_gain, point_weight, grad_out,
):
    outs = fused(
        lengths, query_rows[0], key_rows[0], value_rows[0], residual_in[0], grad_out[0],
        out_weight, point_weight, norm_gain.reshape(NB, 128), conv_kernel,
        conv_bias.reshape(NB, 128), conv_gain.reshape(NB, 128),
    )
    outs = finished(outs[:5], *outs[5:])
    return (*[x[None] for x in outs[:5]], *[x.T for x in outs[5:8]], outs[8])


def solution(mesh):
    rows = P("dp", "ctx", None)
    split = P(None, ("dp", "ctx"))
    in_specs = (rows,) * 4 + (P("dp"),) + (P(),) * 6 + (rows,)
    out_specs = (rows,) * 5 + (split,) * 4
    return jax.shard_map(local, mesh=mesh, in_specs=in_specs, out_specs=out_specs, check_vma=False)
```
